256 devices in a mesh: mesh: 16 (over x, y_lo, core), snap: 16 (over z, y_hi).
Axes of the slice: x: 4, y: 4 (y_hi: 2, y_lo: 2; y = y_hi * 2 + y_lo), z: 8, core: 2. Of those that a mesh axis runs over, the one named last changes fastest.
Arguments:
- snapshots: float32 [1024, 98304], P('snap', 'mesh'), may hold values from -40 to 40, as said below
- connectivity: int32 [3, 196608], P(None, 'mesh'), may hold values from 0 to 6143, as said below
- element_mass: float32 [196608], P('mesh'), may hold values from 0.3 to 3
- lower_shared: int32 [8192], P('mesh'), may hold values from 0 to 6143, as said below
- upper_shared: int32 [8192], P('mesh'), may hold values from 0 to 6143, as said below
Outputs:
- mass_weighted: float32 [1024, 98304], P('snap', 'mesh')
- gram: float32 [1024, 1024], P('snap', 'mesh')
The draws below stay inside these ranges and needn't reach their ends.
Inputs may be any that keep to these rules, and one draw needn't show every extreme that they name: `connectivity`: entries are local slot indices of the element's partition; the three corners of an element differ, and every slot is a corner of some element. `lower_shared`: entry p * 512 + k is a local slot of partition p; a partition's lower and upper lists are disjoint and hold no repeats; slot lower_shared[p, k] of partition p is the same node as slot upper_shared[p - 1, k] of partition p - 1, and snapshots agree there. The lower list of partition 0 has no partner. `upper_shared`: entry p * 512 + k is a local slot of partition p, disjoint from its lower list; the upper list of the last partition has no partner. `snapshots`: values at the two slots of a shared node are equal.
All inputs are finite; a program needn't handle non-finite values.
Results may differ from the reference program's by a relative error of at most 0.0001.
Values sent between devices are 32-bit elements; how exact they have to be, the bound alone decides.
No kernel may reach another device: no remote copies, remote signals or barrier semaphores. Data moves between devices by JAX's collectives and lax.ppermute only.
A program may use at most 128 MiB of HBM per device.

```python
import math
import jax
import jax.numpy as jnp
from jax import lax

NODE_DEV = 6144
SHARED = 512
ELEM_DEV = 12288
ELEMENTS = 196608
SNAPS = 1024
N_MESH = 16


def shared_lists(key):

    def single(subkey):
        order = jax.random.permutation(subkey, NODE_DEV).astype(jnp.int32)
        order = (order + (NODE_DEV - 1 - order[0])) % NODE_DEV
        where_zero = jnp.argmax(order == 0).astype(jnp.int32)
        moved = order[SHARED]
        order = order.at[where_zero].set(moved).at[SHARED].set(0)
        return (order[:SHARED], order[SHARED:2 * SHARED])
    subkeys = jax.random.split(jax.random.fold_in(key, 11), N_MESH)
    lower, upper = jax.vmap(single)(subkeys)
    return (lower.reshape(-1).astype(jnp.int32), upper.reshape(-1).astype(jnp.int32))


def draw_lower_shared(key, part):
    return shared_lists(key)[0]


def draw_upper_shared(key, part):
    return shared_lists(key)[1]


def draw_connectivity(key, part):
    key = jax.random.fold_in(key, 3)
    first_key, second_key = jax.random.split(key)
    element = jnp.arange(ELEM_DEV * N_MESH, dtype=jnp.int32)
    corner_one = element % ELEM_DEV % NODE_DEV
    corner_two = (corner_one + jax.random.randint(first_key, element.shape, 1, 9)) % NODE_DEV
    corner_three = (corner_one + jax.random.randint(second_key, element.shape, 9, 41)) % NODE_DEV
    return jnp.stack([corner_one, corner_two, corner_three]).astype(jnp.int32)


def draw_snapshots(key, part):
    lower, upper = shared_lists(key)
    key = jax.random.fold_in(key, 5)
    common_key, noise_key = jax.random.split(key, 2)
    total = N_MESH * NODE_DEV
    common = jax.random.normal(common_key, (total,), jnp.float32)
    noise = jax.random.normal(noise_key, (SNAPS, total), jnp.float32)
    fields = 0.6 * common + 0.8 * noise
    offsets = jnp.arange(N_MESH - 1, dtype=jnp.int32) * NODE_DEV
    source = (offsets[:, None] + upper.reshape(N_MESH, SHARED)[:-1]).reshape(-1)
    target = (offsets[:, None] + NODE_DEV + lower.reshape(N_MESH, SHARED)[1:]).reshape(-1)
    fields = fields.at[:, target].set(fields[:, source])
    return fields.astype(jnp.float32)


def steps_of(own_key, shape, shards, smallest, top_value):
    factor_of = 1.0
    for axis_at, blocks in shards:
        draws = jax.random.uniform(jax.random.fold_in(jax.random.fold_in(own_key, 6), axis_at), (blocks,), jnp.float32, smallest / len(shards), top_value / len(shards))
        factor_of = factor_of * jnp.repeat(jnp.exp(draws), shape[axis_at] // blocks).reshape((-1,) + (1,) * (len(shape) - 1 - axis_at))
    return factor_of


def setup_inputs(seed: int = 0) -> dict:
    streams_of = jax.random.split(jax.random.key(seed), 6)
    return {
        "snapshots": draw_snapshots(jax.random.fold_in(streams_of[5], 71), 0),
        "connectivity": draw_connectivity(jax.random.fold_in(streams_of[5], 71), 0),
        "element_mass": jnp.clip(jnp.exp(math.log(3.0) - 2.3025851 * jax.random.uniform(streams_of[2], (ELEMENTS,), jnp.float32) ** steps_of(streams_of[2], (ELEMENTS,), ((0, 16),), -0.2, 0.2)), 0.3, 3.0),
        "lower_shared": draw_lower_shared(jax.random.fold_in(streams_of[5], 71), 0),
        "upper_shared": draw_upper_shared(jax.random.fold_in(streams_of[5], 71), 0),
    }


def partial_apply(snapshots, corners, masses):
    values = snapshots[:, corners]
    summed = jnp.sum(values, axis=1, keepdims=True)
    contrib = (masses / 12.0) * (values + summed)
    blank = jnp.zeros_like(snapshots)
    return blank.at[:, corners.reshape(-1)].add(contrib.reshape(snapshots.shape[0], -1))


def reference(snapshots, connectivity, element_mass, lower_shared, upper_shared):
    fields = snapshots.reshape(SNAPS, N_MESH, NODE_DEV).transpose(1, 0, 2)
    corners = connectivity.reshape(3, N_MESH, ELEM_DEV).transpose(1, 0, 2)
    masses = element_mass.reshape(N_MESH, ELEM_DEV)
    lower = lower_shared.reshape(N_MESH, SHARED)
    upper = upper_shared.reshape(N_MESH, SHARED)
    partials = lax.map(lambda items: partial_apply(items[0], items[1], items[2]), (fields, corners, masses))
    upper_vals = jax.vmap(lambda block, index: block[:, index])(partials, upper)
    lower_vals = jax.vmap(lambda block, index: block[:, index])(partials, lower)
    nothing = jnp.zeros_like(upper_vals[:1])
    from_below = jnp.concatenate([nothing, upper_vals[:-1]], axis=0)
    from_above = jnp.concatenate([lower_vals[1:], nothing], axis=0)

    def assemble(block, low_index, high_index, below, above):
        return block.at[:, low_index].add(below).at[:, high_index].add(above)

    weighted = jax.vmap(assemble)(partials, lower, upper, from_below, from_above)
    flags = jnp.where(jnp.arange(N_MESH) > 0, 0.0, 1.0).astype(jnp.float32)
    masks = jax.vmap(lambda low_index, flag: jnp.ones((NODE_DEV,), jnp.float32).at[low_index].set(flag))(lower, flags)
    owned_rows = weighted * masks[:, None, :]

    def accumulate(running, items):
        return running + lax.dot_general(items[0], items[1], (((1,), (1,)), ((), ())),
                                         precision=lax.Precision.HIGHEST,
                                         preferred_element_type=jnp.float32), None

    gram, _ = lax.scan(accumulate, jnp.zeros((SNAPS, SNAPS), jnp.float32), (fields, owned_rows))
    gram = gram / float(N_MESH * NODE_DEV)
    mass_weighted = weighted.transpose(1, 0, 2).reshape(SNAPS, N_MESH * NODE_DEV)
    return mass_weighted, gram
```

```python
import functools

import jax
import jax.numpy as jnp
from jax import lax
from jax.experimental import pallas as pl
from jax.experimental.pallas import tpu as pltpu
from jax.sharding import PartitionSpec as P

LANES = 128
MIB = 2 ** 20


def ring_hop(value, steps, cross=False, closing=False):
    parts, blocks = lax.axis_size("mesh"), lax.axis_size("snap")
    rings = blocks // 2
    pairs = []
    for part in range(parts):
        way = 1 if part % 2 == 0 else -1
        for block in range(blocks):
            z, h = block // 2, block % 2
            target = (z + way * steps) % rings
            if closing and (target < rings // 2) != (part % 2 == 0):
                continue
            pairs.append((part * blocks + block, part * blocks + 2 * target + (h ^ 1 if cross else h)))
    return lax.ppermute(value, ("mesh", "snap"), pairs)


def passed_along(value, axis, steps):
    count = lax.axis_size(axis)
    leading, last = (max(0, -steps), min(count, count - steps))
    return lax.ppermute(value, axis, [(source, source + steps) for source in range(leading, last)])


def partner(value):
    return lax.ppermute(value, "snap", [(i, i ^ 1) for i in range(lax.axis_size("snap"))])


def mirrored(value, cross):
    count = lax.axis_size("snap")
    flip = 1 if cross else 0
    return lax.ppermute(value, ("mesh", "snap"),
                        [(s * count + (m ^ flip), m * count + s) for m in range(count) for s in range(count)])


def apply_kernel(first, start, count, banks, *refs):
    if first:
        (a_hbm, b_hbm, c_hbm, m_hbm, x_ref, rows_out, a_s, b_s, c_s, m_s, sems, xt, *ys) = refs
        sources = (a_hbm, b_hbm, c_hbm, m_hbm)
    else:
        (a_hbm, b_hbm, c_hbm, m_hbm, low_s, up_s, x_ref, rows_in, y_out, rows_out, low_out, up_out,
         a_s, b_s, c_s, m_s, sems, xt, *ys) = refs
        sources = (a_hbm, b_hbm, c_hbm, m_hbm)
    snaps, nodes = x_ref.shape
    copies = []
    for j, (source, target) in enumerate(zip(sources, (a_s, b_s, c_s, m_s))):
        copy = pltpu.make_async_copy(source.at[pl.ds(start, count)], target, sems.at[j])
        copy.start()
        copies.append(copy)

    def prepare(i, carry):
        at = pl.multiple_of(i * LANES, LANES)
        xt[pl.ds(at, LANES), 0:snaps] = x_ref[:, pl.ds(at, LANES)].T
        for y in ys:
            y[pl.ds(at, LANES), :] = jnp.zeros((LANES, LANES), jnp.float32)
        return carry

    lax.fori_loop(0, nodes // LANES, prepare, 0)
    for copy in copies:
        copy.wait()

    def elements(group, carry):
        base = group * banks
        corners = [(a_s[base + k], b_s[base + k], c_s[base + k]) for k in range(banks)]
        updated = []
        for k in range(banks):
            values = [xt[pl.ds(n, 1), :] for n in corners[k]]
            held = [ys[k][pl.ds(n, 1), :] for n in corners[k]]
            total = values[0] + values[1] + values[2]
            mass = m_s[base + k]
            updated.append([h + mass * (v + total) for h, v in zip(held, values)])
        for k in range(banks):
            for n, new in zip(corners[k], updated[k]):
                ys[k][pl.ds(n, 1), :] = new
        return carry

    lax.fori_loop(0, count // banks, elements, 0)

    def finish(i, carry):
        at = pl.multiple_of(i * LANES, LANES)
        total = ys[0][pl.ds(at, LANES), :]
        for y in ys[1:]:
            total = total + y[pl.ds(at, LANES), :]
        if first:
            rows_out[pl.ds(at, LANES), :] = total
        else:
            total = (total + rows_in[pl.ds(at, LANES), :]) * (1.0 / 12.0)
            rows_out[pl.ds(at, LANES), :] = total
            y_out[:, pl.ds(at, LANES)] = total.T[0:snaps, :]
        return carry

    lax.fori_loop(0, nodes // LANES, finish, 0)
    if first:
        return
    for list_s, out in ((low_s, low_out), (up_s, up_out)):
        def gather(i, carry, list_s=list_s):
            at = pl.multiple_of(i * 8, 8)
            for k in range(8):
                xt[pl.ds(at + k, 1), :] = rows_out[pl.ds(list_s[at + k], 1), :]
            return carry

        shared = out.shape[1]
        lax.fori_loop(0, shared // 8, gather, 0)
        for block in range(shared // LANES):
            at = block * LANES
            out[:, at:at + LANES] = xt[at:at + LANES, :].T[0:snaps, :]


def assemble_kernel(low_s, up_s, rows_ref, below_ref, above_ref, out_ref, rows, taken):
    snaps, shared = below_ref.shape
    nodes = rows_ref.shape[0]

    def copy(i, carry):
        at = pl.multiple_of(i * LANES, LANES)
        rows[pl.ds(at, LANES), :] = rows_ref[pl.ds(at, LANES), :]
        return carry

    lax.fori_loop(0, nodes // LANES, copy, 0)
    for list_s, received in ((low_s, below_ref), (up_s, above_ref)):
        for block in range(shared // LANES):
            at = block * LANES
            taken[at:at + LANES, 0:snaps] = received[:, at:at + LANES].T

        def add(i, carry, list_s=list_s):
            at = pl.multiple_of(i * 8, 8)
            nodes_of = [list_s[at + k] for k in range(8)]
            new = [rows[pl.ds(n, 1), :] + taken[pl.ds(at + k, 1), :] for k, n in enumerate(nodes_of)]
            for n, value in zip(nodes_of, new):
                rows[pl.ds(n, 1), :] = value
            return carry

        lax.fori_loop(0, shared // 8, add, 0)

    def write(i, carry):
        at = pl.multiple_of(i * LANES, LANES)
        out_ref[:, pl.ds(at, LANES)] = rows[pl.ds(at, LANES), :].T[0:snaps, :]
        return carry

    lax.fori_loop(0, nodes // LANES, write, 0)


ANYWHERE = pl.BlockSpec(memory_space=pl.ANY)
IN_VMEM = pl.BlockSpec(memory_space=pltpu.VMEM)
IN_SMEM = pl.BlockSpec(memory_space=pltpu.SMEM)


def cost(micros):
    return pl.CostEstimate(flops=int(micros * 1e9), bytes_accessed=int(micros * 3e6), transcendentals=0)


def apply_call(first, start, count, banks, operands, snaps, nodes, shared):
    rows = jax.ShapeDtypeStruct((nodes, LANES), jnp.float32)
    side = jax.ShapeDtypeStruct((snaps, shared), jnp.float32)
    whole = jax.ShapeDtypeStruct((snaps, nodes), jnp.float32)
    return pl.pallas_call(
        functools.partial(apply_kernel, first, start, count, banks),
        out_shape=[rows] if first else [whole, rows, side, side],
        in_specs=[ANYWHERE] * 4 + ([IN_VMEM] if first else [IN_SMEM] * 2 + [IN_VMEM] * 2),
        out_specs=[IN_VMEM] if first else [IN_VMEM] * 4,
        scratch_shapes=[pltpu.SMEM((count,), jnp.int32)] * 3
        + [pltpu.SMEM((count,), jnp.float32), pltpu.SemaphoreType.DMA((4,))]
        + [pltpu.VMEM((nodes, LANES), jnp.float32)] * (banks + 1),
        compiler_params=pltpu.CompilerParams(vmem_limit_bytes=56 * MIB),
        cost_estimate=cost(30),
    )(*operands)


def split3(left, right):
    dims = (((1,), (1,)), ((), ()))
    dot = functools.partial(lax.dot_general, dimension_numbers=dims, preferred_element_type=jnp.float32)
    (l_hi, l_lo), (r_hi, r_lo) = left, right
    return dot(l_hi, r_hi) + (dot(l_hi, r_lo) + dot(l_lo, r_hi))


def halves_of(value):
    high = value.astype(jnp.bfloat16)
    return high, (value - high.astype(jnp.float32)).astype(jnp.bfloat16)


def gram_kernel(place, ya_ref, yb_ref, *refs):
    *blocks, out_ref = refs
    snaps = ya_ref.shape[0]
    rings = out_ref.shape[0] // 2
    z, h, way = place[0], place[1], place[2]

    @pl.when(pl.program_id(0) == 0)
    def _():
        out_ref[...] = jnp.zeros_like(out_ref)

    y = halves_of(jnp.concatenate([ya_ref[...], yb_ref[...]], axis=0))
    for distance, (a, b) in enumerate(zip(blocks[0::2], blocks[1::2])):
        value = split3(halves_of(jnp.concatenate([a[...], b[...]], axis=0)), y)
        if distance == 0:
            value = 0.5 * value
        at = lax.rem(z - way * distance + rings, rings)
        out_ref[2 * at + h] += value[0:snaps]
        out_ref[2 * at + (1 - h)] += value[snaps:2 * snaps]


def gram_call(place, ya, yb, blocks, rings):
    snaps, nodes = ya.shape
    chunk = nodes // 4
    piece = pl.BlockSpec((snaps, chunk), lambda i: (0, i))
    return pl.pallas_call(
        gram_kernel,
        grid=(nodes // chunk,),
        out_shape=jax.ShapeDtypeStruct((2 * rings, snaps, 2 * snaps), jnp.float32),
        in_specs=[IN_SMEM] + [piece] * (2 + len(blocks)),
        out_specs=pl.BlockSpec((2 * rings, snaps, 2 * snaps), lambda i: (0, 0, 0)),
        compiler_params=pltpu.CompilerParams(vmem_limit_bytes=40 * MIB),
        cost_estimate=cost(8),
    )(place, ya, yb, *blocks)


def on_device(snapshots, connectivity, element_mass, lower_shared, upper_shared):
    snaps, nodes = snapshots.shape
    elements = element_mass.shape[0]
    shared = lower_shared.shape[0]
    position = lax.axis_index("mesh")
    block = lax.axis_index("snap")
    rings = lax.axis_size("snap") // 2
    z, h = block // 2, block % 2
    half = nodes // 2

    own = lax.dynamic_slice_in_dim(snapshots, h * half, half, 1)
    given = lax.dynamic_slice_in_dim(snapshots, (1 - h) * half, half, 1)
    a1 = ring_hop(own, 1)
    b1 = ring_hop(given, 1, cross=True)
    a2 = ring_hop(own, 2)

    columns = tuple(connectivity[k] for k in range(3)) + (element_mass,)
    (rows,) = apply_call(True, 0, elements // 2, 8, columns + (snapshots,), snaps, nodes, shared)

    rows, b1, a2 = lax.optimization_barrier((rows, b1, a2))
    b2 = ring_hop(b1, 1)
    a3 = ring_hop(a2, 1)
    b3 = ring_hop(b1, 2)
    b0 = partner(given)

    partial, rows, low, high = apply_call(
        False, elements // 2, elements // 2, 8, columns + (lower_shared, upper_shared, snapshots, rows),
        snaps, nodes, shared)

    partial, a3, b3 = lax.optimization_barrier((partial, a3, b3))
    y_own = lax.dynamic_slice_in_dim(partial, h * half, half, 1)
    y_given = lax.dynamic_slice_in_dim(partial, (1 - h) * half, half, 1)
    y_theirs = partner(y_given)
    a4 = ring_hop(a3, 1, closing=True)
    b4 = ring_hop(b3, 1, closing=True)

    from_below = passed_along(high, "mesh", 1)
    from_above = passed_along(low, "mesh", -1)
    weighted = pl.pallas_call(
        assemble_kernel,
        out_shape=jax.ShapeDtypeStruct((snaps, nodes), jnp.float32),
        in_specs=[IN_SMEM] * 2 + [IN_VMEM] * 3,
        out_specs=IN_VMEM,
        scratch_shapes=[pltpu.VMEM((nodes, LANES), jnp.float32), pltpu.VMEM((shared, LANES), jnp.float32)],
        compiler_params=pltpu.CompilerParams(vmem_limit_bytes=20 * MIB),
        cost_estimate=cost(6),
    )(lower_shared, upper_shared, rows, from_below, from_above)
    weighted, y_theirs = lax.optimization_barrier((weighted, y_theirs))

    place = jnp.stack([z, h, jnp.where(position % 2 == 0, 1, -1)]).astype(jnp.int32)
    tiles = gram_call(place, y_own, y_theirs, [own, b0, a1, b1, a2, b2, a3, b3, a4, b4], rings)
    tile = jnp.sum(lax.all_to_all(tiles, "mesh", 0, 0, tiled=True), axis=0)
    mine, others = tile[:, :snaps], tile[:, snaps:]
    total = (mine + partner(others)).T + (mirrored(mine, False) + mirrored(others, True))
    return weighted, total * (1.0 / float(lax.axis_size("mesh") * nodes))


def solution(mesh):
    placed = (P("snap", "mesh"), P(None, "mesh"), P("mesh"), P("mesh"), P("mesh"))
    return jax.shard_map(
        on_device,
        mesh=mesh,
        in_specs=placed,
        out_specs=(P("snap", "mesh"), P("snap", "mesh")),
        check_vma=False,
    )
```

```python
import functools

import jax
import jax.numpy as jnp
from jax import lax
from jax.experimental import pallas as pl
from jax.experimental.pallas import tpu as pltpu
from jax.sharding import PartitionSpec as P

LANES = 128
MIB = 2 ** 20


def ring_hop(value, steps, cross=False, closing=False):
    parts, blocks = lax.axis_size("mesh"), lax.axis_size("snap")
    rings = blocks // 2
    pairs = []
    for part in range(parts):
        way = 1 if part % 2 == 0 else -1
        for block in range(blocks):
            z, h = block // 2, block % 2
            target = (z + way * steps) % rings
            if closing and (target < rings // 2) != (part % 2 == 0):
                continue
            pairs.append((part * blocks + block, part * blocks + 2 * target + (h ^ 1 if cross else h)))
    return lax.ppermute(value, ("mesh", "snap"), pairs)


def passed_along(value, axis, steps):
    count = lax.axis_size(axis)
    leading, last = (max(0, -steps), min(count, count - steps))
    return lax.ppermute(value, axis, [(source, source + steps) for source in range(leading, last)])


def partner(value):
    return lax.ppermute(value, "snap", [(i, i ^ 1) for i in range(lax.axis_size("snap"))])


def mirrored(value):
    count = lax.axis_size("snap")
    return lax.ppermute(value, ("mesh", "snap"),
                        [(s * count + m, m * count + s) for m in range(count) for s in range(count)])


def apply_kernel(first, last, start, count, arrays, parts, *refs):
    refs = list(refs)
    a_hbm, b_hbm, c_hbm, m_hbm, x_ref = refs[:5]
    del refs[:5]
    rows_in = None if first else refs.pop(0)
    low_s, up_s = (refs.pop(0), refs.pop(0)) if last else (None, None)
    rows_out = refs.pop(0)
    y_out, low_out, up_out = (refs.pop(0), refs.pop(0), refs.pop(0)) if last else (None, None, None)
    a_s, b_s, c_s, m_s, sems, *zs = refs
    snaps, nodes = x_ref.shape
    tiles = LANES // 8
    width = 1 + parts
    copies = []
    for j, (source, target) in enumerate(zip((a_hbm, b_hbm, c_hbm, m_hbm), (a_s, b_s, c_s, m_s))):
        copy = pltpu.make_async_copy(source.at[pl.ds(start, count)], target, sems.at[j])
        copy.start()
        copies.append(copy)

    def tile_of(block, i, part):
        return pl.ds(pl.multiple_of(block * (LANES * width) + (i * width + part) * 8, 8), 8)

    def prepare(block, carry):
        x = x_ref[:, pl.ds(pl.multiple_of(block * LANES, LANES), LANES)]
        rows = jnp.concatenate([x, x], axis=0).T
        blank = jnp.zeros((8, LANES), jnp.float32)
        for z in zs:
            for i in range(tiles):
                z[tile_of(block, i, 0), :] = rows[i * 8:(i + 1) * 8]
                for part in range(parts):
                    z[tile_of(block, i, 1 + part), :] = blank
        return carry

    lax.fori_loop(0, nodes // LANES, prepare, 0)
    for copy in copies:
        copy.wait()

    def elements(group, carry):
        for j, z in enumerate(zs):
            corners, updated = [], []
            for k in range(2 * parts):
                e = group * (arrays * 2 * parts) + (j * 2 * parts + k)
                corners.append((a_s[e], b_s[e], c_s[e]))
                mass = m_s[e]
                values = [z[pl.ds(n, 1), :] for n in corners[k]]
                held = [z[pl.ds(n + 8 * (1 + k // 2), 1), :] for n in corners[k]]
                total = values[0] + values[1] + values[2]
                updated.append([h + mass * (v + total) for h, v in zip(held, values)])
            for k in range(2 * parts):
                at = snaps * (k % 2)
                for n, new in zip(corners[k], updated[k]):
                    z[pl.ds(n + 8 * (1 + k // 2), 1), at:at + snaps] = new[:, at:at + snaps]
        return carry

    lax.fori_loop(0, count // (arrays * 2 * parts), elements, 0)

    def finish(block, carry):
        totals = []
        for i in range(tiles):
            total = None
            for z in zs:
                for part in range(parts):
                    value = z[tile_of(block, i, 1 + part), :]
                    total = value if total is None else total + value
            totals.append(total)
        total = jnp.concatenate(totals, axis=0)
        at = pl.multiple_of(block * LANES, LANES)
        if not first:
            total = total + rows_in[pl.ds(at, LANES), :]
        if last:
            total = total * (1.0 / 12.0)
            columns = total.T
            y_out[:, pl.ds(at, LANES)] = columns[0:snaps, :] + columns[snaps:2 * snaps, :]
        rows_out[pl.ds(at, LANES), :] = total
        return carry

    lax.fori_loop(0, nodes // LANES, finish, 0)
    if not last:
        return
    for list_s, out in ((low_s, low_out), (up_s, up_out)):
        def gather(i, carry, list_s=list_s):
            at = pl.multiple_of(i * 16, 16)
            for k in range(16):
                zs[0][pl.ds(at + k, 1), :] = rows_out[pl.ds(list_s[at + k], 1), :]
            return carry

        shared = out.shape[1]
        lax.fori_loop(0, shared // 16, gather, 0)
        for block in range(shared // LANES):
            at = block * LANES
            columns = zs[0][at:at + LANES, :].T
            out[:, at:at + LANES] = columns[0:snaps, :] + columns[snaps:2 * snaps, :]


def assemble_kernel(low_s, up_s, rows_ref, below_ref, above_ref, out_ref, rows, taken):
    snaps, shared = below_ref.shape
    nodes = rows_ref.shape[0]

    def copy(i, carry):
        at = pl.multiple_of(i * LANES, LANES)
        rows[pl.ds(at, LANES), :] = rows_ref[pl.ds(at, LANES), :]
        return carry

    lax.fori_loop(0, nodes // LANES, copy, 0)
    for list_s, received in ((low_s, below_ref), (up_s, above_ref)):
        for block in range(shared // LANES):
            at = block * LANES
            value = received[:, at:at + LANES]
            taken[at:at + LANES, :] = jnp.concatenate([value, jnp.zeros_like(value)], axis=0).T

        def add(i, carry, list_s=list_s):
            at = pl.multiple_of(i * 8, 8)
            nodes_of = [list_s[at + k] for k in range(8)]
            new = [rows[pl.ds(n, 1), :] + taken[pl.ds(at + k, 1), :] for k, n in enumerate(nodes_of)]
            for n, value in zip(nodes_of, new):
                rows[pl.ds(n, 1), :] = value
            return carry

        lax.fori_loop(0, shared // 8, add, 0)

    def write(i, carry):
        at = pl.multiple_of(i * LANES, LANES)
        columns = rows[pl.ds(at, LANES), :].T
        out_ref[:, pl.ds(at, LANES)] = columns[0:snaps, :] + columns[snaps:2 * snaps, :]
        return carry

    lax.fori_loop(0, nodes // LANES, write, 0)


ANYWHERE = pl.BlockSpec(memory_space=pl.ANY)
IN_VMEM = pl.BlockSpec(memory_space=pltpu.VMEM)
IN_SMEM = pl.BlockSpec(memory_space=pltpu.SMEM)


def cost(micros):
    return pl.CostEstimate(flops=int(micros * 1e9), bytes_accessed=int(micros * 3e6), transcendentals=0)


ARRAYS, PARTS = 4, 2


def apply_call(index, calls, columns, snapshots, rows, lists):
    first, last = index == 0, index == calls - 1
    snaps, nodes = snapshots.shape
    count = columns[0].shape[0] // calls
    shared = lists[0].shape[0]
    row_shape = jax.ShapeDtypeStruct((nodes, LANES), jnp.float32)
    side = jax.ShapeDtypeStruct((snaps, shared), jnp.float32)
    whole = jax.ShapeDtypeStruct((snaps, nodes), jnp.float32)
    operands = columns + (snapshots,) + (() if first else (rows,)) + (lists if last else ())
    return pl.pallas_call(
        functools.partial(apply_kernel, first, last, index * count, count, ARRAYS, PARTS),
        out_shape=[row_shape] + ([whole, side, side] if last else []),
        in_specs=[ANYWHERE] * 4 + [IN_VMEM] + ([] if first else [IN_VMEM]) + ([IN_SMEM] * 2 if last else []),
        out_specs=[IN_VMEM] + ([IN_VMEM] * 3 if last else []),
        scratch_shapes=[pltpu.SMEM((count,), jnp.int32)] * 3
        + [pltpu.SMEM((count,), jnp.float32), pltpu.SemaphoreType.DMA((4,))]
        + [pltpu.VMEM((nodes * (1 + PARTS), LANES), jnp.float32)] * ARRAYS,
        compiler_params=pltpu.CompilerParams(vmem_limit_bytes=56 * MIB),
        cost_estimate=cost(20),
    )(*operands)


def split3(left, right):
    dims = (((1,), (1,)), ((), ()))
    dot = functools.partial(lax.dot_general, dimension_numbers=dims, preferred_element_type=jnp.float32)
    (l_hi, l_lo), (r_hi, r_lo) = left, right
    return dot(l_hi, r_hi) + (dot(l_hi, r_lo) + dot(l_lo, r_hi))


def halves_of(value):
    high = value.astype(jnp.bfloat16)
    return high, (value - high.astype(jnp.float32)).astype(jnp.bfloat16)


def gram_kernel(place, ya_ref, yb_ref, a0_ref, b0_ref, *refs):
    *streams, out_ref, sums = refs
    snaps = ya_ref.shape[0]
    rings = out_ref.shape[0] // 4
    low = snaps // 2
    z, h, way = place[0], place[1], place[2]
    step = pl.program_id(0)

    @pl.when(step == 0)
    def _():
        sums[...] = jnp.zeros_like(sums)

    y = halves_of(jnp.concatenate([ya_ref[...], yb_ref[...]], axis=0))
    sums[0] += split3(halves_of(jnp.concatenate([a0_ref[...], b0_ref[...]], axis=0)), y)
    for distance, stream in enumerate(streams, 1):
        sums[distance] += split3(halves_of(stream[...]), y)

    @pl.when(step == pl.num_programs(0) - 1)
    def _():
        out_ref[...] = jnp.zeros_like(out_ref)
        for distance in range(1 + len(streams)):
            value = sums[distance]
            if distance == 0:
                value = 0.5 * value
            at = lax.rem(z - way * distance + rings, rings)
            for side in range(2):
                row = 2 * at + (h if side == 0 else 1 - h)
                upper, lower = value[side * snaps:side * snaps + low], value[side * snaps + low:(side + 1) * snaps]
                out_ref[2 * row + h] = jnp.concatenate([upper[:, :snaps], lower[:, :snaps]], axis=1)
                out_ref[2 * row + (1 - h)] = jnp.concatenate([upper[:, snaps:], lower[:, snaps:]], axis=1)


def gram_call(place, ya, yb, a0, b0, streams, rings):
    snaps, nodes = ya.shape
    chunk = nodes // 4
    single = pl.BlockSpec((snaps, chunk), lambda i: (0, i))
    double = pl.BlockSpec((2 * snaps, chunk), lambda i: (0, i))
    tiles = (4 * rings, snaps // 2, 2 * snaps)
    return pl.pallas_call(
        gram_kernel,
        grid=(nodes // chunk,),
        out_shape=jax.ShapeDtypeStruct(tiles, jnp.float32),
        in_specs=[IN_SMEM] + [single] * 4 + [double] * len(streams),
        out_specs=pl.BlockSpec(tiles, lambda i: (0, 0, 0)),
        scratch_shapes=[pltpu.VMEM((1 + len(streams), 2 * snaps, 2 * snaps), jnp.float32)],
        compiler_params=pltpu.CompilerParams(vmem_limit_bytes=40 * MIB),
        cost_estimate=cost(8),
    )(place, ya, yb, a0, b0, *streams)


def on_device(snapshots, connectivity, element_mass, lower_shared, upper_shared):
    snaps, nodes = snapshots.shape
    parts = lax.axis_size("mesh")
    blocks = lax.axis_size("snap")
    position = lax.axis_index("mesh")
    block = lax.axis_index("snap")
    rings = blocks // 2
    z, h = block // 2, block % 2
    half = nodes // 2
    tied = lax.optimization_barrier

    own = lax.dynamic_slice_in_dim(snapshots, h * half, half, 1)
    given = lax.dynamic_slice_in_dim(snapshots, (1 - h) * half, half, 1)
    a1 = ring_hop(own, 1)
    b1 = ring_hop(given, 1, cross=True)

    spread = (connectivity >> 3) * (8 * (1 + PARTS)) + (connectivity & 7)
    columns = tuple(spread[k] for k in range(3)) + (element_mass,)
    lists = (lower_shared, upper_shared)
    (rows,) = apply_call(0, 3, columns, snapshots, None, lists)

    rows, a1, b1 = tied((rows, a1, b1))
    pair1 = jnp.concatenate([a1, b1], axis=0)
    pair2 = ring_hop(pair1, 1)
    (rows,) = apply_call(1, 3, columns, snapshots, rows, lists)

    rows, pair2 = tied((rows, pair2))
    pair3 = ring_hop(pair2, 1)
    b0 = partner(given)
    rows, partial, low, high = apply_call(2, 3, columns, snapshots, rows, lists)

    partial, pair3, b0 = tied((partial, pair3, b0))
    y_own = lax.dynamic_slice_in_dim(partial, h * half, half, 1)
    y_theirs = partner(lax.dynamic_slice_in_dim(partial, (1 - h) * half, half, 1))
    pair4 = ring_hop(pair3, 1, closing=True)

    from_below = passed_along(high, "mesh", 1)
    from_above = passed_along(low, "mesh", -1)
    shared = lower_shared.shape[0]
    weighted = pl.pallas_call(
        assemble_kernel,
        out_shape=jax.ShapeDtypeStruct((snaps, nodes), jnp.float32),
        in_specs=[IN_SMEM] * 2 + [IN_VMEM] * 3,
        out_specs=IN_VMEM,
        scratch_shapes=[pltpu.VMEM((nodes, LANES), jnp.float32), pltpu.VMEM((shared, LANES), jnp.float32)],
        compiler_params=pltpu.CompilerParams(vmem_limit_bytes=20 * MIB),
        cost_estimate=cost(8),
    )(lower_shared, upper_shared, rows, from_below, from_above)
    weighted, y_theirs, pair4 = tied((weighted, y_theirs, pair4))

    place = jnp.stack([z, h, jnp.where(position % 2 == 0, 1, -1)]).astype(jnp.int32)
    tiles = gram_call(place, y_own, y_theirs, own, b0, [pair1, pair2, pair3, pair4], rings)
    planes = [[m * blocks + 2 * r + c for m in range(parts) for c in range(2)] for r in range(rings)]
    tile = jnp.sum(lax.all_to_all(tiles, ("mesh", "snap"), 0, 0, axis_index_groups=planes, tiled=True), axis=0)
    other = mirrored(tile)

    def unfolded(value):
        return jnp.concatenate([value[:, :snaps], value[:, snaps:]], axis=0)

    return weighted, (unfolded(tile).T + unfolded(other)) * (1.0 / float(parts * nodes))


def solution(mesh):
    placed = (P("snap", "mesh"), P(None, "mesh"), P("mesh"), P("mesh"), P("mesh"))
    return jax.shard_map(
        on_device,
        mesh=mesh,
        in_specs=placed,
        out_specs=(P("snap", "mesh"), P("snap", "mesh")),
        check_vma=False,
    )
```

```python
import functools

import jax
import jax.numpy as jnp
from jax import lax
from jax.experimental import pallas as pl
from jax.experimental.pallas import tpu as pltpu
from jax.sharding import PartitionSpec as P

LANES = 128
MIB = 2 ** 20


def ring_hop(value, steps, cross=False, closing=False):
    parts, blocks = lax.axis_size("mesh"), lax.axis_size("snap")
    rings = blocks // 2
    pairs = []
    for part in range(parts):
        way = 1 if part % 2 == 0 else -1
        for block in range(blocks):
            z, h = block // 2, block % 2
            target = (z + way * steps) % rings
            if closing and (target < rings // 2) != (part % 2 == 0):
                continue
            pairs.append((part * blocks + block, part * blocks + 2 * target + (h ^ 1 if cross else h)))
    return lax.ppermute(value, ("mesh", "snap"), pairs)


def passed_along(value, axis, steps):
    count = lax.axis_size(axis)
    leading, last = (max(0, -steps), min(count, count - steps))
    return lax.ppermute(value, axis, [(source, source + steps) for source in range(leading, last)])


def partner(value):
    return lax.ppermute(value, "snap", [(i, i ^ 1) for i in range(lax.axis_size("snap"))])


def mirrored(value):
    count = lax.axis_size("snap")
    return lax.ppermute(value, ("mesh", "snap"),
                        [(s * count + m, m * count + s) for m in range(count) for s in range(count)])


def apply_kernel(first, last, start, count, arrays, parts, *refs):
    refs = list(refs)
    a_hbm, b_hbm, c_hbm, m_hbm, x_ref = refs[:5]
    del refs[:5]
    rows_in = None if first else refs.pop(0)
    half_s = refs.pop(0) if last else None
    rows_out = refs.pop(0)
    y_outs = (refs.pop(0), refs.pop(0)) if last else None
    a_s, b_s, c_s, m_s, sems, sums, in_sem, out_sems, *zs = refs
    snaps, nodes = x_ref.shape
    tiles = LANES // 8
    width = 1 + parts
    copies = []
    for j, (source, target) in enumerate(zip((a_hbm, b_hbm, c_hbm, m_hbm), (a_s, b_s, c_s, m_s))):
        copy = pltpu.make_async_copy(source.at[pl.ds(start, count)], target, sems.at[j])
        copy.start()
        copies.append(copy)
    if not first:
        earlier = pltpu.make_async_copy(rows_in, sums, in_sem)
        earlier.start()

    def tile_of(block, i, part):
        return pl.ds(pl.multiple_of(block * (LANES * width) + (i * width + part) * 8, 8), 8)

    def prepare(block, carry):
        x = x_ref[:, pl.ds(pl.multiple_of(block * LANES, LANES), LANES)]
        rows = jnp.concatenate([x, x], axis=0).T
        blank = jnp.zeros((8, LANES), jnp.float32)
        for z in zs:
            for i in range(tiles):
                z[tile_of(block, i, 0), :] = rows[i * 8:(i + 1) * 8]
                for part in range(parts):
                    z[tile_of(block, i, 1 + part), :] = blank
        return carry

    lax.fori_loop(0, nodes // LANES, prepare, 0)
    for copy in copies:
        copy.wait()

    def elements(group, carry):
        for j, z in enumerate(zs):
            corners, updated = [], []
            for k in range(2 * parts):
                e = group * (arrays * 2 * parts) + (j * 2 * parts + k)
                corners.append((a_s[e], b_s[e], c_s[e]))
                mass = m_s[e]
                values = [z[pl.ds(n, 1), :] for n in corners[k]]
                held = [z[pl.ds(n + 8 * (1 + k // 2), 1), :] for n in corners[k]]
                total = values[0] + values[1] + values[2]
                updated.append([h + mass * (v + total) for h, v in zip(held, values)])
            for k in range(2 * parts):
                at = snaps * (k % 2)
                for n, new in zip(corners[k], updated[k]):
                    z[pl.ds(n + 8 * (1 + k // 2), 1), at:at + snaps] = new[:, at:at + snaps]
        return carry

    lax.fori_loop(0, count // (arrays * 2 * parts), elements, 0)

    if not first:
        earlier.wait()

    def finish(block):
        totals = []
        for i in range(tiles):
            total = None
            for z in zs:
                for part in range(parts):
                    value = z[tile_of(block, i, 1 + part), :]
                    total = value if total is None else total + value
            totals.append(total)
        total = jnp.concatenate(totals, axis=0)
        at = pl.multiple_of(block * LANES, LANES)
        if not first:
            total = total + sums[pl.ds(at, LANES), :]
        if last:
            total = total * (1.0 / 12.0)
        sums[pl.ds(at, LANES), :] = total
        return total

    pieces = out_sems.shape[0]
    size = nodes // pieces
    writes = []
    for piece in range(pieces):
        blocks = size // LANES
        begin = piece * blocks
        side = None
        if last:
            side = piece // (pieces // 2)
            begin = lax.rem(half_s[0] + side, 2) * (pieces // 2 * blocks) + piece % (pieces // 2) * blocks

        def inner(i, carry, begin=begin, side=side, piece=piece):
            total = finish(begin + i)
            if last:
                columns = total.T
                at = pl.multiple_of((piece % (pieces // 2) * blocks + i) * LANES, LANES)
                y_outs[side][:, pl.ds(at, LANES)] = columns[0:snaps, :] + columns[snaps:2 * snaps, :]
            return carry

        lax.fori_loop(0, blocks, inner, 0)
        at = pl.multiple_of(begin * LANES, LANES) if last else begin * LANES
        write = pltpu.make_async_copy(sums.at[pl.ds(at, size)], rows_out.at[pl.ds(at, size)], out_sems.at[piece])
        write.start()
        writes.append(write)
    for write in writes:
        write.wait()


def gather_kernel(low_s, up_s, rows, low_out, up_out, taken):
    snaps, shared = low_out.shape
    for list_s, out in ((low_s, low_out), (up_s, up_out)):
        def gather(i, carry, list_s=list_s):
            at = pl.multiple_of(i * 16, 16)
            for k in range(16):
                taken[pl.ds(at + k, 1), :] = rows[pl.ds(list_s[at + k], 1), :]
            return carry

        lax.fori_loop(0, shared // 16, gather, 0)
        for block in range(shared // LANES):
            at = block * LANES
            columns = taken[at:at + LANES, :].T
            out[:, at:at + LANES] = columns[0:snaps, :] + columns[snaps:2 * snaps, :]


def assemble_kernel(low_s, up_s, rows_ref, below_ref, above_ref, out_ref, rows, below, above, sem):
    snaps, shared = below_ref.shape
    nodes = rows_ref.shape[0]
    copy = pltpu.make_async_copy(rows_ref, rows, sem)
    copy.start()
    for received, taken in ((below_ref, below), (above_ref, above)):
        for block in range(shared // LANES):
            at = block * LANES
            value = received[:, at:at + LANES]
            taken[at:at + LANES, :] = jnp.concatenate([value, jnp.zeros_like(value)], axis=0).T
    copy.wait()
    for list_s, taken in ((low_s, below), (up_s, above)):
        def add(i, carry, list_s=list_s, taken=taken):
            at = pl.multiple_of(i * 16, 16)
            nodes_of = [list_s[at + k] for k in range(16)]
            new = [rows[pl.ds(n, 1), :] + taken[pl.ds(at + k, 1), :] for k, n in enumerate(nodes_of)]
            for n, value in zip(nodes_of, new):
                rows[pl.ds(n, 1), :] = value
            return carry

        lax.fori_loop(0, shared // 16, add, 0)

    def write(i, carry):
        at = pl.multiple_of(i * LANES, LANES)
        columns = rows[pl.ds(at, LANES), :].T
        out_ref[:, pl.ds(at, LANES)] = columns[0:snaps, :] + columns[snaps:2 * snaps, :]
        return carry

    lax.fori_loop(0, nodes // LANES, write, 0)


ANYWHERE = pl.BlockSpec(memory_space=pl.ANY)
IN_VMEM = pl.BlockSpec(memory_space=pltpu.VMEM)
IN_SMEM = pl.BlockSpec(memory_space=pltpu.SMEM)


def cost(micros):
    return pl.CostEstimate(flops=int(micros * 1e9), bytes_accessed=int(micros * 3e6), transcendentals=0)


ARRAYS, PARTS = 4, 2


def apply_call(index, calls, columns, snapshots, rows, half):
    first, last = index == 0, index == calls - 1
    snaps, nodes = snapshots.shape
    count = columns[0].shape[0] // calls
    row_shape = jax.ShapeDtypeStruct((nodes, LANES), jnp.float32)
    side = jax.ShapeDtypeStruct((snaps, nodes // 2), jnp.float32)
    operands = columns + (snapshots,) + (() if first else (rows,)) + ((half,) if last else ())
    return pl.pallas_call(
        functools.partial(apply_kernel, first, last, index * count, count, ARRAYS, PARTS),
        out_shape=[row_shape] + ([side, side] if last else []),
        in_specs=[ANYWHERE] * 4 + [IN_VMEM] + ([] if first else [ANYWHERE]) + ([IN_SMEM] if last else []),
        out_specs=[ANYWHERE] + ([IN_VMEM] * 2 if last else []),
        scratch_shapes=[pltpu.SMEM((count,), jnp.int32)] * 3
        + [pltpu.SMEM((count,), jnp.float32), pltpu.SemaphoreType.DMA((4,))]
        + [pltpu.VMEM((nodes, LANES), jnp.float32), pltpu.SemaphoreType.DMA, pltpu.SemaphoreType.DMA((4,))]
        + [pltpu.VMEM((nodes * (1 + PARTS), LANES), jnp.float32)] * ARRAYS,
        compiler_params=pltpu.CompilerParams(vmem_limit_bytes=52 * MIB),
        cost_estimate=cost(20),
    )(*operands)


def split3(left, right):
    dims = (((1,), (1,)), ((), ()))
    dot = functools.partial(lax.dot_general, dimension_numbers=dims, preferred_element_type=jnp.float32)
    (l_hi, l_lo), (r_hi, r_lo) = left, right
    return dot(l_hi, r_hi) + (dot(l_hi, r_lo) + dot(l_lo, r_hi))


def halves_of(value):
    high = value.astype(jnp.bfloat16)
    return high, (value - high.astype(jnp.float32)).astype(jnp.bfloat16)


def gram_kernel(place, ya_ref, yb_ref, a0_ref, b0_ref, *refs):
    *streams, out_ref, sums = refs
    snaps = ya_ref.shape[0]
    rings = out_ref.shape[0] // 4
    low = snaps // 2
    z, h, way = place[0], place[1], place[2]
    step = pl.program_id(0)

    @pl.when(step == 0)
    def _():
        sums[...] = jnp.zeros_like(sums)

    y = halves_of(jnp.concatenate([ya_ref[...], yb_ref[...]], axis=0))
    sums[0] += split3(halves_of(jnp.concatenate([a0_ref[...], b0_ref[...]], axis=0)), y)
    for distance, stream in enumerate(streams, 1):
        sums[distance] += split3(halves_of(stream[...]), y)

    @pl.when(step == pl.num_programs(0) - 1)
    def _():
        out_ref[...] = jnp.zeros_like(out_ref)
        for distance in range(1 + len(streams)):
            value = sums[distance]
            if distance == 0:
                value = 0.5 * value
            at = lax.rem(z - way * distance + rings, rings)
            for side in range(2):
                row = 2 * at + (h if side == 0 else 1 - h)
                upper, lower = value[side * snaps:side * snaps + low], value[side * snaps + low:(side + 1) * snaps]
                out_ref[2 * row + h] = jnp.concatenate([upper[:, :snaps], lower[:, :snaps]], axis=1)
                out_ref[2 * row + (1 - h)] = jnp.concatenate([upper[:, snaps:], lower[:, snaps:]], axis=1)


def gram_call(place, ya, yb, a0, b0, streams, rings):
    snaps, nodes = ya.shape
    chunk = nodes // 4
    single = pl.BlockSpec((snaps, chunk), lambda i: (0, i))
    double = pl.BlockSpec((2 * snaps, chunk), lambda i: (0, i))
    tiles = (4 * rings, snaps // 2, 2 * snaps)
    return pl.pallas_call(
        gram_kernel,
        grid=(nodes // chunk,),
        out_shape=jax.ShapeDtypeStruct(tiles, jnp.float32),
        in_specs=[IN_SMEM] + [single] * 4 + [double] * len(streams),
        out_specs=pl.BlockSpec(tiles, lambda i: (0, 0, 0)),
        scratch_shapes=[pltpu.VMEM((1 + len(streams), 2 * snaps, 2 * snaps), jnp.float32)],
        compiler_params=pltpu.CompilerParams(vmem_limit_bytes=40 * MIB),
        cost_estimate=cost(8),
    )(place, ya, yb, a0, b0, *streams)


def on_device(snapshots, connectivity, element_mass, lower_shared, upper_shared):
    snaps, nodes = snapshots.shape
    parts = lax.axis_size("mesh")
    blocks = lax.axis_size("snap")
    position = lax.axis_index("mesh")
    block = lax.axis_index("snap")
    rings = blocks // 2
    z, h = block // 2, block % 2
    half = nodes // 2
    tied = lax.optimization_barrier

    own = lax.dynamic_slice_in_dim(snapshots, h * half, half, 1)
    given = lax.dynamic_slice_in_dim(snapshots, (1 - h) * half, half, 1)
    a1 = ring_hop(own, 1)
    b1 = ring_hop(given, 1, cross=True)

    spread = (connectivity >> 3) * (8 * (1 + PARTS)) + (connectivity & 7)
    columns = tuple(spread[k] for k in range(3)) + (element_mass,)
    half_at = jnp.reshape(h, (1,)).astype(jnp.int32)
    (rows,) = apply_call(0, 3, columns, snapshots, None, half_at)

    rows, a1, b1 = tied((rows, a1, b1))
    pair1 = jnp.concatenate([a1, b1], axis=0)
    pair2 = ring_hop(pair1, 1)
    (rows,) = apply_call(1, 3, columns, snapshots, rows, half_at)

    rows, pair2 = tied((rows, pair2))
    pair3 = ring_hop(pair2, 1)
    b0 = partner(given)
    rows, y_own, y_given = apply_call(2, 3, columns, snapshots, rows, half_at)

    y_given, pair3, b0 = tied((y_given, pair3, b0))
    y_theirs = partner(y_given)
    pair4 = ring_hop(pair3, 1, closing=True)

    shared = lower_shared.shape[0]
    low, high = pl.pallas_call(
        gather_kernel,
        out_shape=[jax.ShapeDtypeStruct((snaps, shared), jnp.float32)] * 2,
        in_specs=[IN_SMEM] * 2 + [IN_VMEM],
        out_specs=[IN_VMEM] * 2,
        scratch_shapes=[pltpu.VMEM((shared, LANES), jnp.float32)],
        compiler_params=pltpu.CompilerParams(vmem_limit_bytes=12 * MIB),
        cost_estimate=cost(0.01),
    )(lower_shared, upper_shared, rows)
    from_below = passed_along(high, "mesh", 1)
    from_above = passed_along(low, "mesh", -1)
    weighted = pl.pallas_call(
        assemble_kernel,
        out_shape=jax.ShapeDtypeStruct((snaps, nodes), jnp.float32),
        in_specs=[IN_SMEM] * 2 + [ANYWHERE] + [IN_VMEM] * 2,
        out_specs=IN_VMEM,
        scratch_shapes=[pltpu.VMEM((nodes, LANES), jnp.float32)] + [pltpu.VMEM((shared, LANES), jnp.float32)] * 2
        + [pltpu.SemaphoreType.DMA],
        compiler_params=pltpu.CompilerParams(vmem_limit_bytes=20 * MIB),
        cost_estimate=cost(0.01),
    )(lower_shared, upper_shared, rows, from_below, from_above)
    weighted, y_theirs, pair4 = tied((weighted, y_theirs, pair4))

    place = jnp.stack([z, h, jnp.where(position % 2 == 0, 1, -1)]).astype(jnp.int32)
    tiles = gram_call(place, y_own, y_theirs, own, b0, [pair1, pair2, pair3, pair4], rings)
    planes = [[m * blocks + 2 * r + c for m in range(parts) for c in range(2)] for r in range(rings)]
    tile = jnp.sum(lax.all_to_all(tiles, ("mesh", "snap"), 0, 0, axis_index_groups=planes, tiled=True), axis=0)
    other = mirrored(tile)

    def unfolded(value):
        return jnp.concatenate([value[:, :snaps], value[:, snaps:]], axis=0)

    return weighted, (unfolded(tile).T + unfolded(other)) * (1.0 / float(parts * nodes))


def solution(mesh):
    placed = (P("snap", "mesh"), P(None, "mesh"), P("mesh"), P("mesh"), P("mesh"))
    return jax.shard_map(
        on_device,
        mesh=mesh,
        in_specs=placed,
        out_specs=(P("snap", "mesh"), P("snap", "mesh")),
        check_vma=False,
    )
```

```python
import functools

import jax
import jax.numpy as jnp
from jax import lax
from jax.experimental import pallas as pl
from jax.experimental.pallas import tpu as pltpu
from jax.sharding import PartitionSpec as P

LANES = 128
MIB = 2 ** 20


def ring_hop(value, steps, cross=False, closing=False):
    parts, blocks = lax.axis_size("mesh"), lax.axis_size("snap")
    rings = blocks // 2
    pairs = []
    for part in range(parts):
        way = 1 if part % 2 == 0 else -1
        for block in range(blocks):
            z, h = block // 2, block % 2
            target = (z + way * steps) % rings
            if closing and (target < rings // 2) != (part % 2 == 0):
                continue
            pairs.append((part * blocks + block, part * blocks + 2 * target + (h ^ 1 if cross else h)))
    return lax.ppermute(value, ("mesh", "snap"), pairs)


def passed_along(value, axis, steps):
    count = lax.axis_size(axis)
    leading, last = (max(0, -steps), min(count, count - steps))
    return lax.ppermute(value, axis, [(source, source + steps) for source in range(leading, last)])


def partner(value):
    return lax.ppermute(value, "snap", [(i, i ^ 1) for i in range(lax.axis_size("snap"))])


def mirrored(value):
    count = lax.axis_size("snap")
    return lax.ppermute(value, ("mesh", "snap"),
                        [(s * count + m, m * count + s) for m in range(count) for s in range(count)])


def apply_kernel(first, last, start, count, arrays, parts, *refs):
    refs = list(refs)
    a_hbm, b_hbm, c_hbm, m_hbm, x_ref = refs[:5]
    del refs[:5]
    rows_in = None if first else refs.pop(0)
    half_s = refs.pop(0) if last else None
    rows_out = refs.pop(0)
    y_outs = (refs.pop(0), refs.pop(0)) if last else None
    a_s, b_s, c_s, m_s, sems, sums, in_sem, out_sems, *zs = refs
    snaps, nodes = x_ref.shape
    tiles = LANES // 8
    width = 1 + parts
    copies = []
    for j, (source, target) in enumerate(zip((a_hbm, b_hbm, c_hbm, m_hbm), (a_s, b_s, c_s, m_s))):
        copy = pltpu.make_async_copy(source.at[pl.ds(start, count)], target, sems.at[j])
        copy.start()
        copies.append(copy)
    if not first:
        earlier = pltpu.make_async_copy(rows_in, sums, in_sem)
        earlier.start()

    def tile_of(block, i, part):
        return pl.ds(pl.multiple_of(block * (LANES * width) + (i * width + part) * 8, 8), 8)

    def prepare(block, carry):
        x = x_ref[:, pl.ds(pl.multiple_of(block * LANES, LANES), LANES)]
        rows = jnp.concatenate([x, x], axis=0).T
        blank = jnp.zeros((8, LANES), jnp.float32)
        for z in zs:
            for i in range(tiles):
                z[tile_of(block, i, 0), :] = rows[i * 8:(i + 1) * 8]
                for part in range(parts):
                    z[tile_of(block, i, 1 + part), :] = blank
        return carry

    lax.fori_loop(0, nodes // LANES, prepare, 0, unroll=2)
    for copy in copies:
        copy.wait()

    def elements(group, carry):
        for j, z in enumerate(zs):
            corners, updated = [], []
            for k in range(2 * parts):
                e = group * (arrays * 2 * parts) + (j * 2 * parts + k)
                corners.append((a_s[e], b_s[e], c_s[e]))
                mass = m_s[e]
                values = [z[pl.ds(n, 1), :] for n in corners[k]]
                held = [z[pl.ds(n + 8 * (1 + k // 2), 1), :] for n in corners[k]]
                total = values[0] + values[1] + values[2]
                updated.append([h + mass * (v + total) for h, v in zip(held, values)])
            for k in range(2 * parts):
                at = snaps * (k % 2)
                for n, new in zip(corners[k], updated[k]):
                    z[pl.ds(n + 8 * (1 + k // 2), 1), at:at + snaps] = new[:, at:at + snaps]
        return carry

    lax.fori_loop(0, count // (arrays * 2 * parts), elements, 0)

    if not first:
        earlier.wait()

    def finish(block):
        totals = []
        for i in range(tiles):
            total = None
            for z in zs:
                for part in range(parts):
                    value = z[tile_of(block, i, 1 + part), :]
                    total = value if total is None else total + value
            totals.append(total)
        total = jnp.concatenate(totals, axis=0)
        at = pl.multiple_of(block * LANES, LANES)
        if not first:
            total = total + sums[pl.ds(at, LANES), :]
        if last:
            total = total * (1.0 / 12.0)
        sums[pl.ds(at, LANES), :] = total
        return total

    pieces = out_sems.shape[0]
    size = nodes // pieces
    writes = []
    for piece in range(pieces):
        blocks = size // LANES
        begin = piece * blocks
        side = None
        if last:
            side = piece // (pieces // 2)
            begin = lax.rem(half_s[0] + side, 2) * (pieces // 2 * blocks) + piece % (pieces // 2) * blocks

        def inner(i, carry, begin=begin, side=side, piece=piece):
            total = finish(begin + i)
            if last:
                columns = total.T
                at = pl.multiple_of((piece % (pieces // 2) * blocks + i) * LANES, LANES)
                y_outs[side][:, pl.ds(at, LANES)] = columns[0:snaps, :] + columns[snaps:2 * snaps, :]
            return carry

        lax.fori_loop(0, blocks, inner, 0, unroll=2)
        at = pl.multiple_of(begin * LANES, LANES) if last else begin * LANES
        write = pltpu.make_async_copy(sums.at[pl.ds(at, size)], rows_out.at[pl.ds(at, size)], out_sems.at[piece])
        write.start()
        writes.append(write)
    for write in writes:
        write.wait()


def gather_kernel(low_s, up_s, rows, low_out, up_out, taken):
    snaps, shared = low_out.shape
    for list_s, out in ((low_s, low_out), (up_s, up_out)):
        def gather(i, carry, list_s=list_s):
            at = pl.multiple_of(i * 16, 16)
            for k in range(16):
                taken[pl.ds(at + k, 1), :] = rows[pl.ds(list_s[at + k], 1), :]
            return carry

        lax.fori_loop(0, shared // 16, gather, 0)
        for block in range(shared // LANES):
            at = block * LANES
            columns = taken[at:at + LANES, :].T
            out[:, at:at + LANES] = columns[0:snaps, :] + columns[snaps:2 * snaps, :]


def assemble_kernel(low_s, up_s, rows_ref, below_ref, above_ref, out_ref, rows, below, above, sem):
    snaps, shared = below_ref.shape
    nodes = rows_ref.shape[0]
    copy = pltpu.make_async_copy(rows_ref, rows, sem)
    copy.start()
    for received, taken in ((below_ref, below), (above_ref, above)):
        for block in range(shared // LANES):
            at = block * LANES
            value = received[:, at:at + LANES]
            taken[at:at + LANES, :] = jnp.concatenate([value, jnp.zeros_like(value)], axis=0).T
    copy.wait()
    for list_s, taken in ((low_s, below), (up_s, above)):
        def add(i, carry, list_s=list_s, taken=taken):
            at = pl.multiple_of(i * 16, 16)
            nodes_of = [list_s[at + k] for k in range(16)]
            new = [rows[pl.ds(n, 1), :] + taken[pl.ds(at + k, 1), :] for k, n in enumerate(nodes_of)]
            for n, value in zip(nodes_of, new):
                rows[pl.ds(n, 1), :] = value
            return carry

        lax.fori_loop(0, shared // 16, add, 0)

    def write(i, carry):
        at = pl.multiple_of(i * LANES, LANES)
        columns = rows[pl.ds(at, LANES), :].T
        out_ref[:, pl.ds(at, LANES)] = columns[0:snaps, :] + columns[snaps:2 * snaps, :]
        return carry

    lax.fori_loop(0, nodes // LANES, write, 0, unroll=4)


ANYWHERE = pl.BlockSpec(memory_space=pl.ANY)
IN_VMEM = pl.BlockSpec(memory_space=pltpu.VMEM)
IN_SMEM = pl.BlockSpec(memory_space=pltpu.SMEM)


def cost(micros):
    return pl.CostEstimate(flops=int(micros * 1e9), bytes_accessed=int(micros * 3e6), transcendentals=0)


ARRAYS, PARTS = 4, 2


def apply_call(index, calls, columns, snapshots, rows, half):
    first, last = index == 0, index == calls - 1
    snaps, nodes = snapshots.shape
    count = columns[0].shape[0] // calls
    row_shape = jax.ShapeDtypeStruct((nodes, LANES), jnp.float32)
    side = jax.ShapeDtypeStruct((snaps, nodes // 2), jnp.float32)
    operands = columns + (snapshots,) + (() if first else (rows,)) + ((half,) if last else ())
    return pl.pallas_call(
        functools.partial(apply_kernel, first, last, index * count, count, ARRAYS, PARTS),
        out_shape=[row_shape] + ([side, side] if last else []),
        in_specs=[ANYWHERE] * 4 + [IN_VMEM] + ([] if first else [ANYWHERE]) + ([IN_SMEM] if last else []),
        out_specs=[ANYWHERE] + ([IN_VMEM] * 2 if last else []),
        scratch_shapes=[pltpu.SMEM((count,), jnp.int32)] * 3
        + [pltpu.SMEM((count,), jnp.float32), pltpu.SemaphoreType.DMA((4,))]
        + [pltpu.VMEM((nodes, LANES), jnp.float32), pltpu.SemaphoreType.DMA, pltpu.SemaphoreType.DMA((4,))]
        + [pltpu.VMEM((nodes * (1 + PARTS), LANES), jnp.float32)] * ARRAYS,
        compiler_params=pltpu.CompilerParams(vmem_limit_bytes=52 * MIB),
        cost_estimate=cost(20),
    )(*operands)


def halves_of(value):
    high = value.astype(jnp.bfloat16)
    return high, (value - high.astype(jnp.float32)).astype(jnp.bfloat16)


def gram_kernel(place, ya_ref, yb_ref, a0_ref, b0_ref, *refs):
    *streams, out_ref, sums = refs
    snaps = ya_ref.shape[0]
    rings = out_ref.shape[0] // 4
    low = snaps // 2
    z, h, way = place[0], place[1], place[2]
    step = pl.program_id(0)

    @pl.when(step == 0)
    def _():
        sums[...] = jnp.zeros_like(sums)

    y_high, y_low = halves_of(jnp.concatenate([ya_ref[...], yb_ref[...]], axis=0))
    high, low_part = halves_of(jnp.concatenate([a0_ref[...], b0_ref[...]] + [stream[...] for stream in streams], axis=0))
    dot = functools.partial(lax.dot_general, dimension_numbers=(((1,), (1,)), ((), ())),
                            preferred_element_type=jnp.float32)
    both = dot(high, jnp.concatenate([y_high, y_low], axis=0))
    sums[...] += both[:, :2 * snaps] + (both[:, 2 * snaps:] + dot(low_part, y_high))

    @pl.when(step == pl.num_programs(0) - 1)
    def _():
        out_ref[...] = jnp.zeros_like(out_ref)
        for distance in range(1 + len(streams)):
            value = sums[2 * snaps * distance:2 * snaps * (distance + 1)]
            if distance == 0:
                value = 0.5 * value
            at = lax.rem(z - way * distance + rings, rings)
            for side in range(2):
                row = 2 * at + (h if side == 0 else 1 - h)
                upper, lower = value[side * snaps:side * snaps + low], value[side * snaps + low:(side + 1) * snaps]
                out_ref[2 * row + h] = jnp.concatenate([upper[:, :snaps], lower[:, :snaps]], axis=1)
                out_ref[2 * row + (1 - h)] = jnp.concatenate([upper[:, snaps:], lower[:, snaps:]], axis=1)


def gram_call(place, ya, yb, a0, b0, streams, rings):
    snaps, nodes = ya.shape
    chunk = nodes // 6
    single = pl.BlockSpec((snaps, chunk), lambda i: (0, i))
    double = pl.BlockSpec((2 * snaps, chunk), lambda i: (0, i))
    tiles = (4 * rings, snaps // 2, 2 * snaps)
    return pl.pallas_call(
        gram_kernel,
        grid=(nodes // chunk,),
        out_shape=jax.ShapeDtypeStruct(tiles, jnp.float32),
        in_specs=[IN_SMEM] + [single] * 4 + [double] * len(streams),
        out_specs=pl.BlockSpec(tiles, lambda i: (0, 0, 0)),
        scratch_shapes=[pltpu.VMEM(((1 + len(streams)) * 2 * snaps, 2 * snaps), jnp.float32)],
        compiler_params=pltpu.CompilerParams(vmem_limit_bytes=40 * MIB),
        cost_estimate=cost(8),
    )(place, ya, yb, a0, b0, *streams)


def on_device(snapshots, connectivity, element_mass, lower_shared, upper_shared):
    snaps, nodes = snapshots.shape
    parts = lax.axis_size("mesh")
    blocks = lax.axis_size("snap")
    position = lax.axis_index("mesh")
    block = lax.axis_index("snap")
    rings = blocks // 2
    z, h = block // 2, block % 2
    half = nodes // 2
    tied = lax.optimization_barrier

    own = lax.dynamic_slice_in_dim(snapshots, h * half, half, 1)
    given = lax.dynamic_slice_in_dim(snapshots, (1 - h) * half, half, 1)
    a1 = ring_hop(own, 1)
    b1 = ring_hop(given, 1, cross=True)

    spread = (connectivity >> 3) * (8 * (1 + PARTS)) + (connectivity & 7)
    columns = tuple(spread[k] for k in range(3)) + (element_mass,)
    half_at = jnp.reshape(h, (1,)).astype(jnp.int32)
    (rows,) = apply_call(0, 3, columns, snapshots, None, half_at)

    rows, a1, b1, given = tied((rows, a1, b1, given))
    pair1 = jnp.concatenate([a1, b1], axis=0)
    pair2 = ring_hop(pair1, 1)
    (rows,) = apply_call(1, 3, columns, snapshots, rows, half_at)

    rows, pair2 = tied((rows, pair2))
    pair3 = ring_hop(pair2, 1)
    b0 = partner(given)
    rows, y_own, y_given = apply_call(2, 3, columns, snapshots, rows, half_at)

    y_given, pair3, b0 = tied((y_given, pair3, b0))
    y_theirs = partner(y_given)
    pair4 = ring_hop(pair3, 1, closing=True)

    shared = lower_shared.shape[0]
    low, high = pl.pallas_call(
        gather_kernel,
        out_shape=[jax.ShapeDtypeStruct((snaps, shared), jnp.float32)] * 2,
        in_specs=[IN_SMEM] * 2 + [IN_VMEM],
        out_specs=[IN_VMEM] * 2,
        scratch_shapes=[pltpu.VMEM((shared, LANES), jnp.float32)],
        compiler_params=pltpu.CompilerParams(vmem_limit_bytes=12 * MIB),
        cost_estimate=cost(0.01),
    )(lower_shared, upper_shared, rows)
    from_below = passed_along(high, "mesh", 1)
    from_above = passed_along(low, "mesh", -1)
    weighted = pl.pallas_call(
        assemble_kernel,
        out_shape=jax.ShapeDtypeStruct((snaps, nodes), jnp.float32),
        in_specs=[IN_SMEM] * 2 + [ANYWHERE] + [IN_VMEM] * 2,
        out_specs=IN_VMEM,
        scratch_shapes=[pltpu.VMEM((nodes, LANES), jnp.float32)] + [pltpu.VMEM((shared, LANES), jnp.float32)] * 2
        + [pltpu.SemaphoreType.DMA],
        compiler_params=pltpu.CompilerParams(vmem_limit_bytes=20 * MIB),
        cost_estimate=cost(0.01),
    )(lower_shared, upper_shared, rows, from_below, from_above)
    weighted, y_theirs, pair4 = tied((weighted, y_theirs, pair4))

    place = jnp.stack([z, h, jnp.where(position % 2 == 0, 1, -1)]).astype(jnp.int32)
    tiles = gram_call(place, y_own, y_theirs, own, b0, [pair1, pair2, pair3, pair4], rings)
    planes = [[m * blocks + 2 * r + c for m in range(parts) for c in range(2)] for r in range(rings)]
    tile = jnp.sum(lax.all_to_all(tiles, ("mesh", "snap"), 0, 0, axis_index_groups=planes, tiled=True), axis=0)
    other = mirrored(tile)

    def unfolded(value):
        return jnp.concatenate([value[:, :snaps], value[:, snaps:]], axis=0)

    return weighted, (unfolded(tile).T + unfolded(other)) * (1.0 / float(parts * nodes))


def solution(mesh):
    placed = (P("snap", "mesh"), P(None, "mesh"), P("mesh"), P("mesh"), P("mesh"))
    return jax.shard_map(
        on_device,
        mesh=mesh,
        in_specs=placed,
        out_specs=(P("snap", "mesh"), P("snap", "mesh")),
        check_vma=False,
    )
```

```python
import functools

import jax
import jax.numpy as jnp
from jax import lax
from jax.experimental import pallas as pl
from jax.experimental.pallas import tpu as pltpu
from jax.sharding import PartitionSpec as P

LANES = 128
MIB = 2 ** 20


def ring_hop(value, steps, cross=False):
    parts, blocks = lax.axis_size("mesh"), lax.axis_size("snap")
    rings = blocks // 2
    pairs = []
    for part in range(parts):
        way = 1 if part % 2 == 0 else -1
        for block in range(blocks):
            z, h = block // 2, block % 2
            target = (z + way * steps) % rings
            pairs.append((part * blocks + block, part * blocks + 2 * target + (h ^ 1 if cross else h)))
    return lax.ppermute(value, ("mesh", "snap"), pairs)


def passed_along(value, axis, steps):
    count = lax.axis_size(axis)
    leading, last = (max(0, -steps), min(count, count - steps))
    return lax.ppermute(value, axis, [(source, source + steps) for source in range(leading, last)])


def partner(value):
    return lax.ppermute(value, "snap", [(i, i ^ 1) for i in range(lax.axis_size("snap"))])


def apply_kernel(first, last, start, count, arrays, parts, *refs):
    refs = list(refs)
    a_hbm, b_hbm, c_hbm, m_hbm, x_ref = refs[:5]
    del refs[:5]
    rows_in = None if first else refs.pop(0)
    half_s = refs.pop(0) if last else None
    rows_out = refs.pop(0)
    y_outs = (refs.pop(0), refs.pop(0)) if last else None
    a_s, b_s, c_s, m_s, sems, sums, in_sem, out_sems, *zs = refs
    snaps, nodes = x_ref.shape
    tiles = LANES // 8
    width = 1 + parts
    copies = []
    for j, (source, target) in enumerate(zip((a_hbm, b_hbm, c_hbm, m_hbm), (a_s, b_s, c_s, m_s))):
        copy = pltpu.make_async_copy(source.at[pl.ds(start, count)], target, sems.at[j])
        copy.start()
        copies.append(copy)
    if not first:
        earlier = pltpu.make_async_copy(rows_in, sums, in_sem)
        earlier.start()

    def tile_of(block, i, part):
        return pl.ds(pl.multiple_of(block * (LANES * width) + (i * width + part) * 8, 8), 8)

    def prepare(block, carry):
        x = x_ref[:, pl.ds(pl.multiple_of(block * LANES, LANES), LANES)]
        rows = jnp.concatenate([x, x], axis=0).T
        blank = jnp.zeros((8, LANES), jnp.float32)
        for z in zs:
            for i in range(tiles):
                z[tile_of(block, i, 0), :] = rows[i * 8:(i + 1) * 8]
                for part in range(parts):
                    z[tile_of(block, i, 1 + part), :] = blank
        return carry

    lax.fori_loop(0, nodes // LANES, prepare, 0, unroll=2)
    for copy in copies:
        copy.wait()

    def elements(group, carry):
        for j, z in enumerate(zs):
            corners, updated = [], []
            for k in range(2 * parts):
                e = group * (arrays * 2 * parts) + (j * 2 * parts + k)
                corners.append((a_s[e], b_s[e], c_s[e]))
                mass = m_s[e]
                values = [z[pl.ds(n, 1), :] for n in corners[k]]
                held = [z[pl.ds(n + 8 * (1 + k // 2), 1), :] for n in corners[k]]
                total = values[0] + values[1] + values[2]
                updated.append([h + mass * (v + total) for h, v in zip(held, values)])
            for k in range(2 * parts):
                at = snaps * (k % 2)
                for n, new in zip(corners[k], updated[k]):
                    z[pl.ds(n + 8 * (1 + k // 2), 1), at:at + snaps] = new[:, at:at + snaps]
        return carry

    lax.fori_loop(0, count // (arrays * 2 * parts), elements, 0)

    if not first:
        earlier.wait()

    def finish(block):
        totals = []
        for i in range(tiles):
            total = None
            for z in zs:
                for part in range(parts):
                    value = z[tile_of(block, i, 1 + part), :]
                    total = value if total is None else total + value
            totals.append(total)
        total = jnp.concatenate(totals, axis=0)
        at = pl.multiple_of(block * LANES, LANES)
        if not first:
            total = total + sums[pl.ds(at, LANES), :]
        if last:
            total = total * (1.0 / 12.0)
        sums[pl.ds(at, LANES), :] = total
        return total

    pieces = out_sems.shape[0]
    size = nodes // pieces
    writes = []
    for piece in range(pieces):
        blocks = size // LANES
        begin = piece * blocks
        side = None
        if last:
            side = piece // (pieces // 2)
            begin = lax.rem(half_s[0] + side, 2) * (pieces // 2 * blocks) + piece % (pieces // 2) * blocks

        def inner(i, carry, begin=begin, side=side, piece=piece):
            total = finish(begin + i)
            if last:
                columns = total.T
                at = pl.multiple_of((piece % (pieces // 2) * blocks + i) * LANES, LANES)
                y_outs[side][:, pl.ds(at, LANES)] = columns[0:snaps, :] + columns[snaps:2 * snaps, :]
            return carry

        lax.fori_loop(0, blocks, inner, 0, unroll=2)
        at = pl.multiple_of(begin * LANES, LANES) if last else begin * LANES
        write = pltpu.make_async_copy(sums.at[pl.ds(at, size)], rows_out.at[pl.ds(at, size)], out_sems.at[piece])
        write.start()
        writes.append(write)
    for write in writes:
        write.wait()


def gather_kernel(low_s, up_s, rows, low_out, up_out, taken):
    snaps, shared = low_out.shape
    for list_s, out in ((low_s, low_out), (up_s, up_out)):
        def gather(i, carry, list_s=list_s):
            at = pl.multiple_of(i * 16, 16)
            for k in range(16):
                taken[pl.ds(at + k, 1), :] = rows[pl.ds(list_s[at + k], 1), :]
            return carry

        lax.fori_loop(0, shared // 16, gather, 0)
        for block in range(shared // LANES):
            at = block * LANES
            columns = taken[at:at + LANES, :].T
            out[:, at:at + LANES] = columns[0:snaps, :] + columns[snaps:2 * snaps, :]


def assemble_kernel(low_s, up_s, rows_ref, below_ref, above_ref, out_ref, rows, below, above, sem):
    snaps, shared = below_ref.shape
    nodes = rows_ref.shape[0]
    copy = pltpu.make_async_copy(rows_ref, rows, sem)
    copy.start()
    for received, taken in ((below_ref, below), (above_ref, above)):
        for block in range(shared // LANES):
            at = block * LANES
            value = received[:, at:at + LANES]
            taken[at:at + LANES, :] = jnp.concatenate([value, jnp.zeros_like(value)], axis=0).T
    copy.wait()
    for list_s, taken in ((low_s, below), (up_s, above)):
        def add(i, carry, list_s=list_s, taken=taken):
            at = pl.multiple_of(i * 16, 16)
            nodes_of = [list_s[at + k] for k in range(16)]
            new = [rows[pl.ds(n, 1), :] + taken[pl.ds(at + k, 1), :] for k, n in enumerate(nodes_of)]
            for n, value in zip(nodes_of, new):
                rows[pl.ds(n, 1), :] = value
            return carry

        lax.fori_loop(0, shared // 16, add, 0)

    def write(i, carry):
        at = pl.multiple_of(i * LANES, LANES)
        columns = rows[pl.ds(at, LANES), :].T
        out_ref[:, pl.ds(at, LANES)] = columns[0:snaps, :] + columns[snaps:2 * snaps, :]
        return carry

    lax.fori_loop(0, nodes // LANES, write, 0, unroll=4)


ANYWHERE = pl.BlockSpec(memory_space=pl.ANY)
IN_VMEM = pl.BlockSpec(memory_space=pltpu.VMEM)
IN_SMEM = pl.BlockSpec(memory_space=pltpu.SMEM)


def cost(micros):
    return pl.CostEstimate(flops=int(micros * 1e9), bytes_accessed=int(micros * 3e6), transcendentals=0)


ARRAYS, PARTS = 4, 2


SHARES = (1, 1)


def apply_call(index, columns, snapshots, rows, half):
    calls = len(SHARES)
    first, last = index == 0, index == calls - 1
    snaps, nodes = snapshots.shape
    share = columns[0].shape[0] // sum(SHARES)
    start, count = share * sum(SHARES[:index]), share * SHARES[index]
    row_shape = jax.ShapeDtypeStruct((nodes, LANES), jnp.float32)
    side = jax.ShapeDtypeStruct((snaps, nodes // 2), jnp.float32)
    operands = columns + (snapshots,) + (() if first else (rows,)) + ((half,) if last else ())
    return pl.pallas_call(
        functools.partial(apply_kernel, first, last, start, count, ARRAYS, PARTS),
        out_shape=[row_shape] + ([side, side] if last else []),
        in_specs=[ANYWHERE] * 4 + [IN_VMEM] + ([] if first else [ANYWHERE]) + ([IN_SMEM] if last else []),
        out_specs=[ANYWHERE] + ([IN_VMEM] * 2 if last else []),
        scratch_shapes=[pltpu.SMEM((count,), jnp.int32)] * 3
        + [pltpu.SMEM((count,), jnp.float32), pltpu.SemaphoreType.DMA((4,))]
        + [pltpu.VMEM((nodes, LANES), jnp.float32), pltpu.SemaphoreType.DMA, pltpu.SemaphoreType.DMA((4,))]
        + [pltpu.VMEM((nodes * (1 + PARTS), LANES), jnp.float32)] * ARRAYS,
        compiler_params=pltpu.CompilerParams(vmem_limit_bytes=52 * MIB),
        cost_estimate=cost(20),
    )(*operands)


def halves_of(value):
    high = value.astype(jnp.bfloat16)
    return high, (value - high.astype(jnp.float32)).astype(jnp.bfloat16)


def product(x_of, ya_ref, yb_ref, row_sets):
    snaps, nodes = ya_ref.shape
    dot = functools.partial(lax.dot_general, dimension_numbers=(((1,), (1,)), ((), ())),
                            preferred_element_type=jnp.float32)
    chunk = nodes // 6
    totals = [None] * row_sets
    for i in range(6):
        at = slice(i * chunk, (i + 1) * chunk)
        y_high, y_low = halves_of(jnp.concatenate([ya_ref[:, at], yb_ref[:, at]], axis=0))
        both_y = jnp.concatenate([y_high, y_low], axis=0)
        for row_set in range(row_sets):
            high, low = halves_of(x_of(row_set, at))
            both = dot(high, both_y)
            value = both[:, :2 * snaps] + (both[:, 2 * snaps:] + dot(low, y_high))
            totals[row_set] = value if totals[row_set] is None else totals[row_set] + value
    return totals


def near_kernel(ya_ref, yb_ref, a0_ref, b0_ref, *refs):
    streams, out_ref, back = refs[:3], refs[3], refs[4:]

    def rows(distance, at):
        if distance == 0:
            return jnp.concatenate([a0_ref[:, at], b0_ref[:, at]], axis=0)
        return streams[distance - 1][:, at]

    for distance, value in enumerate(product(rows, ya_ref, yb_ref, 1 + len(streams))):
        out_ref[distance] = value
        if distance > 0:
            back[distance - 1][...] = value.T


def far_kernel(place, ya_ref, yb_ref, far_ref, near_ref, *refs):
    *back, out_ref = refs
    snaps = ya_ref.shape[0]
    rings = out_ref.shape[0] // 4
    low = snaps // 2
    z, h, way = place[0], place[1], place[2]

    def put(distance, value):
        at = lax.rem(z - way * distance + rings, rings)
        for side in range(2):
            row = 2 * at + (h if side == 0 else 1 - h)
            upper, lower = value[side * snaps:side * snaps + low], value[side * snaps + low:(side + 1) * snaps]
            out_ref[2 * row + h] = jnp.concatenate([upper[:, :snaps], lower[:, :snaps]], axis=1)
            out_ref[2 * row + (1 - h)] = jnp.concatenate([upper[:, snaps:], lower[:, snaps:]], axis=1)

    put(0, near_ref[0])
    for distance, received in enumerate(back, 1):
        put(distance, near_ref[distance])
        put(-distance, received[...])
    (value,) = product(lambda _, at: far_ref[:, at], ya_ref, yb_ref, 1)
    put(rings // 2, value)


def near_call(ya, yb, a0, b0, streams):
    snaps = ya.shape[0]
    square = jax.ShapeDtypeStruct((2 * snaps, 2 * snaps), jnp.float32)
    return pl.pallas_call(
        near_kernel,
        out_shape=[jax.ShapeDtypeStruct((1 + len(streams), 2 * snaps, 2 * snaps), jnp.float32)] + [square] * len(streams),
        in_specs=[IN_VMEM] * (4 + len(streams)),
        out_specs=[IN_VMEM] * (1 + len(streams)),
        compiler_params=pltpu.CompilerParams(vmem_limit_bytes=16 * MIB),
        cost_estimate=cost(4),
    )(ya, yb, a0, b0, *streams)


def far_call(place, ya, yb, far, near, back, rings):
    snaps = ya.shape[0]
    return pl.pallas_call(
        far_kernel,
        out_shape=jax.ShapeDtypeStruct((4 * rings, snaps // 2, 2 * snaps), jnp.float32),
        in_specs=[IN_SMEM] + [IN_VMEM] * (4 + len(back)),
        out_specs=IN_VMEM,
        compiler_params=pltpu.CompilerParams(vmem_limit_bytes=16 * MIB),
        cost_estimate=cost(2),
    )(place, ya, yb, far, near, *back)


def on_device(snapshots, connectivity, element_mass, lower_shared, upper_shared):
    snaps, nodes = snapshots.shape
    parts = lax.axis_size("mesh")
    blocks = lax.axis_size("snap")
    position = lax.axis_index("mesh")
    block = lax.axis_index("snap")
    rings = blocks // 2
    z, h = block // 2, block % 2
    half = nodes // 2
    tied = lax.optimization_barrier

    own = lax.dynamic_slice_in_dim(snapshots, h * half, half, 1)
    given = lax.dynamic_slice_in_dim(snapshots, (1 - h) * half, half, 1)
    a1 = ring_hop(own, 1)
    b1 = ring_hop(given, 1, cross=True)

    spread = (connectivity >> 3) * (8 * (1 + PARTS)) + (connectivity & 7)
    columns = tuple(spread[k] for k in range(3)) + (element_mass,)
    half_at = jnp.reshape(h, (1,)).astype(jnp.int32)
    (rows,) = apply_call(0, columns, snapshots, None, half_at)

    rows, a1, b1, given = tied((rows, a1, b1, given))
    pair1 = jnp.concatenate([a1, b1], axis=0)
    pair2 = ring_hop(pair1, 1)
    b0 = partner(given)
    rows, y_own, y_given = apply_call(1, columns, snapshots, rows, half_at)

    y_given, pair2, b0 = tied((y_given, pair2, b0))
    pair3 = ring_hop(pair2, 1)
    y_theirs = partner(y_given)

    shared = lower_shared.shape[0]
    low, high = pl.pallas_call(
        gather_kernel,
        out_shape=[jax.ShapeDtypeStruct((snaps, shared), jnp.float32)] * 2,
        in_specs=[IN_SMEM] * 2 + [IN_VMEM],
        out_specs=[IN_VMEM] * 2,
        scratch_shapes=[pltpu.VMEM((shared, LANES), jnp.float32)],
        compiler_params=pltpu.CompilerParams(vmem_limit_bytes=12 * MIB),
        cost_estimate=cost(0.01),
    )(lower_shared, upper_shared, rows)
    from_below = passed_along(high, "mesh", 1)
    from_above = passed_along(low, "mesh", -1)
    from_below, from_above, pair3, y_theirs = tied((from_below, from_above, pair3, y_theirs))
    pair4 = ring_hop(pair3, 1)
    weighted = pl.pallas_call(
        assemble_kernel,
        out_shape=jax.ShapeDtypeStruct((snaps, nodes), jnp.float32),
        in_specs=[IN_SMEM] * 2 + [ANYWHERE] + [IN_VMEM] * 2,
        out_specs=IN_VMEM,
        scratch_shapes=[pltpu.VMEM((nodes, LANES), jnp.float32)] + [pltpu.VMEM((shared, LANES), jnp.float32)] * 2
        + [pltpu.SemaphoreType.DMA],
        compiler_params=pltpu.CompilerParams(vmem_limit_bytes=20 * MIB),
        cost_estimate=cost(0.01),
    )(lower_shared, upper_shared, rows, from_below, from_above)
    weighted, y_theirs = tied((weighted, y_theirs))

    near, *back = near_call(y_own, y_theirs, own, b0, [pair1, pair2, pair3])
    back = [ring_hop(value, -distance) for distance, value in enumerate(back, 1)]
    place = jnp.stack([z, h, jnp.where(position % 2 == 0, 1, -1)]).astype(jnp.int32)
    tiles = far_call(place, y_own, y_theirs, pair4, near, back, rings)
    planes = [[m * blocks + 2 * r + c for m in range(parts) for c in range(2)] for r in range(rings)]
    tile = jnp.sum(lax.all_to_all(tiles, ("mesh", "snap"), 0, 0, axis_index_groups=planes, tiled=True), axis=0)
    column = jnp.concatenate([tile[:, :snaps], tile[:, snaps:]], axis=0)
    return weighted, column.T * (1.0 / float(parts * nodes))


def solution(mesh):
    placed = (P("snap", "mesh"), P(None, "mesh"), P("mesh"), P("mesh"), P("mesh"))
    return jax.shard_map(
        on_device,
        mesh=mesh,
        in_specs=placed,
        out_specs=(P("snap", "mesh"), P("snap", "mesh")),
        check_vma=False,
    )
```

```python
import functools

import jax
import jax.numpy as jnp
from jax import lax
from jax.experimental import pallas as pl
from jax.experimental.pallas import tpu as pltpu
from jax.sharding import PartitionSpec as P

LANES = 128
MIB = 2 ** 20


def ring_hop(value, steps, cross=False):
    parts, blocks = lax.axis_size("mesh"), lax.axis_size("snap")
    rings = blocks // 2
    pairs = []
    for part in range(parts):
        way = 1 if part % 2 == 0 else -1
        for block in range(blocks):
            z, h = block // 2, block % 2
            target = (z + way * steps) % rings
            pairs.append((part * blocks + block, part * blocks + 2 * target + (h ^ 1 if cross else h)))
    return lax.ppermute(value, ("mesh", "snap"), pairs)


def passed_along(value, axis, steps):
    count = lax.axis_size(axis)
    leading, last = (max(0, -steps), min(count, count - steps))
    return lax.ppermute(value, axis, [(source, source + steps) for source in range(leading, last)])


def partner(value):
    return lax.ppermute(value, "snap", [(i, i ^ 1) for i in range(lax.axis_size("snap"))])


def apply_kernel(first, last, start, count, arrays, parts, *refs):
    refs = list(refs)
    a_hbm, b_hbm, c_hbm, m_hbm, x_ref = refs[:5]
    del refs[:5]
    rows_in = None if first else refs.pop(0)
    half_s = refs.pop(0) if last else None
    rows_out = refs.pop(0)
    y_outs = (refs.pop(0), refs.pop(0)) if last else None
    a_s, b_s, c_s, m_s, sems, sums, in_sem, out_sems, *zs = refs
    snaps, nodes = x_ref.shape
    tiles = LANES // 8
    width = 1 + parts
    copies = []
    for j, (source, target) in enumerate(zip((a_hbm, b_hbm, c_hbm, m_hbm), (a_s, b_s, c_s, m_s))):
        copy = pltpu.make_async_copy(source.at[pl.ds(start, count)], target, sems.at[j])
        copy.start()
        copies.append(copy)
    if not first:
        earlier = pltpu.make_async_copy(rows_in, sums, in_sem)
        earlier.start()

    def tile_of(block, i, part):
        return pl.ds(pl.multiple_of(block * (LANES * width) + (i * width + part) * 8, 8), 8)

    def prepare(block, carry):
        x = x_ref[:, pl.ds(pl.multiple_of(block * LANES, LANES), LANES)]
        rows = jnp.concatenate([x, x], axis=0).T
        blank = jnp.zeros((8, LANES), jnp.float32)
        for z in zs:
            for i in range(tiles):
                z[tile_of(block, i, 0), :] = rows[i * 8:(i + 1) * 8]
                for part in range(parts):
                    z[tile_of(block, i, 1 + part), :] = blank
        return carry

    lax.fori_loop(0, nodes // LANES, prepare, 0, unroll=2)
    for copy in copies:
        copy.wait()

    def elements(group, carry):
        for j, z in enumerate(zs):
            corners, updated = [], []
            for k in range(2 * parts):
                e = group * (arrays * 2 * parts) + (j * 2 * parts + k)
                corners.append((a_s[e], b_s[e], c_s[e]))
                mass = m_s[e]
                values = [z[pl.ds(n, 1), :] for n in corners[k]]
                held = [z[pl.ds(n + 8 * (1 + k // 2), 1), :] for n in corners[k]]
                total = values[0] + values[1] + values[2]
                updated.append([h + mass * (v + total) for h, v in zip(held, values)])
            for k in range(2 * parts):
                at = snaps * (k % 2)
                for n, new in zip(corners[k], updated[k]):
                    z[pl.ds(n + 8 * (1 + k // 2), 1), at:at + snaps] = new[:, at:at + snaps]
        return carry

    lax.fori_loop(0, count // (arrays * 2 * parts), elements, 0)

    if not first:
        earlier.wait()

    def finish(block):
        totals = []
        for i in range(tiles):
            total = None
            for z in zs:
                for part in range(parts):
                    value = z[tile_of(block, i, 1 + part), :]
                    total = value if total is None else total + value
            totals.append(total)
        total = jnp.concatenate(totals, axis=0)
        at = pl.multiple_of(block * LANES, LANES)
        if not first:
            total = total + sums[pl.ds(at, LANES), :]
        if last:
            total = total * (1.0 / 12.0)
        sums[pl.ds(at, LANES), :] = total
        return total

    pieces = out_sems.shape[0]
    size = nodes // pieces
    writes = []
    for piece in range(pieces):
        blocks = size // LANES
        begin = piece * blocks
        side = None
        if last:
            side = piece // (pieces // 2)
            begin = lax.rem(half_s[0] + side, 2) * (pieces // 2 * blocks) + piece % (pieces // 2) * blocks

        def inner(i, carry, begin=begin, side=side, piece=piece):
            total = finish(begin + i)
            if last:
                columns = total.T
                at = pl.multiple_of((piece % (pieces // 2) * blocks + i) * LANES, LANES)
                y_outs[side][:, pl.ds(at, LANES)] = columns[0:snaps, :] + columns[snaps:2 * snaps, :]
            return carry

        lax.fori_loop(0, blocks, inner, 0, unroll=2)
        at = pl.multiple_of(begin * LANES, LANES) if last else begin * LANES
        write = pltpu.make_async_copy(sums.at[pl.ds(at, size)], rows_out.at[pl.ds(at, size)], out_sems.at[piece])
        write.start()
        writes.append(write)
    for write in writes:
        write.wait()


def gather_kernel(low_s, up_s, rows, low_out, up_out, taken):
    snaps, shared = low_out.shape
    for list_s, out in ((low_s, low_out), (up_s, up_out)):
        def gather(i, carry, list_s=list_s):
            at = pl.multiple_of(i * 16, 16)
            for k in range(16):
                taken[pl.ds(at + k, 1), :] = rows[pl.ds(list_s[at + k], 1), :]
            return carry

        lax.fori_loop(0, shared // 16, gather, 0)
        for block in range(shared // LANES):
            at = block * LANES
            columns = taken[at:at + LANES, :].T
            out[:, at:at + LANES] = columns[0:snaps, :] + columns[snaps:2 * snaps, :]


def assemble_kernel(low_s, up_s, rows_ref, below_ref, above_ref, out_ref, rows, below, above, sem):
    snaps, shared = below_ref.shape
    nodes = rows_ref.shape[0]
    copy = pltpu.make_async_copy(rows_ref, rows, sem)
    copy.start()
    for received, taken in ((below_ref, below), (above_ref, above)):
        for block in range(shared // LANES):
            at = block * LANES
            value = received[:, at:at + LANES]
            taken[at:at + LANES, :] = jnp.concatenate([value, jnp.zeros_like(value)], axis=0).T
    copy.wait()
    for list_s, taken in ((low_s, below), (up_s, above)):
        def add(i, carry, list_s=list_s, taken=taken):
            at = pl.multiple_of(i * 16, 16)
            nodes_of = [list_s[at + k] for k in range(16)]
            new = [rows[pl.ds(n, 1), :] + taken[pl.ds(at + k, 1), :] for k, n in enumerate(nodes_of)]
            for n, value in zip(nodes_of, new):
                rows[pl.ds(n, 1), :] = value
            return carry

        lax.fori_loop(0, shared // 16, add, 0)

    def write(i, carry):
        at = pl.multiple_of(i * LANES, LANES)
        columns = rows[pl.ds(at, LANES), :].T
        out_ref[:, pl.ds(at, LANES)] = columns[0:snaps, :] + columns[snaps:2 * snaps, :]
        return carry

    lax.fori_loop(0, nodes // LANES, write, 0, unroll=4)


ANYWHERE = pl.BlockSpec(memory_space=pl.ANY)
IN_VMEM = pl.BlockSpec(memory_space=pltpu.VMEM)
IN_SMEM = pl.BlockSpec(memory_space=pltpu.SMEM)


def cost(micros):
    return pl.CostEstimate(flops=int(micros * 1e9), bytes_accessed=int(micros * 3e6), transcendentals=0)


ARRAYS, PARTS = 4, 2


SHARES = (1, 1)


def apply_call(index, columns, snapshots, rows, half):
    calls = len(SHARES)
    first, last = index == 0, index == calls - 1
    snaps, nodes = snapshots.shape
    share = columns[0].shape[0] // sum(SHARES)
    start, count = share * sum(SHARES[:index]), share * SHARES[index]
    row_shape = jax.ShapeDtypeStruct((nodes, LANES), jnp.float32)
    side = jax.ShapeDtypeStruct((snaps, nodes // 2), jnp.float32)
    operands = columns + (snapshots,) + (() if first else (rows,)) + ((half,) if last else ())
    return pl.pallas_call(
        functools.partial(apply_kernel, first, last, start, count, ARRAYS, PARTS),
        out_shape=[row_shape] + ([side, side] if last else []),
        in_specs=[ANYWHERE] * 4 + [IN_VMEM] + ([] if first else [ANYWHERE]) + ([IN_SMEM] if last else []),
        out_specs=[ANYWHERE] + ([IN_VMEM] * 2 if last else []),
        scratch_shapes=[pltpu.SMEM((count,), jnp.int32)] * 3
        + [pltpu.SMEM((count,), jnp.float32), pltpu.SemaphoreType.DMA((4,))]
        + [pltpu.VMEM((nodes, LANES), jnp.float32), pltpu.SemaphoreType.DMA, pltpu.SemaphoreType.DMA((4,))]
        + [pltpu.VMEM((nodes * (1 + PARTS), LANES), jnp.float32)] * ARRAYS,
        compiler_params=pltpu.CompilerParams(vmem_limit_bytes=44 * MIB),
        cost_estimate=cost(20),
    )(*operands)


def halves_of(value):
    high = value.astype(jnp.bfloat16)
    return high, (value - high.astype(jnp.float32)).astype(jnp.bfloat16)


def product(x_of, ya_ref, yb_ref, row_sets):
    snaps, nodes = ya_ref.shape
    dot = functools.partial(lax.dot_general, dimension_numbers=(((1,), (1,)), ((), ())),
                            preferred_element_type=jnp.float32)
    chunk = nodes // 6
    totals = [None] * row_sets
    for i in range(6):
        at = slice(i * chunk, (i + 1) * chunk)
        y_high, y_low = halves_of(jnp.concatenate([ya_ref[:, at], yb_ref[:, at]], axis=0))
        both_y = jnp.concatenate([y_high, y_low], axis=0)
        for row_set in range(row_sets):
            high, low = halves_of(x_of(row_set, at))
            both = dot(high, both_y)
            value = both[:, :2 * snaps] + (both[:, 2 * snaps:] + dot(low, y_high))
            totals[row_set] = value if totals[row_set] is None else totals[row_set] + value
    return totals


def near_kernel(ya_ref, yb_ref, a0_ref, b0_ref, pair1_ref, pair2_ref, a3_ref, b3_ref, out_ref, *back):
    blocks = ((a0_ref, b0_ref), (pair1_ref,), (pair2_ref,), (a3_ref, b3_ref))

    def rows(distance, at):
        found = [ref[:, at] for ref in blocks[distance]]
        return found[0] if len(found) == 1 else jnp.concatenate(found, axis=0)

    for distance, value in enumerate(product(rows, ya_ref, yb_ref, len(blocks))):
        out_ref[distance] = value
        if distance > 0:
            back[distance - 1][...] = value.T


def far_kernel(place, ya_ref, yb_ref, a4_ref, b4_ref, near_ref, *refs):
    *back, out_ref = refs
    snaps = ya_ref.shape[0]
    rings = out_ref.shape[0] // 4
    low = snaps // 2
    z, h, way = place[0], place[1], place[2]

    def put(distance, value):
        at = lax.rem(z - way * distance + rings, rings)
        for side in range(2):
            row = 2 * at + (h if side == 0 else 1 - h)
            upper, lower = value[side * snaps:side * snaps + low], value[side * snaps + low:(side + 1) * snaps]
            out_ref[2 * row + h] = jnp.concatenate([upper[:, :snaps], lower[:, :snaps]], axis=1)
            out_ref[2 * row + (1 - h)] = jnp.concatenate([upper[:, snaps:], lower[:, snaps:]], axis=1)

    put(0, near_ref[0])
    for distance, received in enumerate(back, 1):
        put(distance, near_ref[distance])
        put(-distance, received[...])
    (value,) = product(lambda _, at: jnp.concatenate([a4_ref[:, at], b4_ref[:, at]], axis=0), ya_ref, yb_ref, 1)
    put(rings // 2, value)


def near_call(ya, yb, *blocks):
    snaps = ya.shape[0]
    square = jax.ShapeDtypeStruct((2 * snaps, 2 * snaps), jnp.float32)
    return pl.pallas_call(
        near_kernel,
        out_shape=[jax.ShapeDtypeStruct((4, 2 * snaps, 2 * snaps), jnp.float32)] + [square] * 3,
        in_specs=[IN_VMEM] * (2 + len(blocks)),
        out_specs=[IN_VMEM] * 4,
        compiler_params=pltpu.CompilerParams(vmem_limit_bytes=16 * MIB),
        cost_estimate=cost(0.01),
    )(ya, yb, *blocks)


def far_call(place, ya, yb, a4, b4, near, back, rings):
    snaps = ya.shape[0]
    return pl.pallas_call(
        far_kernel,
        out_shape=jax.ShapeDtypeStruct((4 * rings, snaps // 2, 2 * snaps), jnp.float32),
        in_specs=[IN_SMEM] + [IN_VMEM] * (5 + len(back)),
        out_specs=IN_VMEM,
        compiler_params=pltpu.CompilerParams(vmem_limit_bytes=16 * MIB),
        cost_estimate=cost(2),
    )(place, ya, yb, a4, b4, near, *back)


def on_device(snapshots, connectivity, element_mass, lower_shared, upper_shared):
    snaps, nodes = snapshots.shape
    parts = lax.axis_size("mesh")
    blocks = lax.axis_size("snap")
    position = lax.axis_index("mesh")
    block = lax.axis_index("snap")
    rings = blocks // 2
    z, h = block // 2, block % 2
    half = nodes // 2
    tied = lax.optimization_barrier

    own = lax.dynamic_slice_in_dim(snapshots, h * half, half, 1)
    given = lax.dynamic_slice_in_dim(snapshots, (1 - h) * half, half, 1)
    a1 = ring_hop(own, 1)
    b1 = ring_hop(given, 1, cross=True)

    spread = (connectivity >> 3) * (8 * (1 + PARTS)) + (connectivity & 7)
    columns = tuple(spread[k] for k in range(3)) + (element_mass,)
    half_at = jnp.reshape(h, (1,)).astype(jnp.int32)
    (rows,) = apply_call(0, columns, snapshots, None, half_at)

    rows, a1, b1, given = tied((rows, a1, b1, given))
    pair1 = jnp.concatenate([a1, b1], axis=0)
    pair2 = ring_hop(pair1, 1)
    b3 = ring_hop(b1, 2)
    b0 = partner(given)
    rows, y_own, y_given = apply_call(1, columns, snapshots, rows, half_at)

    y_given, pair2, b0 = tied((y_given, pair2, b0))
    a3 = ring_hop(pair2[:snaps], 1)
    y_theirs = partner(y_given)

    shared = lower_shared.shape[0]
    low, high = pl.pallas_call(
        gather_kernel,
        out_shape=[jax.ShapeDtypeStruct((snaps, shared), jnp.float32)] * 2,
        in_specs=[IN_SMEM] * 2 + [IN_VMEM],
        out_specs=[IN_VMEM] * 2,
        scratch_shapes=[pltpu.VMEM((shared, LANES), jnp.float32)],
        compiler_params=pltpu.CompilerParams(vmem_limit_bytes=12 * MIB),
        cost_estimate=cost(0.01),
    )(lower_shared, upper_shared, rows)
    from_below = passed_along(high, "mesh", 1)
    from_above = passed_along(low, "mesh", -1)
    from_below, from_above, b3 = tied((from_below, from_above, b3))
    b4 = ring_hop(b3, 1)
    from_below, from_above, a3, y_theirs = tied((from_below, from_above, a3, y_theirs))
    a4 = ring_hop(a3, 1)

    near, *back = near_call(y_own, y_theirs, own, b0, pair1, pair2, a3, b3)
    rows, near = tied((rows, near))
    back = [ring_hop(value, -distance) for distance, value in enumerate(back, 1)]
    weighted = pl.pallas_call(
        assemble_kernel,
        out_shape=jax.ShapeDtypeStruct((snaps, nodes), jnp.float32),
        in_specs=[IN_SMEM] * 2 + [ANYWHERE] + [IN_VMEM] * 2,
        out_specs=IN_VMEM,
        scratch_shapes=[pltpu.VMEM((nodes, LANES), jnp.float32)] + [pltpu.VMEM((shared, LANES), jnp.float32)] * 2
        + [pltpu.SemaphoreType.DMA],
        compiler_params=pltpu.CompilerParams(vmem_limit_bytes=20 * MIB),
        cost_estimate=cost(0.01),
    )(lower_shared, upper_shared, rows, from_below, from_above)
    weighted, *back = tied((weighted, *back))

    place = jnp.stack([z, h, jnp.where(position % 2 == 0, 1, -1)]).astype(jnp.int32)
    tiles = far_call(place, y_own, y_theirs, a4, b4, near, back, rings)
    planes = [[m * blocks + 2 * r + c for m in range(parts) for c in range(2)] for r in range(rings)]
    tile = jnp.sum(lax.all_to_all(tiles, ("mesh", "snap"), 0, 0, axis_index_groups=planes, tiled=True), axis=0)
    column = jnp.concatenate([tile[:, :snaps], tile[:, snaps:]], axis=0)
    return weighted, column.T * (1.0 / float(parts * nodes))


def solution(mesh):
    placed = (P("snap", "mesh"), P(None, "mesh"), P("mesh"), P("mesh"), P("mesh"))
    return jax.shard_map(
        on_device,
        mesh=mesh,
        in_specs=placed,
        out_specs=(P("snap", "mesh"), P("snap", "mesh")),
        check_vma=False,
    )
```

```python
import functools

import jax
import jax.numpy as jnp
from jax import lax
from jax.experimental import pallas as pl
from jax.experimental.pallas import tpu as pltpu
from jax.sharding import PartitionSpec as P

LANES = 128
MIB = 2 ** 20


def ring_hop(value, steps, cross=False):
    parts, blocks = lax.axis_size("mesh"), lax.axis_size("snap")
    rings = blocks // 2
    pairs = []
    for part in range(parts):
        way = 1 if part % 2 == 0 else -1
        for block in range(blocks):
            z, h = block // 2, block % 2
            target = (z + way * steps) % rings
            pairs.append((part * blocks + block, part * blocks + 2 * target + (h ^ 1 if cross else h)))
    return lax.ppermute(value, ("mesh", "snap"), pairs)


def passed_along(value, axis, steps):
    count = lax.axis_size(axis)
    leading, last = (max(0, -steps), min(count, count - steps))
    return lax.ppermute(value, axis, [(source, source + steps) for source in range(leading, last)])


def partner(value):
    return lax.ppermute(value, "snap", [(i, i ^ 1) for i in range(lax.axis_size("snap"))])


def apply_kernel(first, last, start, count, arrays, parts, *refs):
    refs = list(refs)
    a_hbm, b_hbm, c_hbm, m_hbm, x_ref = refs[:5]
    del refs[:5]
    rows_in = None if first else refs.pop(0)
    half_s = refs.pop(0) if last else None
    rows_out = refs.pop(0)
    y_outs = (refs.pop(0), refs.pop(0)) if last else None
    a_s, b_s, c_s, m_s, sems, sums, in_sem, out_sems, *zs = refs
    snaps, nodes = x_ref.shape
    tiles = LANES // 8
    width = 1 + parts
    copies = []
    for j, (source, target) in enumerate(zip((a_hbm, b_hbm, c_hbm, m_hbm), (a_s, b_s, c_s, m_s))):
        copy = pltpu.make_async_copy(source.at[pl.ds(start, count)], target, sems.at[j])
        copy.start()
        copies.append(copy)
    if not first:
        earlier = pltpu.make_async_copy(rows_in, sums, in_sem)
        earlier.start()

    def tile_of(block, i, part):
        return pl.ds(pl.multiple_of(block * (LANES * width) + (i * width + part) * 8, 8), 8)

    def prepare(block, carry):
        x = x_ref[:, pl.ds(pl.multiple_of(block * LANES, LANES), LANES)]
        rows = jnp.concatenate([x, x], axis=0).T
        blank = jnp.zeros((8, LANES), jnp.float32)
        for z in zs:
            for i in range(tiles):
                z[tile_of(block, i, 0), :] = rows[i * 8:(i + 1) * 8]
                for part in range(parts):
                    z[tile_of(block, i, 1 + part), :] = blank
        return carry

    lax.fori_loop(0, nodes // LANES, prepare, 0, unroll=2)
    for copy in copies:
        copy.wait()

    def elements(group, carry):
        for j, z in enumerate(zs):
            corners, updated = [], []
            for k in range(2 * parts):
                e = group * (arrays * 2 * parts) + (j * 2 * parts + k)
                corners.append((a_s[e], b_s[e], c_s[e]))
                mass = m_s[e]
                values = [z[pl.ds(n, 1), :] for n in corners[k]]
                held = [z[pl.ds(n + 8 * (1 + k // 2), 1), :] for n in corners[k]]
                total = values[0] + values[1] + values[2]
                updated.append([h + mass * (v + total) for h, v in zip(held, values)])
            for k in range(2 * parts):
                at = snaps * (k % 2)
                for n, new in zip(corners[k], updated[k]):
                    z[pl.ds(n + 8 * (1 + k // 2), 1), at:at + snaps] = new[:, at:at + snaps]
        return carry

    lax.fori_loop(0, count // (arrays * 2 * parts), elements, 0)

    if not first:
        earlier.wait()

    def finish(block):
        totals = []
        for i in range(tiles):
            total = None
            for z in zs:
                for part in range(parts):
                    value = z[tile_of(block, i, 1 + part), :]
                    total = value if total is None else total + value
            totals.append(total)
        total = jnp.concatenate(totals, axis=0)
        at = pl.multiple_of(block * LANES, LANES)
        if not first:
            total = total + sums[pl.ds(at, LANES), :]
        if last:
            total = total * (1.0 / 12.0)
        sums[pl.ds(at, LANES), :] = total
        return total

    pieces = out_sems.shape[0]
    size = nodes // pieces
    writes = []
    for piece in range(pieces):
        blocks = size // LANES
        begin = piece * blocks
        side = None
        if last:
            side = piece // (pieces // 2)
            begin = lax.rem(half_s[0] + side, 2) * (pieces // 2 * blocks) + piece % (pieces // 2) * blocks

        def inner(i, carry, begin=begin, side=side, piece=piece):
            total = finish(begin + i)
            if last:
                columns = total.T
                at = pl.multiple_of((piece % (pieces // 2) * blocks + i) * LANES, LANES)
                y_outs[side][:, pl.ds(at, LANES)] = columns[0:snaps, :] + columns[snaps:2 * snaps, :]
            return carry

        lax.fori_loop(0, blocks, inner, 0, unroll=2)
        at = pl.multiple_of(begin * LANES, LANES) if last else begin * LANES
        write = pltpu.make_async_copy(sums.at[pl.ds(at, size)], rows_out.at[pl.ds(at, size)], out_sems.at[piece])
        write.start()
        writes.append(write)
    for write in writes:
        write.wait()


def gather_kernel(low_s, up_s, rows, low_out, up_out, taken):
    snaps, shared = low_out.shape
    for list_s, out in ((low_s, low_out), (up_s, up_out)):
        def gather(i, carry, list_s=list_s):
            at = pl.multiple_of(i * 16, 16)
            for k in range(16):
                taken[pl.ds(at + k, 1), :] = rows[pl.ds(list_s[at + k], 1), :]
            return carry

        lax.fori_loop(0, shared // 16, gather, 0)
        for block in range(shared // LANES):
            at = block * LANES
            columns = taken[at:at + LANES, :].T
            out[:, at:at + LANES] = columns[0:snaps, :] + columns[snaps:2 * snaps, :]


def assemble_kernel(low_s, up_s, rows_ref, below_ref, above_ref, out_ref, rows, below, above, sem):
    snaps, shared = below_ref.shape
    nodes = rows_ref.shape[0]
    copy = pltpu.make_async_copy(rows_ref, rows, sem)
    copy.start()
    for received, taken in ((below_ref, below), (above_ref, above)):
        for block in range(shared // LANES):
            at = block * LANES
            value = received[:, at:at + LANES]
            taken[at:at + LANES, :] = jnp.concatenate([value, jnp.zeros_like(value)], axis=0).T
    copy.wait()
    for list_s, taken in ((low_s, below), (up_s, above)):
        def add(i, carry, list_s=list_s, taken=taken):
            at = pl.multiple_of(i * 16, 16)
            nodes_of = [list_s[at + k] for k in range(16)]
            new = [rows[pl.ds(n, 1), :] + taken[pl.ds(at + k, 1), :] for k, n in enumerate(nodes_of)]
            for n, value in zip(nodes_of, new):
                rows[pl.ds(n, 1), :] = value
            return carry

        lax.fori_loop(0, shared // 16, add, 0)

    def write(i, carry):
        at = pl.multiple_of(i * LANES, LANES)
        columns = rows[pl.ds(at, LANES), :].T
        out_ref[:, pl.ds(at, LANES)] = columns[0:snaps, :] + columns[snaps:2 * snaps, :]
        return carry

    lax.fori_loop(0, nodes // LANES, write, 0, unroll=4)


ANYWHERE = pl.BlockSpec(memory_space=pl.ANY)
IN_VMEM = pl.BlockSpec(memory_space=pltpu.VMEM)
IN_SMEM = pl.BlockSpec(memory_space=pltpu.SMEM)


def cost(micros):
    return pl.CostEstimate(flops=int(micros * 1e9), bytes_accessed=int(micros * 3e6), transcendentals=0)


ARRAYS, PARTS = 4, 2


SHARES = (1, 1)


def apply_call(index, columns, snapshots, rows, half):
    calls = len(SHARES)
    first, last = index == 0, index == calls - 1
    snaps, nodes = snapshots.shape
    share = columns[0].shape[0] // sum(SHARES)
    start, count = share * sum(SHARES[:index]), share * SHARES[index]
    row_shape = jax.ShapeDtypeStruct((nodes, LANES), jnp.float32)
    side = jax.ShapeDtypeStruct((snaps, nodes // 2), jnp.float32)
    operands = columns + (snapshots,) + (() if first else (rows,)) + ((half,) if last else ())
    return pl.pallas_call(
        functools.partial(apply_kernel, first, last, start, count, ARRAYS, PARTS),
        out_shape=[row_shape] + ([side, side] if last else []),
        in_specs=[ANYWHERE] * 4 + [IN_VMEM] + ([] if first else [ANYWHERE]) + ([IN_SMEM] if last else []),
        out_specs=[ANYWHERE] + ([IN_VMEM] * 2 if last else []),
        scratch_shapes=[pltpu.SMEM((count,), jnp.int32)] * 3
        + [pltpu.SMEM((count,), jnp.float32), pltpu.SemaphoreType.DMA((4,))]
        + [pltpu.VMEM((nodes, LANES), jnp.float32), pltpu.SemaphoreType.DMA, pltpu.SemaphoreType.DMA((4,))]
        + [pltpu.VMEM((nodes * (1 + PARTS), LANES), jnp.float32)] * ARRAYS,
        compiler_params=pltpu.CompilerParams(vmem_limit_bytes=44 * MIB),
        cost_estimate=cost(20),
    )(*operands)


def halves_of(value):
    high = value.astype(jnp.bfloat16)
    return high, (value - high.astype(jnp.float32)).astype(jnp.bfloat16)


def product(x_of, ya_ref, yb_ref, row_sets):
    snaps, nodes = ya_ref.shape
    dot = functools.partial(lax.dot_general, dimension_numbers=(((1,), (1,)), ((), ())),
                            preferred_element_type=jnp.float32)
    chunk = nodes // 6
    totals = [None] * row_sets
    for i in range(6):
        at = slice(i * chunk, (i + 1) * chunk)
        y_high, y_low = halves_of(jnp.concatenate([ya_ref[:, at], yb_ref[:, at]], axis=0))
        both_y = jnp.concatenate([y_high, y_low], axis=0)
        for row_set in range(row_sets):
            high, low = halves_of(x_of(row_set, at))
            both = dot(high, both_y)
            value = both[:, :2 * snaps] + (both[:, 2 * snaps:] + dot(low, y_high))
            totals[row_set] = value if totals[row_set] is None else totals[row_set] + value
    return totals


def near_kernel(*refs):
    sources, refs = refs[:7], refs[7:]
    out_ref, back, held, sems = refs[0], refs[1:4], refs[4:11], refs[11]
    copies = [pltpu.make_async_copy(source, target, sems.at[i]) for i, (source, target) in enumerate(zip(sources, held))]
    for copy in copies:
        copy.start()
    y_refs, blocks = held[:2], (held[2:4], held[4:5], held[5:6], held[6:7])
    waits = (copies[:4], copies[4:5], copies[5:6], copies[6:7])
    for distance, (block, waited) in enumerate(zip(blocks, waits)):
        for copy in waited:
            copy.wait()
        (value,) = product(lambda _, at, block=block: jnp.concatenate([ref[:, at] for ref in block], axis=0),
                           *y_refs, 1)
        out_ref[distance] = value
        if distance > 0:
            back[distance - 1][...] = value.T


def far_kernel(place, ya_ref, yb_ref, far_ref, near_ref, *refs):
    *back, out_ref = refs
    snaps = ya_ref.shape[0]
    rings = out_ref.shape[0] // 4
    low = snaps // 2
    z, h, way = place[0], place[1], place[2]

    def put(distance, value):
        at = lax.rem(z - way * distance + rings, rings)
        for side in range(2):
            row = 2 * at + (h if side == 0 else 1 - h)
            upper, lower = value[side * snaps:side * snaps + low], value[side * snaps + low:(side + 1) * snaps]
            out_ref[2 * row + h] = jnp.concatenate([upper[:, :snaps], lower[:, :snaps]], axis=1)
            out_ref[2 * row + (1 - h)] = jnp.concatenate([upper[:, snaps:], lower[:, snaps:]], axis=1)

    put(0, near_ref[0])
    for distance, received in enumerate(back, 1):
        put(distance, near_ref[distance])
        put(-distance, received[...])
    (value,) = product(lambda _, at: far_ref[:, at], ya_ref, yb_ref, 1)
    put(rings // 2, value)


def near_call(*operands):
    snaps = operands[0].shape[0]
    square = jax.ShapeDtypeStruct((2 * snaps, 2 * snaps), jnp.float32)
    return pl.pallas_call(
        near_kernel,
        out_shape=[jax.ShapeDtypeStruct((4, 2 * snaps, 2 * snaps), jnp.float32)] + [square] * 3,
        in_specs=[ANYWHERE] * len(operands),
        out_specs=[IN_VMEM] * 4,
        scratch_shapes=[pltpu.VMEM(operand.shape, operand.dtype) for operand in operands]
        + [pltpu.SemaphoreType.DMA((len(operands),))],
        compiler_params=pltpu.CompilerParams(vmem_limit_bytes=20 * MIB),
        cost_estimate=cost(0.01),
    )(*operands)


def far_call(place, ya, yb, far, near, back, rings):
    snaps = ya.shape[0]
    return pl.pallas_call(
        far_kernel,
        out_shape=jax.ShapeDtypeStruct((4 * rings, snaps // 2, 2 * snaps), jnp.float32),
        in_specs=[IN_SMEM] + [IN_VMEM] * (4 + len(back)),
        out_specs=IN_VMEM,
        compiler_params=pltpu.CompilerParams(vmem_limit_bytes=16 * MIB),
        cost_estimate=cost(2),
    )(place, ya, yb, far, near, *back)


def on_device(snapshots, connectivity, element_mass, lower_shared, upper_shared):
    snaps, nodes = snapshots.shape
    parts = lax.axis_size("mesh")
    blocks = lax.axis_size("snap")
    position = lax.axis_index("mesh")
    block = lax.axis_index("snap")
    rings = blocks // 2
    z, h = block // 2, block % 2
    half = nodes // 2
    tied = lax.optimization_barrier

    own = lax.dynamic_slice_in_dim(snapshots, h * half, half, 1)
    given = lax.dynamic_slice_in_dim(snapshots, (1 - h) * half, half, 1)
    a1 = ring_hop(own, 1)
    b1 = ring_hop(given, 1, cross=True)

    spread = (connectivity >> 3) * (8 * (1 + PARTS)) + (connectivity & 7)
    columns = tuple(spread[k] for k in range(3)) + (element_mass,)
    half_at = jnp.reshape(h, (1,)).astype(jnp.int32)
    (rows,) = apply_call(0, columns, snapshots, None, half_at)

    rows, a1, b1, given = tied((rows, a1, b1, given))
    pair1 = jnp.concatenate([a1, b1], axis=0)
    pair2 = ring_hop(pair1, 1)
    b0 = partner(given)
    rows, y_own, y_given = apply_call(1, columns, snapshots, rows, half_at)

    y_given, pair2, b0 = tied((y_given, pair2, b0))
    pair3 = ring_hop(pair2, 1)
    y_theirs = partner(y_given)

    shared = lower_shared.shape[0]
    low, high = pl.pallas_call(
        gather_kernel,
        out_shape=[jax.ShapeDtypeStruct((snaps, shared), jnp.float32)] * 2,
        in_specs=[IN_SMEM] * 2 + [IN_VMEM],
        out_specs=[IN_VMEM] * 2,
        scratch_shapes=[pltpu.VMEM((shared, LANES), jnp.float32)],
        compiler_params=pltpu.CompilerParams(vmem_limit_bytes=12 * MIB),
        cost_estimate=cost(0.01),
    )(lower_shared, upper_shared, rows)
    from_below = passed_along(high, "mesh", 1)
    from_above = passed_along(low, "mesh", -1)
    from_below, from_above, pair3, y_theirs = tied((from_below, from_above, pair3, y_theirs))
    pair4 = ring_hop(pair3, 1)
    near, *back = near_call(y_own, y_theirs, own, b0, pair1, pair2, pair3)
    rows, near = tied((rows, near))
    back = [ring_hop(value, -distance) for distance, value in enumerate(back, 1)]
    weighted = pl.pallas_call(
        assemble_kernel,
        out_shape=jax.ShapeDtypeStruct((snaps, nodes), jnp.float32),
        in_specs=[IN_SMEM] * 2 + [ANYWHERE] + [IN_VMEM] * 2,
        out_specs=IN_VMEM,
        scratch_shapes=[pltpu.VMEM((nodes, LANES), jnp.float32)] + [pltpu.VMEM((shared, LANES), jnp.float32)] * 2
        + [pltpu.SemaphoreType.DMA],
        compiler_params=pltpu.CompilerParams(vmem_limit_bytes=20 * MIB),
        cost_estimate=cost(0.01),
    )(lower_shared, upper_shared, rows, from_below, from_above)
    weighted, *back = tied((weighted, *back))
    place = jnp.stack([z, h, jnp.where(position % 2 == 0, 1, -1)]).astype(jnp.int32)
    tiles = far_call(place, y_own, y_theirs, pair4, near, back, rings)
    planes = [[m * blocks + 2 * r + c for m in range(parts) for c in range(2)] for r in range(rings)]
    tile = jnp.sum(lax.all_to_all(tiles, ("mesh", "snap"), 0, 0, axis_index_groups=planes, tiled=True), axis=0)
    column = jnp.concatenate([tile[:, :snaps], tile[:, snaps:]], axis=0)
    return weighted, column.T * (1.0 / float(parts * nodes))


def solution(mesh):
    placed = (P("snap", "mesh"), P(None, "mesh"), P("mesh"), P("mesh"), P("mesh"))
    return jax.shard_map(
        on_device,
        mesh=mesh,
        in_specs=placed,
        out_specs=(P("snap", "mesh"), P("snap", "mesh")),
        check_vma=False,
    )
```

```python
import functools

import jax
import jax.numpy as jnp
from jax import lax
from jax.experimental import pallas as pl
from jax.experimental.pallas import tpu as pltpu
from jax.sharding import PartitionSpec as P

LANES = 128
MIB = 2 ** 20


def ring_hop(value, steps, cross=False):
    parts, blocks = lax.axis_size("mesh"), lax.axis_size("snap")
    rings = blocks // 2
    pairs = []
    for part in range(parts):
        way = 1 if part % 2 == 0 else -1
        for block in range(blocks):
            z, h = block // 2, block % 2
            target = (z + way * steps) % rings
            pairs.append((part * blocks + block, part * blocks + 2 * target + (h ^ 1 if cross else h)))
    return lax.ppermute(value, ("mesh", "snap"), pairs)


def passed_along(value, axis, steps):
    count = lax.axis_size(axis)
    leading, last = (max(0, -steps), min(count, count - steps))
    return lax.ppermute(value, axis, [(source, source + steps) for source in range(leading, last)])


def partner(value):
    return lax.ppermute(value, "snap", [(i, i ^ 1) for i in range(lax.axis_size("snap"))])


def apply_kernel(first, last, start, count, arrays, parts, *refs):
    refs = list(refs)
    a_hbm, b_hbm, c_hbm, m_hbm, x_ref = refs[:5]
    del refs[:5]
    rows_in = None if first else refs.pop(0)
    half_s = refs.pop(0) if last else None
    rows_out = refs.pop(0)
    y_outs = (refs.pop(0), refs.pop(0)) if last else None
    a_s, b_s, c_s, m_s, sems, sums, in_sem, out_sems, *zs = refs
    snaps, nodes = x_ref.shape
    tiles = LANES // 8
    width = 1 + parts
    copies = []
    for j, (source, target) in enumerate(zip((a_hbm, b_hbm, c_hbm, m_hbm), (a_s, b_s, c_s, m_s))):
        copy = pltpu.make_async_copy(source.at[pl.ds(start, count)], target, sems.at[j])
        copy.start()
        copies.append(copy)
    if not first:
        earlier = pltpu.make_async_copy(rows_in, sums, in_sem)
        earlier.start()

    def tile_of(block, i, part):
        return pl.ds(pl.multiple_of(block * (LANES * width) + (i * width + part) * 8, 8), 8)

    def prepare(block, carry):
        x = x_ref[:, pl.ds(pl.multiple_of(block * LANES, LANES), LANES)]
        rows = jnp.concatenate([x, x], axis=0).T
        blank = jnp.zeros((8, LANES), jnp.float32)
        for z in zs:
            for i in range(tiles):
                z[tile_of(block, i, 0), :] = rows[i * 8:(i + 1) * 8]
                for part in range(parts):
                    z[tile_of(block, i, 1 + part), :] = blank
        return carry

    lax.fori_loop(0, nodes // LANES, prepare, 0, unroll=2)
    for copy in copies:
        copy.wait()

    def elements(group, carry):
        for j, z in enumerate(zs):
            corners, updated = [], []
            for k in range(2 * parts):
                e = group * (arrays * 2 * parts) + (j * 2 * parts + k)
                corners.append((a_s[e], b_s[e], c_s[e]))
                mass = m_s[e]
                values = [z[pl.ds(n, 1), :] for n in corners[k]]
                held = [z[pl.ds(n + 8 * (1 + k // 2), 1), :] for n in corners[k]]
                total = values[0] + values[1] + values[2]
                updated.append([h + mass * (v + total) for h, v in zip(held, values)])
            for k in range(2 * parts):
                at = snaps * (k % 2)
                for n, new in zip(corners[k], updated[k]):
                    z[pl.ds(n + 8 * (1 + k // 2), 1), at:at + snaps] = new[:, at:at + snaps]
        return carry

    lax.fori_loop(0, count // (arrays * 2 * parts), elements, 0, unroll=8)

    if not first:
        earlier.wait()

    def finish(block):
        totals = []
        for i in range(tiles):
            total = None
            for z in zs:
                for part in range(parts):
                    value = z[tile_of(block, i, 1 + part), :]
                    total = value if total is None else total + value
            totals.append(total)
        total = jnp.concatenate(totals, axis=0)
        at = pl.multiple_of(block * LANES, LANES)
        if not first:
            total = total + sums[pl.ds(at, LANES), :]
        if last:
            total = total * (1.0 / 12.0)
        sums[pl.ds(at, LANES), :] = total
        return total

    pieces = out_sems.shape[0]
    size = nodes // pieces
    writes = []
    for piece in range(pieces):
        blocks = size // LANES
        begin = piece * blocks
        side = None
        if last:
            side = piece // (pieces // 2)
            begin = lax.rem(half_s[0] + side, 2) * (pieces // 2 * blocks) + piece % (pieces // 2) * blocks

        def inner(i, carry, begin=begin, side=side, piece=piece):
            total = finish(begin + i)
            if last:
                columns = total.T
                at = pl.multiple_of((piece % (pieces // 2) * blocks + i) * LANES, LANES)
                y_outs[side][:, pl.ds(at, LANES)] = columns[0:snaps, :] + columns[snaps:2 * snaps, :]
            return carry

        lax.fori_loop(0, blocks, inner, 0, unroll=2)
        at = pl.multiple_of(begin * LANES, LANES) if last else begin * LANES
        write = pltpu.make_async_copy(sums.at[pl.ds(at, size)], rows_out.at[pl.ds(at, size)], out_sems.at[piece])
        write.start()
        writes.append(write)
    for write in writes:
        write.wait()


def gather_kernel(low_s, up_s, rows, low_out, up_out, taken):
    snaps, shared = low_out.shape
    for list_s, out in ((low_s, low_out), (up_s, up_out)):
        def gather(i, carry, list_s=list_s):
            at = pl.multiple_of(i * 16, 16)
            for k in range(16):
                taken[pl.ds(at + k, 1), :] = rows[pl.ds(list_s[at + k], 1), :]
            return carry

        lax.fori_loop(0, shared // 16, gather, 0)
        for block in range(shared // LANES):
            at = block * LANES
            columns = taken[at:at + LANES, :].T
            out[:, at:at + LANES] = columns[0:snaps, :] + columns[snaps:2 * snaps, :]


def assemble_kernel(low_s, up_s, rows_ref, below_ref, above_ref, out_ref, rows, below, above, sem):
    snaps, shared = below_ref.shape
    nodes = rows_ref.shape[0]
    copy = pltpu.make_async_copy(rows_ref, rows, sem)
    copy.start()
    for received, taken in ((below_ref, below), (above_ref, above)):
        for block in range(shared // LANES):
            at = block * LANES
            value = received[:, at:at + LANES]
            taken[at:at + LANES, :] = jnp.concatenate([value, jnp.zeros_like(value)], axis=0).T
    copy.wait()
    for list_s, taken in ((low_s, below), (up_s, above)):
        def add(i, carry, list_s=list_s, taken=taken):
            at = pl.multiple_of(i * 16, 16)
            nodes_of = [list_s[at + k] for k in range(16)]
            new = [rows[pl.ds(n, 1), :] + taken[pl.ds(at + k, 1), :] for k, n in enumerate(nodes_of)]
            for n, value in zip(nodes_of, new):
                rows[pl.ds(n, 1), :] = value
            return carry

        lax.fori_loop(0, shared // 16, add, 0)

    def write(i, carry):
        at = pl.multiple_of(i * LANES, LANES)
        columns = rows[pl.ds(at, LANES), :].T
        out_ref[:, pl.ds(at, LANES)] = columns[0:snaps, :] + columns[snaps:2 * snaps, :]
        return carry

    lax.fori_loop(0, nodes // LANES, write, 0, unroll=4)


ANYWHERE = pl.BlockSpec(memory_space=pl.ANY)
IN_VMEM = pl.BlockSpec(memory_space=pltpu.VMEM)
IN_SMEM = pl.BlockSpec(memory_space=pltpu.SMEM)


def cost(micros):
    return pl.CostEstimate(flops=int(micros * 1e9), bytes_accessed=int(micros * 3e6), transcendentals=0)


ARRAYS, PARTS = 4, 1


SHARES = (1, 1)


def apply_call(index, columns, snapshots, rows, half):
    calls = len(SHARES)
    first, last = index == 0, index == calls - 1
    snaps, nodes = snapshots.shape
    share = columns[0].shape[0] // sum(SHARES)
    start, count = share * sum(SHARES[:index]), share * SHARES[index]
    row_shape = jax.ShapeDtypeStruct((nodes, LANES), jnp.float32)
    side = jax.ShapeDtypeStruct((snaps, nodes // 2), jnp.float32)
    operands = columns + (snapshots,) + (() if first else (rows,)) + ((half,) if last else ())
    return pl.pallas_call(
        functools.partial(apply_kernel, first, last, start, count, ARRAYS, PARTS),
        out_shape=[row_shape] + ([side, side] if last else []),
        in_specs=[ANYWHERE] * 4 + [IN_VMEM] + ([] if first else [ANYWHERE]) + ([IN_SMEM] if last else []),
        out_specs=[ANYWHERE] + ([IN_VMEM] * 2 if last else []),
        scratch_shapes=[pltpu.SMEM((count,), jnp.int32)] * 3
        + [pltpu.SMEM((count,), jnp.float32), pltpu.SemaphoreType.DMA((4,))]
        + [pltpu.VMEM((nodes, LANES), jnp.float32), pltpu.SemaphoreType.DMA, pltpu.SemaphoreType.DMA((4,))]
        + [pltpu.VMEM((nodes * (1 + PARTS), LANES), jnp.float32)] * ARRAYS,
        compiler_params=pltpu.CompilerParams(vmem_limit_bytes=33 * MIB),
        cost_estimate=cost(20),
    )(*operands)


def halves_of(value):
    high = value.astype(jnp.bfloat16)
    return high, (value - high.astype(jnp.float32)).astype(jnp.bfloat16)


def product(x_of, ya_ref, yb_ref, row_sets):
    snaps, nodes = ya_ref.shape
    dot = functools.partial(lax.dot_general, dimension_numbers=(((1,), (1,)), ((), ())),
                            preferred_element_type=jnp.float32)
    chunk = nodes // 6
    totals = [None] * row_sets
    for i in range(6):
        at = slice(i * chunk, (i + 1) * chunk)
        y_high, y_low = halves_of(jnp.concatenate([ya_ref[:, at], yb_ref[:, at]], axis=0))
        both_y = jnp.concatenate([y_high, y_low], axis=0)
        for row_set in range(row_sets):
            high, low = halves_of(x_of(row_set, at))
            both = dot(high, both_y)
            value = both[:, :2 * snaps] + (both[:, 2 * snaps:] + dot(low, y_high))
            totals[row_set] = value if totals[row_set] is None else totals[row_set] + value
    return totals


def near_kernel(*refs):
    sources, refs = refs[:7], refs[7:]
    out_ref, back, held, sems = refs[0], refs[1:4], refs[4:11], refs[11]
    copies = [pltpu.make_async_copy(source, target, sems.at[i]) for i, (source, target) in enumerate(zip(sources, held))]
    for copy in copies:
        copy.start()
    y_refs, blocks = held[:2], (held[2:4], held[4:5], held[5:6], held[6:7])
    waits = (copies[:4], copies[4:5], copies[5:6], copies[6:7])
    for distance, (block, waited) in enumerate(zip(blocks, waits)):
        for copy in waited:
            copy.wait()
        (value,) = product(lambda _, at, block=block: jnp.concatenate([ref[:, at] for ref in block], axis=0),
                           *y_refs, 1)
        out_ref[distance] = value
        if distance > 0:
            back[distance - 1][...] = value.T


def far_kernel(place, ya_ref, yb_ref, far_ref, near_ref, *refs):
    *back, out_ref = refs
    snaps = ya_ref.shape[0]
    rings = out_ref.shape[0] // 4
    low = snaps // 2
    z, h, way = place[0], place[1], place[2]

    def put(distance, value):
        at = lax.rem(z - way * distance + rings, rings)
        for side in range(2):
            row = 2 * at + (h if side == 0 else 1 - h)
            upper, lower = value[side * snaps:side * snaps + low], value[side * snaps + low:(side + 1) * snaps]
            out_ref[2 * row + h] = jnp.concatenate([upper[:, :snaps], lower[:, :snaps]], axis=1)
            out_ref[2 * row + (1 - h)] = jnp.concatenate([upper[:, snaps:], lower[:, snaps:]], axis=1)

    put(0, near_ref[0])
    for distance, received in enumerate(back, 1):
        put(distance, near_ref[distance])
        put(-distance, received[...])
    (value,) = product(lambda _, at: far_ref[:, at], ya_ref, yb_ref, 1)
    put(rings // 2, value)


def near_call(*operands):
    snaps = operands[0].shape[0]
    square = jax.ShapeDtypeStruct((2 * snaps, 2 * snaps), jnp.float32)
    return pl.pallas_call(
        near_kernel,
        out_shape=[jax.ShapeDtypeStruct((4, 2 * snaps, 2 * snaps), jnp.float32)] + [square] * 3,
        in_specs=[ANYWHERE] * len(operands),
        out_specs=[IN_VMEM] * 4,
        scratch_shapes=[pltpu.VMEM(operand.shape, operand.dtype) for operand in operands]
        + [pltpu.SemaphoreType.DMA((len(operands),))],
        compiler_params=pltpu.CompilerParams(vmem_limit_bytes=20 * MIB),
        cost_estimate=cost(0.01),
    )(*operands)


def far_call(place, ya, yb, far, near, back, rings):
    snaps = ya.shape[0]
    return pl.pallas_call(
        far_kernel,
        out_shape=jax.ShapeDtypeStruct((4 * rings, snaps // 2, 2 * snaps), jnp.float32),
        in_specs=[IN_SMEM] + [IN_VMEM] * (4 + len(back)),
        out_specs=IN_VMEM,
        compiler_params=pltpu.CompilerParams(vmem_limit_bytes=16 * MIB),
        cost_estimate=cost(2),
    )(place, ya, yb, far, near, *back)


def on_device(snapshots, connectivity, element_mass, lower_shared, upper_shared):
    snaps, nodes = snapshots.shape
    parts = lax.axis_size("mesh")
    blocks = lax.axis_size("snap")
    position = lax.axis_index("mesh")
    block = lax.axis_index("snap")
    rings = blocks // 2
    z, h = block // 2, block % 2
    half = nodes // 2
    tied = lax.optimization_barrier

    own = lax.dynamic_slice_in_dim(snapshots, h * half, half, 1)
    given = lax.dynamic_slice_in_dim(snapshots, (1 - h) * half, half, 1)
    a1 = ring_hop(own, 1)
    b1 = ring_hop(given, 1, cross=True)

    spread = (connectivity >> 3) * (8 * (1 + PARTS)) + (connectivity & 7)
    columns = tuple(spread[k] for k in range(3)) + (element_mass,)
    half_at = jnp.reshape(h, (1,)).astype(jnp.int32)
    (rows,) = apply_call(0, columns, snapshots, None, half_at)

    rows, a1, b1, given = tied((rows, a1, b1, given))
    pair1 = jnp.concatenate([a1, b1], axis=0)
    pair2 = ring_hop(pair1, 1)
    b0 = partner(given)
    rows, y_own, y_given = apply_call(1, columns, snapshots, rows, half_at)

    y_given, pair2, b0 = tied((y_given, pair2, b0))
    pair3 = ring_hop(pair2, 1)
    y_theirs = partner(y_given)

    shared = lower_shared.shape[0]
    low, high = pl.pallas_call(
        gather_kernel,
        out_shape=[jax.ShapeDtypeStruct((snaps, shared), jnp.float32)] * 2,
        in_specs=[IN_SMEM] * 2 + [IN_VMEM],
        out_specs=[IN_VMEM] * 2,
        scratch_shapes=[pltpu.VMEM((shared, LANES), jnp.float32)],
        compiler_params=pltpu.CompilerParams(vmem_limit_bytes=12 * MIB),
        cost_estimate=cost(0.01),
    )(lower_shared, upper_shared, rows)
    from_below = passed_along(high, "mesh", 1)
    from_above = passed_along(low, "mesh", -1)
    from_below, from_above, pair3, y_theirs = tied((from_below, from_above, pair3, y_theirs))
    pair4 = ring_hop(pair3, 1)
    near, *back = near_call(y_own, y_theirs, own, b0, pair1, pair2, pair3)
    rows, near = tied((rows, near))
    back = [ring_hop(value, -distance) for distance, value in enumerate(back, 1)]
    weighted = pl.pallas_call(
        assemble_kernel,
        out_shape=jax.ShapeDtypeStruct((snaps, nodes), jnp.float32),
        in_specs=[IN_SMEM] * 2 + [ANYWHERE] + [IN_VMEM] * 2,
        out_specs=IN_VMEM,
        scratch_shapes=[pltpu.VMEM((nodes, LANES), jnp.float32)] + [pltpu.VMEM((shared, LANES), jnp.float32)] * 2
        + [pltpu.SemaphoreType.DMA],
        compiler_params=pltpu.CompilerParams(vmem_limit_bytes=20 * MIB),
        cost_estimate=cost(0.01),
    )(lower_shared, upper_shared, rows, from_below, from_above)
    weighted, *back = tied((weighted, *back))
    place = jnp.stack([z, h, jnp.where(position % 2 == 0, 1, -1)]).astype(jnp.int32)
    tiles = far_call(place, y_own, y_theirs, pair4, near, back, rings)
    planes = [[m * blocks + 2 * r + c for m in range(parts) for c in range(2)] for r in range(rings)]
    tile = jnp.sum(lax.all_to_all(tiles, ("mesh", "snap"), 0, 0, axis_index_groups=planes, tiled=True), axis=0)
    column = jnp.concatenate([tile[:, :snaps], tile[:, snaps:]], axis=0)
    return weighted, column.T * (1.0 / float(parts * nodes))


def solution(mesh):
    placed = (P("snap", "mesh"), P(None, "mesh"), P("mesh"), P("mesh"), P("mesh"))
    return jax.shard_map(
        on_device,
        mesh=mesh,
        in_specs=placed,
        out_specs=(P("snap", "mesh"), P("snap", "mesh")),
        check_vma=False,
    )
```

```python
import functools

import jax
import jax.numpy as jnp
from jax import lax
from jax.experimental import pallas as pl
from jax.experimental.pallas import tpu as pltpu
from jax.sharding import PartitionSpec as P

LANES = 128
MIB = 2 ** 20


def ring_hop(value, steps, cross=False):
    parts, blocks = lax.axis_size("mesh"), lax.axis_size("snap")
    rings = blocks // 2
    pairs = []
    for part in range(parts):
        way = 1 if part % 2 == 0 else -1
        for block in range(blocks):
            z, h = block // 2, block % 2
            target = (z + way * steps) % rings
            pairs.append((part * blocks + block, part * blocks + 2 * target + (h ^ 1 if cross else h)))
    return lax.ppermute(value, ("mesh", "snap"), pairs)


def passed_along(value, axis, steps):
    count = lax.axis_size(axis)
    leading, last = (max(0, -steps), min(count, count - steps))
    return lax.ppermute(value, axis, [(source, source + steps) for source in range(leading, last)])


def partner(value):
    return lax.ppermute(value, "snap", [(i, i ^ 1) for i in range(lax.axis_size("snap"))])


def apply_kernel(first, last, start, count, arrays, parts, *refs):
    refs = list(refs)
    a_hbm, b_hbm, c_hbm, m_hbm, x_ref = refs[:5]
    del refs[:5]
    rows_in = None if first else refs.pop(0)
    half_s = refs.pop(0) if last else None
    rows_out = refs.pop(0)
    y_outs = (refs.pop(0), refs.pop(0)) if last else None
    a_s, b_s, c_s, m_s, sems, sums, in_sem, out_sems, *zs = refs
    snaps, nodes = x_ref.shape
    tiles = LANES // 8
    width = 1 + parts
    copies = []
    for j, (source, target) in enumerate(zip((a_hbm, b_hbm, c_hbm, m_hbm), (a_s, b_s, c_s, m_s))):
        copy = pltpu.make_async_copy(source.at[pl.ds(start, count)], target, sems.at[j])
        copy.start()
        copies.append(copy)
    if not first:
        earlier = pltpu.make_async_copy(rows_in, sums, in_sem)
        earlier.start()

    def tile_of(block, i, part):
        return pl.ds(pl.multiple_of(block * (LANES * width) + (i * width + part) * 8, 8), 8)

    def prepare(block, carry):
        x = x_ref[:, pl.ds(pl.multiple_of(block * LANES, LANES), LANES)]
        rows = jnp.concatenate([x, x], axis=0).T
        blank = jnp.zeros((8, LANES), jnp.float32)
        for z in zs:
            for i in range(tiles):
                z[tile_of(block, i, 0), :] = rows[i * 8:(i + 1) * 8]
                for part in range(parts):
                    z[tile_of(block, i, 1 + part), :] = blank
        return carry

    lax.fori_loop(0, nodes // LANES, prepare, 0, unroll=2)
    for copy in copies:
        copy.wait()

    def elements(group, carry):
        for j, z in enumerate(zs):
            corners, updated = [], []
            for k in range(2 * parts):
                e = group * (arrays * 2 * parts) + (j * 2 * parts + k)
                corners.append((a_s[e], b_s[e], c_s[e]))
                mass = m_s[e]
                values = [z[pl.ds(n, 1), :] for n in corners[k]]
                held = [z[pl.ds(n + 8 * (1 + k // 2), 1), :] for n in corners[k]]
                total = values[0] + values[1] + values[2]
                updated.append([h + mass * (v + total) for h, v in zip(held, values)])
            for k in range(2 * parts):
                at = snaps * (k % 2)
                for n, new in zip(corners[k], updated[k]):
                    z[pl.ds(n + 8 * (1 + k // 2), 1), at:at + snaps] = new[:, at:at + snaps]
        return carry

    lax.fori_loop(0, count // (arrays * 2 * parts), elements, 0, unroll=8)

    if not first:
        earlier.wait()

    def finish(block):
        totals = []
        for i in range(tiles):
            total = None
            for z in zs:
                for part in range(parts):
                    value = z[tile_of(block, i, 1 + part), :]
                    total = value if total is None else total + value
            totals.append(total)
        total = jnp.concatenate(totals, axis=0)
        at = pl.multiple_of(block * LANES, LANES)
        if not first:
            total = total + sums[pl.ds(at, LANES), :]
        if last:
            total = total * (1.0 / 12.0)
        sums[pl.ds(at, LANES), :] = total
        return total

    pieces = out_sems.shape[0]
    size = nodes // pieces
    writes = []
    for piece in range(pieces):
        blocks = size // LANES
        begin = piece * blocks
        side = None
        if last:
            side = piece // (pieces // 2)
            begin = lax.rem(half_s[0] + side, 2) * (pieces // 2 * blocks) + piece % (pieces // 2) * blocks

        def inner(i, carry, begin=begin, side=side, piece=piece):
            total = finish(begin + i)
            if last:
                columns = total.T
                at = pl.multiple_of((piece % (pieces // 2) * blocks + i) * LANES, LANES)
                y_outs[side][:, pl.ds(at, LANES)] = columns[0:snaps, :] + columns[snaps:2 * snaps, :]
            return carry

        lax.fori_loop(0, blocks, inner, 0, unroll=2)
        at = pl.multiple_of(begin * LANES, LANES) if last else begin * LANES
        write = pltpu.make_async_copy(sums.at[pl.ds(at, size)], rows_out.at[pl.ds(at, size)], out_sems.at[piece])
        write.start()
        writes.append(write)
    for write in writes:
        write.wait()


def gather_kernel(low_s, up_s, rows, low_out, up_out, taken):
    snaps, shared = low_out.shape
    for list_s, out in ((low_s, low_out), (up_s, up_out)):
        def gather(i, carry, list_s=list_s):
            at = pl.multiple_of(i * 16, 16)
            for k in range(16):
                taken[pl.ds(at + k, 1), :] = rows[pl.ds(list_s[at + k], 1), :]
            return carry

        lax.fori_loop(0, shared // 16, gather, 0)
        for block in range(shared // LANES):
            at = block * LANES
            columns = taken[at:at + LANES, :].T
            out[:, at:at + LANES] = columns[0:snaps, :] + columns[snaps:2 * snaps, :]


def assemble_kernel(low_s, up_s, rows_ref, below_ref, above_ref, out_ref, rows, below, above, sem):
    snaps, shared = below_ref.shape
    nodes = rows_ref.shape[0]
    copy = pltpu.make_async_copy(rows_ref, rows, sem)
    copy.start()
    for received, taken in ((below_ref, below), (above_ref, above)):
        for block in range(shared // LANES):
            at = block * LANES
            value = received[:, at:at + LANES]
            taken[at:at + LANES, :] = jnp.concatenate([value, jnp.zeros_like(value)], axis=0).T
    copy.wait()
    for list_s, taken in ((low_s, below), (up_s, above)):
        def add(i, carry, list_s=list_s, taken=taken):
            at = pl.multiple_of(i * 16, 16)
            nodes_of = [list_s[at + k] for k in range(16)]
            new = [rows[pl.ds(n, 1), :] + taken[pl.ds(at + k, 1), :] for k, n in enumerate(nodes_of)]
            for n, value in zip(nodes_of, new):
                rows[pl.ds(n, 1), :] = value
            return carry

        lax.fori_loop(0, shared // 16, add, 0)

    def write(i, carry):
        at = pl.multiple_of(i * LANES, LANES)
        columns = rows[pl.ds(at, LANES), :].T
        out_ref[:, pl.ds(at, LANES)] = columns[0:snaps, :] + columns[snaps:2 * snaps, :]
        return carry

    lax.fori_loop(0, nodes // LANES, write, 0, unroll=4)


ANYWHERE = pl.BlockSpec(memory_space=pl.ANY)
IN_VMEM = pl.BlockSpec(memory_space=pltpu.VMEM)
IN_SMEM = pl.BlockSpec(memory_space=pltpu.SMEM)


def cost(micros):
    return pl.CostEstimate(flops=int(micros * 1e9), bytes_accessed=int(micros * 3e6), transcendentals=0)


ARRAYS, PARTS = 4, 1


SHARES = (7, 5)


def apply_call(index, columns, snapshots, rows, half):
    calls = len(SHARES)
    first, last = index == 0, index == calls - 1
    snaps, nodes = snapshots.shape
    share = columns[0].shape[0] // sum(SHARES)
    start, count = share * sum(SHARES[:index]), share * SHARES[index]
    row_shape = jax.ShapeDtypeStruct((nodes, LANES), jnp.float32)
    side = jax.ShapeDtypeStruct((snaps, nodes // 2), jnp.float32)
    operands = columns + (snapshots,) + (() if first else (rows,)) + ((half,) if last else ())
    return pl.pallas_call(
        functools.partial(apply_kernel, first, last, start, count, ARRAYS, PARTS),
        out_shape=[row_shape] + ([side, side] if last else []),
        in_specs=[ANYWHERE] * 4 + [IN_VMEM] + ([] if first else [ANYWHERE]) + ([IN_SMEM] if last else []),
        out_specs=[ANYWHERE] + ([IN_VMEM] * 2 if last else []),
        scratch_shapes=[pltpu.SMEM((count,), jnp.int32)] * 3
        + [pltpu.SMEM((count,), jnp.float32), pltpu.SemaphoreType.DMA((4,))]
        + [pltpu.VMEM((nodes, LANES), jnp.float32), pltpu.SemaphoreType.DMA, pltpu.SemaphoreType.DMA((4,))]
        + [pltpu.VMEM((nodes * (1 + PARTS), LANES), jnp.float32)] * ARRAYS,
        compiler_params=pltpu.CompilerParams(vmem_limit_bytes=33 * MIB),
        cost_estimate=cost(20),
    )(*operands)


def halves_of(value):
    high = value.astype(jnp.bfloat16)
    return high, (value - high.astype(jnp.float32)).astype(jnp.bfloat16)


def product(x_of, ya_ref, yb_ref, row_sets):
    snaps, nodes = ya_ref.shape
    dot = functools.partial(lax.dot_general, dimension_numbers=(((1,), (1,)), ((), ())),
                            preferred_element_type=jnp.float32)
    chunk = nodes // 6
    totals = [None] * row_sets
    for i in range(6):
        at = slice(i * chunk, (i + 1) * chunk)
        y_high, y_low = halves_of(jnp.concatenate([ya_ref[:, at], yb_ref[:, at]], axis=0))
        both_y = jnp.concatenate([y_high, y_low], axis=0)
        for row_set in range(row_sets):
            high, low = halves_of(x_of(row_set, at))
            both = dot(high, both_y)
            value = both[:, :2 * snaps] + (both[:, 2 * snaps:] + dot(low, y_high))
            totals[row_set] = value if totals[row_set] is None else totals[row_set] + value
    return totals


def near_kernel(*refs):
    sources, refs = refs[:7], refs[7:]
    out_ref, back, held, sems = refs[0], refs[1:4], refs[4:11], refs[11]
    copies = [pltpu.make_async_copy(source, target, sems.at[i]) for i, (source, target) in enumerate(zip(sources, held))]
    for copy in copies:
        copy.start()
    y_refs, blocks = held[:2], (held[2:4], held[4:5], held[5:6], held[6:7])
    waits = (copies[:4], copies[4:5], copies[5:6], copies[6:7])
    for distance, (block, waited) in enumerate(zip(blocks, waits)):
        for copy in waited:
            copy.wait()
        (value,) = product(lambda _, at, block=block: jnp.concatenate([ref[:, at] for ref in block], axis=0),
                           *y_refs, 1)
        out_ref[distance] = value
        if distance > 0:
            back[distance - 1][...] = value.T


def far_kernel(place, ya_hbm, yb_hbm, far_hbm, near_ref, *refs):
    back, out_ref, held, sems = refs[:3], refs[3], refs[4:7], refs[7]
    copies = [pltpu.make_async_copy(source, target, sems.at[i])
              for i, (source, target) in enumerate(zip((ya_hbm, yb_hbm, far_hbm), held))]
    for copy in copies:
        copy.start()
    ya_ref, yb_ref, far_ref = held
    snaps = ya_ref.shape[0]
    rings = out_ref.shape[0] // 4
    low = snaps // 2
    z, h, way = place[0], place[1], place[2]

    def put(distance, value):
        at = lax.rem(z - way * distance + rings, rings)
        for side in range(2):
            row = 2 * at + (h if side == 0 else 1 - h)
            upper, lower = value[side * snaps:side * snaps + low], value[side * snaps + low:(side + 1) * snaps]
            out_ref[2 * row + h] = jnp.concatenate([upper[:, :snaps], lower[:, :snaps]], axis=1)
            out_ref[2 * row + (1 - h)] = jnp.concatenate([upper[:, snaps:], lower[:, snaps:]], axis=1)

    put(0, near_ref[0])
    for distance, received in enumerate(back, 1):
        put(distance, near_ref[distance])
        put(-distance, received[...])
    for copy in copies:
        copy.wait()
    (value,) = product(lambda _, at: far_ref[:, at], ya_ref, yb_ref, 1)
    put(rings // 2, value)


def near_call(*operands):
    snaps = operands[0].shape[0]
    square = jax.ShapeDtypeStruct((2 * snaps, 2 * snaps), jnp.float32)
    return pl.pallas_call(
        near_kernel,
        out_shape=[jax.ShapeDtypeStruct((4, 2 * snaps, 2 * snaps), jnp.float32)] + [square] * 3,
        in_specs=[ANYWHERE] * len(operands),
        out_specs=[IN_VMEM] * 4,
        scratch_shapes=[pltpu.VMEM(operand.shape, operand.dtype) for operand in operands]
        + [pltpu.SemaphoreType.DMA((len(operands),))],
        compiler_params=pltpu.CompilerParams(vmem_limit_bytes=60 * MIB),
        cost_estimate=cost(0.01),
    )(*operands)


def far_call(place, ya, yb, far, near, back, rings):
    snaps = ya.shape[0]
    return pl.pallas_call(
        far_kernel,
        out_shape=jax.ShapeDtypeStruct((4 * rings, snaps // 2, 2 * snaps), jnp.float32),
        in_specs=[IN_SMEM] + [ANYWHERE] * 3 + [IN_VMEM] * (1 + len(back)),
        out_specs=IN_VMEM,
        scratch_shapes=[pltpu.VMEM(operand.shape, operand.dtype) for operand in (ya, yb, far)]
        + [pltpu.SemaphoreType.DMA((3,))],
        compiler_params=pltpu.CompilerParams(vmem_limit_bytes=60 * MIB),
        cost_estimate=cost(2),
    )(place, ya, yb, far, near, *back)


def on_device(snapshots, connectivity, element_mass, lower_shared, upper_shared):
    snaps, nodes = snapshots.shape
    parts = lax.axis_size("mesh")
    blocks = lax.axis_size("snap")
    position = lax.axis_index("mesh")
    block = lax.axis_index("snap")
    rings = blocks // 2
    z, h = block // 2, block % 2
    half = nodes // 2
    tied = lax.optimization_barrier

    own = lax.dynamic_slice_in_dim(snapshots, h * half, half, 1)
    given = lax.dynamic_slice_in_dim(snapshots, (1 - h) * half, half, 1)
    a1 = ring_hop(own, 1)
    b1 = ring_hop(given, 1, cross=True)

    spread = (connectivity >> 3) * (8 * (1 + PARTS)) + (connectivity & 7)
    columns = tuple(spread[k] for k in range(3)) + (element_mass,)
    half_at = jnp.reshape(h, (1,)).astype(jnp.int32)
    (rows,) = apply_call(0, columns, snapshots, None, half_at)

    rows, a1, b1, given = tied((rows, a1, b1, given))
    pair1 = jnp.concatenate([a1, b1], axis=0)
    pair2 = ring_hop(pair1, 1)
    b0 = partner(given)
    rows, y_own, y_given = apply_call(1, columns, snapshots, rows, half_at)

    y_given, pair2, b0 = tied((y_given, pair2, b0))
    pair3 = ring_hop(pair2, 1)
    y_theirs = partner(y_given)

    shared = lower_shared.shape[0]
    low, high = pl.pallas_call(
        gather_kernel,
        out_shape=[jax.ShapeDtypeStruct((snaps, shared), jnp.float32)] * 2,
        in_specs=[IN_SMEM] * 2 + [IN_VMEM],
        out_specs=[IN_VMEM] * 2,
        scratch_shapes=[pltpu.VMEM((shared, LANES), jnp.float32)],
        compiler_params=pltpu.CompilerParams(vmem_limit_bytes=12 * MIB),
        cost_estimate=cost(0.01),
    )(lower_shared, upper_shared, rows)
    from_below = passed_along(high, "mesh", 1)
    from_above = passed_along(low, "mesh", -1)
    from_below, from_above, pair3, y_theirs = tied((from_below, from_above, pair3, y_theirs))
    pair4 = ring_hop(pair3, 1)
    near, *back = near_call(y_own, y_theirs, own, b0, pair1, pair2, pair3)
    rows, near = tied((rows, near))
    back = [ring_hop(value, -distance) for distance, value in enumerate(back, 1)]
    weighted = pl.pallas_call(
        assemble_kernel,
        out_shape=jax.ShapeDtypeStruct((snaps, nodes), jnp.float32),
        in_specs=[IN_SMEM] * 2 + [ANYWHERE] + [IN_VMEM] * 2,
        out_specs=IN_VMEM,
        scratch_shapes=[pltpu.VMEM((nodes, LANES), jnp.float32)] + [pltpu.VMEM((shared, LANES), jnp.float32)] * 2
        + [pltpu.SemaphoreType.DMA],
        compiler_params=pltpu.CompilerParams(vmem_limit_bytes=20 * MIB),
        cost_estimate=cost(0.01),
    )(lower_shared, upper_shared, rows, from_below, from_above)
    weighted, *back = tied((weighted, *back))
    place = jnp.stack([z, h, jnp.where(position % 2 == 0, 1, -1)]).astype(jnp.int32)
    tiles = far_call(place, y_own, y_theirs, pair4, near, back, rings)
    planes = [[m * blocks + 2 * r + c for m in range(parts) for c in range(2)] for r in range(rings)]
    tile = jnp.sum(lax.all_to_all(tiles, ("mesh", "snap"), 0, 0, axis_index_groups=planes, tiled=True), axis=0)
    column = jnp.concatenate([tile[:, :snaps], tile[:, snaps:]], axis=0)
    return weighted, column.T * (1.0 / float(parts * nodes))


def solution(mesh):
    placed = (P("snap", "mesh"), P(None, "mesh"), P("mesh"), P("mesh"), P("mesh"))
    return jax.shard_map(
        on_device,
        mesh=mesh,
        in_specs=placed,
        out_specs=(P("snap", "mesh"), P("snap", "mesh")),
        check_vma=False,
    )
```

```python
import functools

import jax
import jax.numpy as jnp
from jax import lax
from jax.experimental import pallas as pl
from jax.experimental.pallas import tpu as pltpu
from jax.sharding import PartitionSpec as P

LANES = 128
MIB = 2 ** 20


def ring_hop(value, steps, cross=False):
    parts, blocks = lax.axis_size("mesh"), lax.axis_size("snap")
    rings = blocks // 2
    pairs = []
    for part in range(parts):
        way = 1 if part % 2 == 0 else -1
        for block in range(blocks):
            z, h = block // 2, block % 2
            target = (z + way * steps) % rings
            pairs.append((part * blocks + block, part * blocks + 2 * target + (h ^ 1 if cross else h)))
    return lax.ppermute(value, ("mesh", "snap"), pairs)


def passed_along(value, axis, steps):
    count = lax.axis_size(axis)
    leading, last = (max(0, -steps), min(count, count - steps))
    return lax.ppermute(value, axis, [(source, source + steps) for source in range(leading, last)])


def partner(value):
    return lax.ppermute(value, "snap", [(i, i ^ 1) for i in range(lax.axis_size("snap"))])


def apply_kernel(first, last, start, count, arrays, parts, *refs):
    refs = list(refs)
    a_hbm, b_hbm, c_hbm, m_hbm, x_ref = refs[:5]
    del refs[:5]
    rows_in = None if first else refs.pop(0)
    half_s = refs.pop(0) if last else None
    rows_out = refs.pop(0)
    y_outs = (refs.pop(0), refs.pop(0)) if last else None
    a_s, b_s, c_s, m_s, sems, sums, in_sem, out_sems, *zs = refs
    snaps, nodes = x_ref.shape
    tiles = LANES // 8
    width = 1 + parts
    copies = []
    for j, (source, target) in enumerate(zip((a_hbm, b_hbm, c_hbm, m_hbm), (a_s, b_s, c_s, m_s))):
        copy = pltpu.make_async_copy(source.at[pl.ds(start, count)], target, sems.at[j])
        copy.start()
        copies.append(copy)
    if not first:
        earlier = pltpu.make_async_copy(rows_in, sums, in_sem)
        earlier.start()

    def tile_of(block, i, part):
        return pl.ds(pl.multiple_of(block * (LANES * width) + (i * width + part) * 8, 8), 8)

    def prepare(block, carry):
        x = x_ref[:, pl.ds(pl.multiple_of(block * LANES, LANES), LANES)]
        rows = jnp.concatenate([x, x], axis=0).T
        blank = jnp.zeros((8, LANES), jnp.float32)
        for z in zs:
            for i in range(tiles):
                z[tile_of(block, i, 0), :] = rows[i * 8:(i + 1) * 8]
                for part in range(parts):
                    z[tile_of(block, i, 1 + part), :] = blank
        return carry

    lax.fori_loop(0, nodes // LANES, prepare, 0, unroll=2)
    for copy in copies:
        copy.wait()

    def elements(group, carry):
        for j, z in enumerate(zs):
            corners, updated = [], []
            for k in range(2 * parts):
                e = group * (arrays * 2 * parts) + (j * 2 * parts + k)
                corners.append((a_s[e], b_s[e], c_s[e]))
                mass = m_s[e]
                values = [z[pl.ds(n, 1), :] for n in corners[k]]
                held = [z[pl.ds(n + 8 * (1 + k // 2), 1), :] for n in corners[k]]
                total = values[0] + values[1] + values[2]
                updated.append([h + mass * (v + total) for h, v in zip(held, values)])
            for k in range(2 * parts):
                at = snaps * (k % 2)
                for n, new in zip(corners[k], updated[k]):
                    z[pl.ds(n + 8 * (1 + k // 2), 1), at:at + snaps] = new[:, at:at + snaps]
        return carry

    lax.fori_loop(0, count // (arrays * 2 * parts), elements, 0, unroll=8)

    if not first:
        earlier.wait()

    def finish(block):
        totals = []
        for i in range(tiles):
            total = None
            for z in zs:
                for part in range(parts):
                    value = z[tile_of(block, i, 1 + part), :]
                    total = value if total is None else total + value
            totals.append(total)
        total = jnp.concatenate(totals, axis=0)
        at = pl.multiple_of(block * LANES, LANES)
        if not first:
            total = total + sums[pl.ds(at, LANES), :]
        if last:
            total = total * (1.0 / 12.0)
        sums[pl.ds(at, LANES), :] = total
        return total

    pieces = out_sems.shape[0]
    size = nodes // pieces
    writes = []
    for piece in range(pieces):
        blocks = size // LANES
        begin = piece * blocks
        side = None
        if last:
            side = piece // (pieces // 2)
            begin = lax.rem(half_s[0] + side, 2) * (pieces // 2 * blocks) + piece % (pieces // 2) * blocks

        def inner(i, carry, begin=begin, side=side, piece=piece):
            total = finish(begin + i)
            if last:
                columns = total.T
                at = pl.multiple_of((piece % (pieces // 2) * blocks + i) * LANES, LANES)
                y_outs[side][:, pl.ds(at, LANES)] = columns[0:snaps, :] + columns[snaps:2 * snaps, :]
            return carry

        lax.fori_loop(0, blocks, inner, 0, unroll=2)
        at = pl.multiple_of(begin * LANES, LANES) if last else begin * LANES
        write = pltpu.make_async_copy(sums.at[pl.ds(at, size)], rows_out.at[pl.ds(at, size)], out_sems.at[piece])
        write.start()
        writes.append(write)
    for write in writes:
        write.wait()


def gather_kernel(low_s, up_s, rows, low_out, up_out, taken):
    snaps, shared = low_out.shape
    for list_s, out in ((low_s, low_out), (up_s, up_out)):
        def gather(i, carry, list_s=list_s):
            at = pl.multiple_of(i * 16, 16)
            for k in range(16):
                taken[pl.ds(at + k, 1), :] = rows[pl.ds(list_s[at + k], 1), :]
            return carry

        lax.fori_loop(0, shared // 16, gather, 0)
        for block in range(shared // LANES):
            at = block * LANES
            columns = taken[at:at + LANES, :].T
            out[:, at:at + LANES] = columns[0:snaps, :] + columns[snaps:2 * snaps, :]


def assemble_kernel(low_s, up_s, rows_ref, below_ref, above_ref, out_ref, rows, below, above, sem):
    snaps, shared = below_ref.shape
    nodes = rows_ref.shape[0]
    copy = pltpu.make_async_copy(rows_ref, rows, sem)
    copy.start()
    for received, taken in ((below_ref, below), (above_ref, above)):
        for block in range(shared // LANES):
            at = block * LANES
            value = received[:, at:at + LANES]
            taken[at:at + LANES, :] = jnp.concatenate([value, jnp.zeros_like(value)], axis=0).T
    copy.wait()
    for list_s, taken in ((low_s, below), (up_s, above)):
        def add(i, carry, list_s=list_s, taken=taken):
            at = pl.multiple_of(i * 16, 16)
            nodes_of = [list_s[at + k] for k in range(16)]
            new = [rows[pl.ds(n, 1), :] + taken[pl.ds(at + k, 1), :] for k, n in enumerate(nodes_of)]
            for n, value in zip(nodes_of, new):
                rows[pl.ds(n, 1), :] = value
            return carry

        lax.fori_loop(0, shared // 16, add, 0)

    def write(i, carry):
        at = pl.multiple_of(i * LANES, LANES)
        columns = rows[pl.ds(at, LANES), :].T
        out_ref[:, pl.ds(at, LANES)] = columns[0:snaps, :] + columns[snaps:2 * snaps, :]
        return carry

    lax.fori_loop(0, nodes // LANES, write, 0, unroll=4)


ANYWHERE = pl.BlockSpec(memory_space=pl.ANY)
IN_VMEM = pl.BlockSpec(memory_space=pltpu.VMEM)
IN_SMEM = pl.BlockSpec(memory_space=pltpu.SMEM)


def cost(micros):
    return pl.CostEstimate(flops=int(micros * 1e9), bytes_accessed=int(micros * 3e6), transcendentals=0)


ARRAYS, PARTS = 4, 1


SHARES = (7, 5)


def apply_call(index, columns, snapshots, rows, half):
    calls = len(SHARES)
    first, last = index == 0, index == calls - 1
    snaps, nodes = snapshots.shape
    share = columns[0].shape[0] // sum(SHARES)
    start, count = share * sum(SHARES[:index]), share * SHARES[index]
    row_shape = jax.ShapeDtypeStruct((nodes, LANES), jnp.float32)
    side = jax.ShapeDtypeStruct((snaps, nodes // 2), jnp.float32)
    operands = columns + (snapshots,) + (() if first else (rows,)) + ((half,) if last else ())
    return pl.pallas_call(
        functools.partial(apply_kernel, first, last, start, count, ARRAYS, PARTS),
        out_shape=[row_shape] + ([side, side] if last else []),
        in_specs=[ANYWHERE] * 4 + [IN_VMEM] + ([] if first else [ANYWHERE]) + ([IN_SMEM] if last else []),
        out_specs=[ANYWHERE] + ([IN_VMEM] * 2 if last else []),
        scratch_shapes=[pltpu.SMEM((count,), jnp.int32)] * 3
        + [pltpu.SMEM((count,), jnp.float32), pltpu.SemaphoreType.DMA((4,))]
        + [pltpu.VMEM((nodes, LANES), jnp.float32), pltpu.SemaphoreType.DMA, pltpu.SemaphoreType.DMA((4,))]
        + [pltpu.VMEM((nodes * (1 + PARTS), LANES), jnp.float32)] * ARRAYS,
        compiler_params=pltpu.CompilerParams(vmem_limit_bytes=33 * MIB),
        cost_estimate=cost(20),
    )(*operands)


def halves_of(value):
    high = value.astype(jnp.bfloat16)
    return high, (value - high.astype(jnp.float32)).astype(jnp.bfloat16)


def product(x_of, ya_ref, yb_ref, row_sets):
    snaps, nodes = ya_ref.shape
    dot = functools.partial(lax.dot_general, dimension_numbers=(((1,), (1,)), ((), ())),
                            preferred_element_type=jnp.float32)
    chunk = nodes // 6
    totals = [None] * row_sets
    for i in range(6):
        at = slice(i * chunk, (i + 1) * chunk)
        y_high, y_low = halves_of(jnp.concatenate([ya_ref[:, at], yb_ref[:, at]], axis=0))
        both_y = jnp.concatenate([y_high, y_low], axis=0)
        for row_set in range(row_sets):
            high, low = halves_of(x_of(row_set, at))
            both = dot(high, both_y)
            value = both[:, :2 * snaps] + (both[:, 2 * snaps:] + dot(low, y_high))
            totals[row_set] = value if totals[row_set] is None else totals[row_set] + value
    return totals


def near_kernel(*refs):
    sources, refs = refs[:7], refs[7:]
    out_ref, back, held, sems = refs[0], refs[1:4], refs[4:11], refs[11]
    copies = [pltpu.make_async_copy(source, target, sems.at[i]) for i, (source, target) in enumerate(zip(sources, held))]
    for copy in copies:
        copy.start()
    y_refs, blocks = held[:2], (held[2:4], held[4:5], held[5:6], held[6:7])
    waits = (copies[:4], copies[4:5], copies[5:6], copies[6:7])
    for distance, (block, waited) in enumerate(zip(blocks, waits)):
        for copy in waited:
            copy.wait()
        (value,) = product(lambda _, at, block=block: jnp.concatenate([ref[:, at] for ref in block], axis=0),
                           *y_refs, 1)
        out_ref[distance] = value
        if distance > 0:
            back[distance - 1][...] = value.T


def far_kernel(place, ya_ref, yb_ref, far_ref, near_ref, *refs):
    *back, out_ref = refs
    snaps = ya_ref.shape[0]
    rings = out_ref.shape[0] // 4
    low = snaps // 2
    z, h, way = place[0], place[1], place[2]

    def put(distance, value):
        at = lax.rem(z - way * distance + rings, rings)
        for side in range(2):
            row = 2 * at + (h if side == 0 else 1 - h)
            upper, lower = value[side * snaps:side * snaps + low], value[side * snaps + low:(side + 1) * snaps]
            out_ref[2 * row + h] = jnp.concatenate([upper[:, :snaps], lower[:, :snaps]], axis=1)
            out_ref[2 * row + (1 - h)] = jnp.concatenate([upper[:, snaps:], lower[:, snaps:]], axis=1)

    put(0, near_ref[0])
    for distance, received in enumerate(back, 1):
        put(distance, near_ref[distance])
        put(-distance, received[...])
    (value,) = product(lambda _, at: far_ref[:, at], ya_ref, yb_ref, 1)
    put(rings // 2, value)


def near_call(*operands):
    snaps = operands[0].shape[0]
    square = jax.ShapeDtypeStruct((2 * snaps, 2 * snaps), jnp.float32)
    return pl.pallas_call(
        near_kernel,
        out_shape=[jax.ShapeDtypeStruct((4, 2 * snaps, 2 * snaps), jnp.float32)] + [square] * 3,
        in_specs=[ANYWHERE] * len(operands),
        out_specs=[IN_VMEM] * 4,
        scratch_shapes=[pltpu.VMEM(operand.shape, operand.dtype) for operand in operands]
        + [pltpu.SemaphoreType.DMA((len(operands),))],
        compiler_params=pltpu.CompilerParams(vmem_limit_bytes=60 * MIB),
        cost_estimate=cost(0.01),
    )(*operands)


def far_call(place, ya, yb, far, near, back, rings):
    snaps = ya.shape[0]
    return pl.pallas_call(
        far_kernel,
        out_shape=jax.ShapeDtypeStruct((4 * rings, snaps // 2, 2 * snaps), jnp.float32),
        in_specs=[IN_SMEM] + [IN_VMEM] * (4 + len(back)),
        out_specs=IN_VMEM,
        compiler_params=pltpu.CompilerParams(vmem_limit_bytes=16 * MIB),
        cost_estimate=cost(2),
    )(place, ya, yb, far, near, *back)


def on_device(snapshots, connectivity, element_mass, lower_shared, upper_shared):
    snaps, nodes = snapshots.shape
    parts = lax.axis_size("mesh")
    blocks = lax.axis_size("snap")
    position = lax.axis_index("mesh")
    block = lax.axis_index("snap")
    rings = blocks // 2
    z, h = block // 2, block % 2
    half = nodes // 2
    tied = lax.optimization_barrier

    own = lax.dynamic_slice_in_dim(snapshots, h * half, half, 1)
    given = lax.dynamic_slice_in_dim(snapshots, (1 - h) * half, half, 1)
    a1 = ring_hop(own, 1)
    b1 = ring_hop(given, 1, cross=True)

    spread = (connectivity >> 3) * (8 * (1 + PARTS)) + (connectivity & 7)
    columns = tuple(spread[k] for k in range(3)) + (element_mass,)
    half_at = jnp.reshape(h, (1,)).astype(jnp.int32)
    (rows,) = apply_call(0, columns, snapshots, None, half_at)

    rows, a1, b1, given = tied((rows, a1, b1, given))
    pair1 = jnp.concatenate([a1, b1], axis=0)
    pair2 = ring_hop(pair1, 1)
    b0 = partner(given)
    rows, y_own, y_given = apply_call(1, columns, snapshots, rows, half_at)

    y_given, pair2, b0 = tied((y_given, pair2, b0))
    pair3 = ring_hop(pair2, 1)
    y_theirs = partner(y_given)

    shared = lower_shared.shape[0]
    low, high = pl.pallas_call(
        gather_kernel,
        out_shape=[jax.ShapeDtypeStruct((snaps, shared), jnp.float32)] * 2,
        in_specs=[IN_SMEM] * 2 + [IN_VMEM],
        out_specs=[IN_VMEM] * 2,
        scratch_shapes=[pltpu.VMEM((shared, LANES), jnp.float32)],
        compiler_params=pltpu.CompilerParams(vmem_limit_bytes=12 * MIB),
        cost_estimate=cost(0.01),
    )(lower_shared, upper_shared, rows)
    from_below = passed_along(high, "mesh", 1)
    from_above = passed_along(low, "mesh", -1)
    from_below, from_above, pair3, y_theirs = tied((from_below, from_above, pair3, y_theirs))
    pair4 = ring_hop(pair3, 1)
    near, *back = near_call(y_own, y_theirs, own, b0, pair1, pair2, pair3)
    rows, near = tied((rows, near))
    back = [ring_hop(value, -distance) for distance, value in enumerate(back, 1)]
    weighted = pl.pallas_call(
        assemble_kernel,
        out_shape=jax.ShapeDtypeStruct((snaps, nodes), jnp.float32),
        in_specs=[IN_SMEM] * 2 + [ANYWHERE] + [IN_VMEM] * 2,
        out_specs=IN_VMEM,
        scratch_shapes=[pltpu.VMEM((nodes, LANES), jnp.float32)] + [pltpu.VMEM((shared, LANES), jnp.float32)] * 2
        + [pltpu.SemaphoreType.DMA],
        compiler_params=pltpu.CompilerParams(vmem_limit_bytes=20 * MIB),
        cost_estimate=cost(0.01),
    )(lower_shared, upper_shared, rows, from_below, from_above)
    weighted, *back = tied((weighted, *back))
    place = jnp.stack([z, h, jnp.where(position % 2 == 0, 1, -1)]).astype(jnp.int32)
    tiles = far_call(place, y_own, y_theirs, pair4, near, back, rings)
    planes = [[m * blocks + 2 * r + c for m in range(parts) for c in range(2)] for r in range(rings)]
    tile = jnp.sum(lax.all_to_all(tiles, ("mesh", "snap"), 0, 0, axis_index_groups=planes, tiled=True), axis=0)
    column = jnp.concatenate([tile[:, :snaps], tile[:, snaps:]], axis=0)
    return weighted, column.T * (1.0 / float(parts * nodes))


def solution(mesh):
    placed = (P("snap", "mesh"), P(None, "mesh"), P("mesh"), P("mesh"), P("mesh"))
    return jax.shard_map(
        on_device,
        mesh=mesh,
        in_specs=placed,
        out_specs=(P("snap", "mesh"), P("snap", "mesh")),
        check_vma=False,
    )
```

```python
import functools

import jax
import jax.numpy as jnp
from jax import lax
from jax.experimental import pallas as pl
from jax.experimental.pallas import tpu as pltpu
from jax.sharding import PartitionSpec as P

LANES = 128
MIB = 2 ** 20


def ring_hop(value, steps, cross=False):
    parts, blocks = lax.axis_size("mesh"), lax.axis_size("snap")
    rings = blocks // 2
    pairs = []
    for part in range(parts):
        way = 1 if part % 2 == 0 else -1
        for block in range(blocks):
            z, h = block // 2, block % 2
            target = (z + way * steps) % rings
            pairs.append((part * blocks + block, part * blocks + 2 * target + (h ^ 1 if cross else h)))
    return lax.ppermute(value, ("mesh", "snap"), pairs)


def passed_along(value, axis, steps):
    count = lax.axis_size(axis)
    leading, last = (max(0, -steps), min(count, count - steps))
    return lax.ppermute(value, axis, [(source, source + steps) for source in range(leading, last)])


def partner(value):
    return lax.ppermute(value, "snap", [(i, i ^ 1) for i in range(lax.axis_size("snap"))])


def apply_kernel(first, last, start, count, arrays, parts, *refs):
    refs = list(refs)
    a_hbm, b_hbm, c_hbm, m_hbm, x_ref = refs[:5]
    del refs[:5]
    rows_in = None if first else refs.pop(0)
    half_s = refs.pop(0) if last else None
    rows_out = refs.pop(0)
    y_outs = (refs.pop(0), refs.pop(0)) if last else None
    a_s, b_s, c_s, m_s, sems, sums, in_sem, out_sems, *zs = refs
    snaps, nodes = x_ref.shape
    tiles = LANES // 8
    width = 1 + parts
    copies = []
    for j, (source, target) in enumerate(zip((a_hbm, b_hbm, c_hbm, m_hbm), (a_s, b_s, c_s, m_s))):
        copy = pltpu.make_async_copy(source.at[pl.ds(start, count)], target, sems.at[j])
        copy.start()
        copies.append(copy)
    if not first:
        earlier = pltpu.make_async_copy(rows_in, sums, in_sem)
        earlier.start()

    def tile_of(block, i, part):
        return pl.ds(pl.multiple_of(block * (LANES * width) + (i * width + part) * 8, 8), 8)

    def prepare(block, carry):
        x = x_ref[:, pl.ds(pl.multiple_of(block * LANES, LANES), LANES)]
        rows = jnp.concatenate([x, x], axis=0).T
        blank = jnp.zeros((8, LANES), jnp.float32)
        for z in zs:
            for i in range(tiles):
                z[tile_of(block, i, 0), :] = rows[i * 8:(i + 1) * 8]
                for part in range(parts):
                    z[tile_of(block, i, 1 + part), :] = blank
        return carry

    lax.fori_loop(0, nodes // LANES, prepare, 0, unroll=2)
    for copy in copies:
        copy.wait()

    def elements(group, carry):
        for j, z in enumerate(zs):
            corners, updated = [], []
            for k in range(2 * parts):
                e = group * (arrays * 2 * parts) + (j * 2 * parts + k)
                corners.append((a_s[e], b_s[e], c_s[e]))
                mass = m_s[e]
                values = [z[pl.ds(n, 1), :] for n in corners[k]]
                held = [z[pl.ds(n + 8 * (1 + k // 2), 1), :] for n in corners[k]]
                total = values[0] + values[1] + values[2]
                updated.append([h + mass * (v + total) for h, v in zip(held, values)])
            for k in range(2 * parts):
                at = snaps * (k % 2)
                for n, new in zip(corners[k], updated[k]):
                    z[pl.ds(n + 8 * (1 + k // 2), 1), at:at + snaps] = new[:, at:at + snaps]
        return carry

    lax.fori_loop(0, count // (arrays * 2 * parts), elements, 0, unroll=16)

    if not first:
        earlier.wait()

    def finish(block):
        totals = []
        for i in range(tiles):
            total = None
            for z in zs:
                for part in range(parts):
                    value = z[tile_of(block, i, 1 + part), :]
                    total = value if total is None else total + value
            totals.append(total)
        total = jnp.concatenate(totals, axis=0)
        at = pl.multiple_of(block * LANES, LANES)
        if not first:
            total = total + sums[pl.ds(at, LANES), :]
        if last:
            total = total * (1.0 / 12.0)
        sums[pl.ds(at, LANES), :] = total
        return total

    pieces = out_sems.shape[0]
    size = nodes // pieces
    writes = []
    for piece in range(pieces):
        blocks = size // LANES
        begin = piece * blocks
        side = None
        if last:
            side = piece // (pieces // 2)
            begin = lax.rem(half_s[0] + side, 2) * (pieces // 2 * blocks) + piece % (pieces // 2) * blocks

        def inner(i, carry, begin=begin, side=side, piece=piece):
            total = finish(begin + i)
            if last:
                columns = total.T
                at = pl.multiple_of((piece % (pieces // 2) * blocks + i) * LANES, LANES)
                y_outs[side][:, pl.ds(at, LANES)] = columns[0:snaps, :] + columns[snaps:2 * snaps, :]
            return carry

        lax.fori_loop(0, blocks, inner, 0, unroll=2)
        at = pl.multiple_of(begin * LANES, LANES) if last else begin * LANES
        write = pltpu.make_async_copy(sums.at[pl.ds(at, size)], rows_out.at[pl.ds(at, size)], out_sems.at[piece])
        write.start()
        writes.append(write)
    for write in writes:
        write.wait()


def gather_kernel(low_s, up_s, rows, low_out, up_out, taken):
    snaps, shared = low_out.shape
    for list_s, out in ((low_s, low_out), (up_s, up_out)):
        def gather(i, carry, list_s=list_s):
            at = pl.multiple_of(i * 16, 16)
            for k in range(16):
                taken[pl.ds(at + k, 1), :] = rows[pl.ds(list_s[at + k], 1), :]
            return carry

        lax.fori_loop(0, shared // 16, gather, 0)
        for block in range(shared // LANES):
            at = block * LANES
            columns = taken[at:at + LANES, :].T
            out[:, at:at + LANES] = columns[0:snaps, :] + columns[snaps:2 * snaps, :]


def assemble_kernel(low_s, up_s, rows_ref, below_ref, above_ref, out_ref, rows, below, above, sem):
    snaps, shared = below_ref.shape
    nodes = rows_ref.shape[0]
    copy = pltpu.make_async_copy(rows_ref, rows, sem)
    copy.start()
    for received, taken in ((below_ref, below), (above_ref, above)):
        for block in range(shared // LANES):
            at = block * LANES
            value = received[:, at:at + LANES]
            taken[at:at + LANES, :] = jnp.concatenate([value, jnp.zeros_like(value)], axis=0).T
    copy.wait()
    for list_s, taken in ((low_s, below), (up_s, above)):
        def add(i, carry, list_s=list_s, taken=taken):
            at = pl.multiple_of(i * 16, 16)
            nodes_of = [list_s[at + k] for k in range(16)]
            new = [rows[pl.ds(n, 1), :] + taken[pl.ds(at + k, 1), :] for k, n in enumerate(nodes_of)]
            for n, value in zip(nodes_of, new):
                rows[pl.ds(n, 1), :] = value
            return carry

        lax.fori_loop(0, shared // 16, add, 0)

    def write(i, carry):
        at = pl.multiple_of(i * LANES, LANES)
        columns = rows[pl.ds(at, LANES), :].T
        out_ref[:, pl.ds(at, LANES)] = columns[0:snaps, :] + columns[snaps:2 * snaps, :]
        return carry

    lax.fori_loop(0, nodes // LANES, write, 0, unroll=4)


ANYWHERE = pl.BlockSpec(memory_space=pl.ANY)
IN_VMEM = pl.BlockSpec(memory_space=pltpu.VMEM)
IN_SMEM = pl.BlockSpec(memory_space=pltpu.SMEM)


def cost(micros):
    return pl.CostEstimate(flops=int(micros * 1e9), bytes_accessed=int(micros * 3e6), transcendentals=0)


ARRAYS, PARTS = 4, 1


SHARES = (7, 5)


def apply_call(index, columns, snapshots, rows, half):
    calls = len(SHARES)
    first, last = index == 0, index == calls - 1
    snaps, nodes = snapshots.shape
    share = columns[0].shape[0] // sum(SHARES)
    start, count = share * sum(SHARES[:index]), share * SHARES[index]
    row_shape = jax.ShapeDtypeStruct((nodes, LANES), jnp.float32)
    side = jax.ShapeDtypeStruct((snaps, nodes // 2), jnp.float32)
    operands = columns + (snapshots,) + (() if first else (rows,)) + ((half,) if last else ())
    return pl.pallas_call(
        functools.partial(apply_kernel, first, last, start, count, ARRAYS, PARTS),
        out_shape=[row_shape] + ([side, side] if last else []),
        in_specs=[ANYWHERE] * 4 + [IN_VMEM] + ([] if first else [ANYWHERE]) + ([IN_SMEM] if last else []),
        out_specs=[ANYWHERE] + ([IN_VMEM] * 2 if last else []),
        scratch_shapes=[pltpu.SMEM((count,), jnp.int32)] * 3
        + [pltpu.SMEM((count,), jnp.float32), pltpu.SemaphoreType.DMA((4,))]
        + [pltpu.VMEM((nodes, LANES), jnp.float32), pltpu.SemaphoreType.DMA, pltpu.SemaphoreType.DMA((4,))]
        + [pltpu.VMEM((nodes * (1 + PARTS), LANES), jnp.float32)] * ARRAYS,
        compiler_params=pltpu.CompilerParams(vmem_limit_bytes=33 * MIB),
        cost_estimate=cost(20),
    )(*operands)


def halves_of(value):
    high = value.astype(jnp.bfloat16)
    return high, (value - high.astype(jnp.float32)).astype(jnp.bfloat16)


def product(x_of, ya_ref, yb_ref, row_sets):
    snaps, nodes = ya_ref.shape
    dot = functools.partial(lax.dot_general, dimension_numbers=(((1,), (1,)), ((), ())),
                            preferred_element_type=jnp.float32)
    chunk = nodes // 6
    totals = [None] * row_sets
    for i in range(6):
        at = slice(i * chunk, (i + 1) * chunk)
        y_high, y_low = halves_of(jnp.concatenate([ya_ref[:, at], yb_ref[:, at]], axis=0))
        both_y = jnp.concatenate([y_high, y_low], axis=0)
        for row_set in range(row_sets):
            high, low = halves_of(x_of(row_set, at))
            both = dot(high, both_y)
            value = both[:, :2 * snaps] + (both[:, 2 * snaps:] + dot(low, y_high))
            totals[row_set] = value if totals[row_set] is None else totals[row_set] + value
    return totals


def near_kernel(*refs):
    sources, refs = refs[:7], refs[7:]
    out_ref, back, held, sems = refs[0], refs[1:4], refs[4:11], refs[11]
    copies = [pltpu.make_async_copy(source, target, sems.at[i]) for i, (source, target) in enumerate(zip(sources, held))]
    for copy in copies:
        copy.start()
    y_refs, blocks = held[:2], (held[2:4], held[4:5], held[5:6], held[6:7])
    waits = (copies[:4], copies[4:5], copies[5:6], copies[6:7])
    for distance, (block, waited) in enumerate(zip(blocks, waits)):
        for copy in waited:
            copy.wait()
        (value,) = product(lambda _, at, block=block: jnp.concatenate([ref[:, at] for ref in block], axis=0),
                           *y_refs, 1)
        out_ref[distance] = value
        if distance > 0:
            back[distance - 1][...] = value.T


def put(out_ref, place, distance, value):
    z, h, way = place[0], place[1], place[2]
    rings, low, snaps = out_ref.shape[0] // 4, out_ref.shape[1], out_ref.shape[2] // 2
    at = lax.rem(z - way * distance + rings, rings)
    for side in range(2):
        row = 2 * at + (h if side == 0 else 1 - h)
        upper, lower = value[side * snaps:side * snaps + low], value[side * snaps + low:(side + 1) * snaps]
        out_ref[2 * row + h] = jnp.concatenate([upper[:, :snaps], lower[:, :snaps]], axis=1)
        out_ref[2 * row + (1 - h)] = jnp.concatenate([upper[:, snaps:], lower[:, snaps:]], axis=1)


def lay_kernel(place, near_ref, *refs):
    *back, out_ref = refs
    put(out_ref, place, 0, near_ref[0])
    for distance, received in enumerate(back, 1):
        put(out_ref, place, distance, near_ref[distance])
        put(out_ref, place, -distance, received[...])
    put(out_ref, place, out_ref.shape[0] // 8, jnp.zeros_like(near_ref[0]))


def far_kernel(place, ya_ref, yb_ref, far_ref, laid_ref, out_ref):
    (value,) = product(lambda _, at: far_ref[:, at], ya_ref, yb_ref, 1)
    put(out_ref, place, out_ref.shape[0] // 8, value)


def near_call(*operands):
    snaps = operands[0].shape[0]
    square = jax.ShapeDtypeStruct((2 * snaps, 2 * snaps), jnp.float32)
    return pl.pallas_call(
        near_kernel,
        out_shape=[jax.ShapeDtypeStruct((4, 2 * snaps, 2 * snaps), jnp.float32)] + [square] * 3,
        in_specs=[ANYWHERE] * len(operands),
        out_specs=[IN_VMEM] * 4,
        scratch_shapes=[pltpu.VMEM(operand.shape, operand.dtype) for operand in operands]
        + [pltpu.SemaphoreType.DMA((len(operands),))],
        compiler_params=pltpu.CompilerParams(vmem_limit_bytes=60 * MIB),
        cost_estimate=cost(0.01),
    )(*operands)


def lay_call(place, near, back, rings):
    snaps = near.shape[1] // 2
    return pl.pallas_call(
        lay_kernel,
        out_shape=jax.ShapeDtypeStruct((4 * rings, snaps // 2, 2 * snaps), jnp.float32),
        in_specs=[IN_SMEM] + [IN_VMEM] * (1 + len(back)),
        out_specs=IN_VMEM,
        compiler_params=pltpu.CompilerParams(vmem_limit_bytes=16 * MIB),
        cost_estimate=cost(0.01),
    )(place, near, *back)


def far_call(place, ya, yb, far, laid):
    return pl.pallas_call(
        far_kernel,
        out_shape=jax.ShapeDtypeStruct(laid.shape, laid.dtype),
        in_specs=[IN_SMEM] + [IN_VMEM] * 4,
        out_specs=IN_VMEM,
        input_output_aliases={4: 0},
        compiler_params=pltpu.CompilerParams(vmem_limit_bytes=16 * MIB),
        cost_estimate=cost(2),
    )(place, ya, yb, far, laid)


def on_device(snapshots, connectivity, element_mass, lower_shared, upper_shared):
    snaps, nodes = snapshots.shape
    parts = lax.axis_size("mesh")
    blocks = lax.axis_size("snap")
    position = lax.axis_index("mesh")
    block = lax.axis_index("snap")
    rings = blocks // 2
    z, h = block // 2, block % 2
    half = nodes // 2
    tied = lax.optimization_barrier

    own = lax.dynamic_slice_in_dim(snapshots, h * half, half, 1)
    given = lax.dynamic_slice_in_dim(snapshots, (1 - h) * half, half, 1)
    a1 = ring_hop(own, 1)
    b1 = ring_hop(given, 1, cross=True)

    spread = (connectivity >> 3) * (8 * (1 + PARTS)) + (connectivity & 7)
    columns = tuple(spread[k] for k in range(3)) + (element_mass,)
    half_at = jnp.reshape(h, (1,)).astype(jnp.int32)
    (rows,) = apply_call(0, columns, snapshots, None, half_at)

    rows, a1, b1, given = tied((rows, a1, b1, given))
    pair1 = jnp.concatenate([a1, b1], axis=0)
    pair2 = ring_hop(pair1, 1)
    b0 = partner(given)
    rows, y_own, y_given = apply_call(1, columns, snapshots, rows, half_at)

    y_given, pair2, b0 = tied((y_given, pair2, b0))
    pair3 = ring_hop(pair2, 1)
    y_theirs = partner(y_given)

    shared = lower_shared.shape[0]
    low, high = pl.pallas_call(
        gather_kernel,
        out_shape=[jax.ShapeDtypeStruct((snaps, shared), jnp.float32)] * 2,
        in_specs=[IN_SMEM] * 2 + [IN_VMEM],
        out_specs=[IN_VMEM] * 2,
        scratch_shapes=[pltpu.VMEM((shared, LANES), jnp.float32)],
        compiler_params=pltpu.CompilerParams(vmem_limit_bytes=12 * MIB),
        cost_estimate=cost(0.01),
    )(lower_shared, upper_shared, rows)
    from_below = passed_along(high, "mesh", 1)
    from_above = passed_along(low, "mesh", -1)
    from_below, from_above, pair3, y_theirs = tied((from_below, from_above, pair3, y_theirs))
    pair4 = ring_hop(pair3, 1)
    near, *back = near_call(y_own, y_theirs, own, b0, pair1, pair2, pair3)
    rows, near = tied((rows, near))
    back = [ring_hop(value, -distance) for distance, value in enumerate(back, 1)]
    weighted = pl.pallas_call(
        assemble_kernel,
        out_shape=jax.ShapeDtypeStruct((snaps, nodes), jnp.float32),
        in_specs=[IN_SMEM] * 2 + [ANYWHERE] + [IN_VMEM] * 2,
        out_specs=IN_VMEM,
        scratch_shapes=[pltpu.VMEM((nodes, LANES), jnp.float32)] + [pltpu.VMEM((shared, LANES), jnp.float32)] * 2
        + [pltpu.SemaphoreType.DMA],
        compiler_params=pltpu.CompilerParams(vmem_limit_bytes=20 * MIB),
        cost_estimate=cost(0.01),
    )(lower_shared, upper_shared, rows, from_below, from_above)
    weighted, *back = tied((weighted, *back))
    place = jnp.stack([z, h, jnp.where(position % 2 == 0, 1, -1)]).astype(jnp.int32)
    laid = lay_call(place, near, back, rings)
    laid, pair4 = tied((laid, pair4))
    tiles = far_call(place, y_own, y_theirs, pair4, laid)
    planes = [[m * blocks + 2 * r + c for m in range(parts) for c in range(2)] for r in range(rings)]
    tile = jnp.sum(lax.all_to_all(tiles, ("mesh", "snap"), 0, 0, axis_index_groups=planes, tiled=True), axis=0)
    column = jnp.concatenate([tile[:, :snaps], tile[:, snaps:]], axis=0)
    return weighted, column.T * (1.0 / float(parts * nodes))


def solution(mesh):
    placed = (P("snap", "mesh"), P(None, "mesh"), P("mesh"), P("mesh"), P("mesh"))
    return jax.shard_map(
        on_device,
        mesh=mesh,
        in_specs=placed,
        out_specs=(P("snap", "mesh"), P("snap", "mesh")),
        check_vma=False,
    )
```

```python
import functools

import jax
import jax.numpy as jnp
from jax import lax
from jax.experimental import pallas as pl
from jax.experimental.pallas import tpu as pltpu
from jax.sharding import PartitionSpec as P

LANES = 128
MIB = 2 ** 20


def ring_hop(value, steps, cross=False):
    parts, blocks = lax.axis_size("mesh"), lax.axis_size("snap")
    rings = blocks // 2
    pairs = []
    for part in range(parts):
        way = 1 if part % 2 == 0 else -1
        for block in range(blocks):
            z, h = block // 2, block % 2
            target = (z + way * steps) % rings
            pairs.append((part * blocks + block, part * blocks + 2 * target + (h ^ 1 if cross else h)))
    return lax.ppermute(value, ("mesh", "snap"), pairs)


def passed_along(value, axis, steps):
    count = lax.axis_size(axis)
    leading, last = (max(0, -steps), min(count, count - steps))
    return lax.ppermute(value, axis, [(source, source + steps) for source in range(leading, last)])


def partner(value):
    return lax.ppermute(value, "snap", [(i, i ^ 1) for i in range(lax.axis_size("snap"))])


def apply_kernel(first, last, start, count, arrays, parts, *refs):
    refs = list(refs)
    a_hbm, b_hbm, c_hbm, m_hbm, x_ref = refs[:5]
    del refs[:5]
    rows_in = None if first else refs.pop(0)
    half_s = refs.pop(0) if last else None
    rows_out = refs.pop(0)
    y_outs = (refs.pop(0), refs.pop(0)) if last else None
    a_s, b_s, c_s, m_s, sems, sums, in_sem, out_sems, *zs = refs
    snaps, nodes = x_ref.shape
    tiles = LANES // 8
    width = 1 + parts
    copies = []
    for j, (source, target) in enumerate(zip((a_hbm, b_hbm, c_hbm, m_hbm), (a_s, b_s, c_s, m_s))):
        copy = pltpu.make_async_copy(source.at[pl.ds(start, count)], target, sems.at[j])
        copy.start()
        copies.append(copy)
    if not first:
        earlier = pltpu.make_async_copy(rows_in, sums, in_sem)
        earlier.start()

    def tile_of(block, i, part):
        return pl.ds(pl.multiple_of(block * (LANES * width) + (i * width + part) * 8, 8), 8)

    def prepare(block, carry):
        x = x_ref[:, pl.ds(pl.multiple_of(block * LANES, LANES), LANES)]
        rows = jnp.concatenate([x, x], axis=0).T
        blank = jnp.zeros((8, LANES), jnp.float32)
        for z in zs:
            for i in range(tiles):
                z[tile_of(block, i, 0), :] = rows[i * 8:(i + 1) * 8]
                for part in range(parts):
                    z[tile_of(block, i, 1 + part), :] = blank
        return carry

    lax.fori_loop(0, nodes // LANES, prepare, 0, unroll=2)
    for copy in copies:
        copy.wait()

    def elements(group, carry):
        for j, z in enumerate(zs):
            corners, updated = [], []
            for k in range(2 * parts):
                e = group * (arrays * 2 * parts) + (j * 2 * parts + k)
                corners.append((a_s[e], b_s[e], c_s[e]))
                mass = m_s[e]
                values = [z[pl.ds(n, 1), :] for n in corners[k]]
                held = [z[pl.ds(n + 8 * (1 + k // 2), 1), :] for n in corners[k]]
                total = values[0] + values[1] + values[2]
                updated.append([h + mass * (v + total) for h, v in zip(held, values)])
            for k in range(2 * parts):
                at = snaps * (k % 2)
                for n, new in zip(corners[k], updated[k]):
                    z[pl.ds(n + 8 * (1 + k // 2), 1), at:at + snaps] = new[:, at:at + snaps]
        return carry

    lax.fori_loop(0, count // (arrays * 2 * parts), elements, 0, unroll=16)

    if not first:
        earlier.wait()

    def finish(block):
        totals = []
        for i in range(tiles):
            total = None
            for z in zs:
                for part in range(parts):
                    value = z[tile_of(block, i, 1 + part), :]
                    total = value if total is None else total + value
            totals.append(total)
        total = jnp.concatenate(totals, axis=0)
        at = pl.multiple_of(block * LANES, LANES)
        if not first:
            total = total + sums[pl.ds(at, LANES), :]
        if last:
            total = total * (1.0 / 12.0)
        sums[pl.ds(at, LANES), :] = total
        return total

    pieces = out_sems.shape[0]
    size = nodes // pieces
    writes = []
    for piece in range(pieces):
        blocks = size // LANES
        begin = piece * blocks
        side = None
        if last:
            side = piece // (pieces // 2)
            begin = lax.rem(half_s[0] + side, 2) * (pieces // 2 * blocks) + piece % (pieces // 2) * blocks

        def inner(i, carry, begin=begin, side=side, piece=piece):
            total = finish(begin + i)
            if last:
                columns = total.T
                at = pl.multiple_of((piece % (pieces // 2) * blocks + i) * LANES, LANES)
                y_outs[side][:, pl.ds(at, LANES)] = columns[0:snaps, :] + columns[snaps:2 * snaps, :]
            return carry

        lax.fori_loop(0, blocks, inner, 0, unroll=2)
        at = pl.multiple_of(begin * LANES, LANES) if last else begin * LANES
        write = pltpu.make_async_copy(sums.at[pl.ds(at, size)], rows_out.at[pl.ds(at, size)], out_sems.at[piece])
        write.start()
        writes.append(write)
    for write in writes:
        write.wait()


def gather_kernel(low_s, up_s, rows, low_out, up_out, taken):
    snaps, shared = low_out.shape
    for list_s, out in ((low_s, low_out), (up_s, up_out)):
        def gather(i, carry, list_s=list_s):
            at = pl.multiple_of(i * 16, 16)
            for k in range(16):
                taken[pl.ds(at + k, 1), :] = rows[pl.ds(list_s[at + k], 1), :]
            return carry

        lax.fori_loop(0, shared // 16, gather, 0)
        for block in range(shared // LANES):
            at = block * LANES
            columns = taken[at:at + LANES, :].T
            out[:, at:at + LANES] = columns[0:snaps, :] + columns[snaps:2 * snaps, :]


def assemble_kernel(low_s, up_s, rows_ref, below_ref, above_ref, out_ref, rows, below, above, sem):
    snaps, shared = below_ref.shape
    nodes = rows_ref.shape[0]
    copy = pltpu.make_async_copy(rows_ref, rows, sem)
    copy.start()
    for received, taken in ((below_ref, below), (above_ref, above)):
        for block in range(shared // LANES):
            at = block * LANES
            value = received[:, at:at + LANES]
            taken[at:at + LANES, :] = jnp.concatenate([value, jnp.zeros_like(value)], axis=0).T
    copy.wait()
    for list_s, taken in ((low_s, below), (up_s, above)):
        def add(i, carry, list_s=list_s, taken=taken):
            at = pl.multiple_of(i * 16, 16)
            nodes_of = [list_s[at + k] for k in range(16)]
            new = [rows[pl.ds(n, 1), :] + taken[pl.ds(at + k, 1), :] for k, n in enumerate(nodes_of)]
            for n, value in zip(nodes_of, new):
                rows[pl.ds(n, 1), :] = value
            return carry

        lax.fori_loop(0, shared // 16, add, 0)

    def write(i, carry):
        at = pl.multiple_of(i * LANES, LANES)
        columns = rows[pl.ds(at, LANES), :].T
        out_ref[:, pl.ds(at, LANES)] = columns[0:snaps, :] + columns[snaps:2 * snaps, :]
        return carry

    lax.fori_loop(0, nodes // LANES, write, 0, unroll=4)


ANYWHERE = pl.BlockSpec(memory_space=pl.ANY)
IN_VMEM = pl.BlockSpec(memory_space=pltpu.VMEM)
IN_SMEM = pl.BlockSpec(memory_space=pltpu.SMEM)


def cost(micros):
    return pl.CostEstimate(flops=int(micros * 1e9), bytes_accessed=int(micros * 3e6), transcendentals=0)


ARRAYS, PARTS = 4, 1


SHARES = (7, 5)


def apply_call(index, columns, snapshots, rows, half):
    calls = len(SHARES)
    first, last = index == 0, index == calls - 1
    snaps, nodes = snapshots.shape
    share = columns[0].shape[0] // sum(SHARES)
    start, count = share * sum(SHARES[:index]), share * SHARES[index]
    row_shape = jax.ShapeDtypeStruct((nodes, LANES), jnp.float32)
    side = jax.ShapeDtypeStruct((snaps, nodes // 2), jnp.float32)
    operands = columns + (snapshots,) + (() if first else (rows,)) + ((half,) if last else ())
    return pl.pallas_call(
        functools.partial(apply_kernel, first, last, start, count, ARRAYS, PARTS),
        out_shape=[row_shape] + ([side, side] if last else []),
        in_specs=[ANYWHERE] * 4 + [IN_VMEM] + ([] if first else [ANYWHERE]) + ([IN_SMEM] if last else []),
        out_specs=[ANYWHERE] + ([IN_VMEM] * 2 if last else []),
        scratch_shapes=[pltpu.SMEM((count,), jnp.int32)] * 3
        + [pltpu.SMEM((count,), jnp.float32), pltpu.SemaphoreType.DMA((4,))]
        + [pltpu.VMEM((nodes, LANES), jnp.float32), pltpu.SemaphoreType.DMA, pltpu.SemaphoreType.DMA((4,))]
        + [pltpu.VMEM((nodes * (1 + PARTS), LANES), jnp.float32)] * ARRAYS,
        compiler_params=pltpu.CompilerParams(vmem_limit_bytes=33 * MIB),
        cost_estimate=cost(20),
    )(*operands)


def halves_of(value):
    high = value.astype(jnp.bfloat16)
    return high, (value - high.astype(jnp.float32)).astype(jnp.bfloat16)


def product(x_of, ya_ref, yb_ref, row_sets):
    snaps, nodes = ya_ref.shape
    dot = functools.partial(lax.dot_general, dimension_numbers=(((1,), (1,)), ((), ())),
                            preferred_element_type=jnp.float32)
    chunk = nodes // 6
    totals = [None] * row_sets
    for i in range(6):
        at = slice(i * chunk, (i + 1) * chunk)
        y_high, y_low = halves_of(jnp.concatenate([ya_ref[:, at], yb_ref[:, at]], axis=0))
        both_y = jnp.concatenate([y_high, y_low], axis=0)
        for row_set in range(row_sets):
            high, low = halves_of(x_of(row_set, at))
            both = dot(high, both_y)
            value = both[:, :2 * snaps] + (both[:, 2 * snaps:] + dot(low, y_high))
            totals[row_set] = value if totals[row_set] is None else totals[row_set] + value
    return totals


def near_kernel(*refs):
    sources, refs = refs[:7], refs[7:]
    out_ref, back, held, sems = refs[0], refs[1:4], refs[4:11], refs[11]
    copies = [pltpu.make_async_copy(source, target, sems.at[i]) for i, (source, target) in enumerate(zip(sources, held))]
    for copy in copies:
        copy.start()
    y_refs, blocks = held[:2], (held[2:4], held[4:5], held[5:6], held[6:7])
    waits = (copies[:4], copies[4:5], copies[5:6], copies[6:7])
    for distance, (block, waited) in enumerate(zip(blocks, waits)):
        for copy in waited:
            copy.wait()
        (value,) = product(lambda _, at, block=block: jnp.concatenate([ref[:, at] for ref in block], axis=0),
                           *y_refs, 1)
        out_ref[distance] = value
        if distance > 0:
            back[distance - 1][...] = value.T


def put(out_ref, place, distance, value):
    z, h, way = place[0], place[1], place[2]
    rings, low, snaps = out_ref.shape[0] // 4, out_ref.shape[1], out_ref.shape[2] // 2
    at = lax.rem(z - way * distance + rings, rings)
    turned = value.T
    for side in range(2):
        row = 2 * at + (h if side == 0 else 1 - h)
        for part in range(2):
            block = turned[part * snaps:(part + 1) * snaps, side * snaps:(side + 1) * snaps]
            out_ref[2 * row + (h if part == 0 else 1 - h)] = jnp.concatenate([block[:low], block[low:]], axis=1)


def lay_kernel(place, near_ref, *refs):
    *back, out_ref = refs
    put(out_ref, place, 0, near_ref[0])
    for distance, received in enumerate(back, 1):
        put(out_ref, place, distance, near_ref[distance])
        put(out_ref, place, -distance, received[...])
    put(out_ref, place, out_ref.shape[0] // 8, jnp.zeros_like(near_ref[0]))


def far_kernel(place, ya_ref, yb_ref, far_ref, laid_ref, out_ref):
    (value,) = product(lambda _, at: far_ref[:, at], ya_ref, yb_ref, 1)
    put(out_ref, place, out_ref.shape[0] // 8, value)


def near_call(*operands):
    snaps = operands[0].shape[0]
    square = jax.ShapeDtypeStruct((2 * snaps, 2 * snaps), jnp.float32)
    return pl.pallas_call(
        near_kernel,
        out_shape=[jax.ShapeDtypeStruct((4, 2 * snaps, 2 * snaps), jnp.float32)] + [square] * 3,
        in_specs=[ANYWHERE] * len(operands),
        out_specs=[IN_VMEM] * 4,
        scratch_shapes=[pltpu.VMEM(operand.shape, operand.dtype) for operand in operands]
        + [pltpu.SemaphoreType.DMA((len(operands),))],
        compiler_params=pltpu.CompilerParams(vmem_limit_bytes=60 * MIB),
        cost_estimate=cost(0.01),
    )(*operands)


def lay_call(place, near, back, rings):
    snaps = near.shape[1] // 2
    return pl.pallas_call(
        lay_kernel,
        out_shape=jax.ShapeDtypeStruct((4 * rings, snaps // 2, 2 * snaps), jnp.float32),
        in_specs=[IN_SMEM] + [IN_VMEM] * (1 + len(back)),
        out_specs=IN_VMEM,
        compiler_params=pltpu.CompilerParams(vmem_limit_bytes=16 * MIB),
        cost_estimate=cost(0.01),
    )(place, near, *back)


def far_call(place, ya, yb, far, laid):
    return pl.pallas_call(
        far_kernel,
        out_shape=jax.ShapeDtypeStruct(laid.shape, laid.dtype),
        in_specs=[IN_SMEM] + [IN_VMEM] * 4,
        out_specs=IN_VMEM,
        input_output_aliases={4: 0},
        compiler_params=pltpu.CompilerParams(vmem_limit_bytes=16 * MIB),
        cost_estimate=cost(2),
    )(place, ya, yb, far, laid)


def on_device(snapshots, connectivity, element_mass, lower_shared, upper_shared):
    snaps, nodes = snapshots.shape
    parts = lax.axis_size("mesh")
    blocks = lax.axis_size("snap")
    position = lax.axis_index("mesh")
    block = lax.axis_index("snap")
    rings = blocks // 2
    z, h = block // 2, block % 2
    half = nodes // 2
    tied = lax.optimization_barrier

    own = lax.dynamic_slice_in_dim(snapshots, h * half, half, 1)
    given = lax.dynamic_slice_in_dim(snapshots, (1 - h) * half, half, 1)
    a1 = ring_hop(own, 1)
    b1 = ring_hop(given, 1, cross=True)

    spread = (connectivity >> 3) * (8 * (1 + PARTS)) + (connectivity & 7)
    columns = tuple(spread[k] for k in range(3)) + (element_mass,)
    half_at = jnp.reshape(h, (1,)).astype(jnp.int32)
    (rows,) = apply_call(0, columns, snapshots, None, half_at)

    rows, a1, b1, given = tied((rows, a1, b1, given))
    pair1 = jnp.concatenate([a1, b1], axis=0)
    pair2 = ring_hop(pair1, 1)
    b0 = partner(given)
    rows, y_own, y_given = apply_call(1, columns, snapshots, rows, half_at)

    y_given, pair2, b0 = tied((y_given, pair2, b0))
    pair3 = ring_hop(pair2, 1)
    y_theirs = partner(y_given)

    shared = lower_shared.shape[0]
    low, high = pl.pallas_call(
        gather_kernel,
        out_shape=[jax.ShapeDtypeStruct((snaps, shared), jnp.float32)] * 2,
        in_specs=[IN_SMEM] * 2 + [IN_VMEM],
        out_specs=[IN_VMEM] * 2,
        scratch_shapes=[pltpu.VMEM((shared, LANES), jnp.float32)],
        compiler_params=pltpu.CompilerParams(vmem_limit_bytes=12 * MIB),
        cost_estimate=cost(0.01),
    )(lower_shared, upper_shared, rows)
    from_below = passed_along(high, "mesh", 1)
    from_above = passed_along(low, "mesh", -1)
    from_below, from_above, pair3, y_theirs = tied((from_below, from_above, pair3, y_theirs))
    pair4 = ring_hop(pair3, 1)
    near, *back = near_call(y_own, y_theirs, own, b0, pair1, pair2, pair3)
    rows, near = tied((rows, near))
    back = [ring_hop(value, -distance) for distance, value in enumerate(back, 1)]
    weighted = pl.pallas_call(
        assemble_kernel,
        out_shape=jax.ShapeDtypeStruct((snaps, nodes), jnp.float32),
        in_specs=[IN_SMEM] * 2 + [ANYWHERE] + [IN_VMEM] * 2,
        out_specs=IN_VMEM,
        scratch_shapes=[pltpu.VMEM((nodes, LANES), jnp.float32)] + [pltpu.VMEM((shared, LANES), jnp.float32)] * 2
        + [pltpu.SemaphoreType.DMA],
        compiler_params=pltpu.CompilerParams(vmem_limit_bytes=20 * MIB),
        cost_estimate=cost(0.01),
    )(lower_shared, upper_shared, rows, from_below, from_above)
    weighted, *back = tied((weighted, *back))
    place = jnp.stack([z, h, jnp.where(position % 2 == 0, 1, -1)]).astype(jnp.int32)
    laid = lay_call(place, near, back, rings)
    laid, pair4 = tied((laid, pair4))
    tiles = far_call(place, y_own, y_theirs, pair4, laid)
    planes = [[m * blocks + 2 * r + c for m in range(parts) for c in range(2)] for r in range(rings)]
    tile = jnp.sum(lax.all_to_all(tiles, ("mesh", "snap"), 0, 0, axis_index_groups=planes, tiled=True), axis=0)
    column = jnp.concatenate([tile[:, :snaps], tile[:, snaps:]], axis=0)
    return weighted, column * (1.0 / float(parts * nodes))


def solution(mesh):
    placed = (P("snap", "mesh"), P(None, "mesh"), P("mesh"), P("mesh"), P("mesh"))
    return jax.shard_map(
        on_device,
        mesh=mesh,
        in_specs=placed,
        out_specs=(P("snap", "mesh"), P("snap", "mesh")),
        check_vma=False,
    )
```
